128 devices in a mesh: ctx: 128 (over y, x, z, core).
Axes of the slice: x: 4, y: 4, z: 4, core: 2. Of those that a mesh axis runs over, the one named last changes fastest.
Arguments:
- layer_input: bfloat16 [16384, 576], P('ctx'), may hold values from -6 to 6
- attn_gain: float32 [576], replicated, may hold values from 0.5 to 1.5
- w_query: bfloat16 [576, 576], replicated, may hold values from -0.25 to 0.25
- w_key: bfloat16 [576, 192], replicated, may hold values from -0.25 to 0.25
- w_value: bfloat16 [576, 192], replicated, may hold values from -0.25 to 0.25
- w_out: bfloat16 [576, 576], replicated, may hold values from -0.75 to 0.75
- mlp_gain: float32 [576], replicated, may hold values from 0.5 to 1.5
- w_gate: bfloat16 [576, 1536], replicated, may hold values from -0.25 to 0.25
- w_up: bfloat16 [576, 1536], replicated, may hold values from -0.25 to 0.25
- w_down: bfloat16 [1536, 576], replicated, may hold values from -0.15625 to 0.15625
- cotangent: bfloat16 [16384, 576], P('ctx'), may hold values from -6 to 6
- segment_ids: int32 [16384], P('ctx'), may hold values from 0 to 17, as said below
- pair_table: int32 [128], P('ctx'), may hold values from 0 to 127, as said below
Outputs:
- layer_output: bfloat16 [16384, 576], P('ctx')
- grad_x: float32 [16384, 576], P('ctx')
- grad_attn_gain: float32 [576], replicated
- grad_w_query: float32 [576, 576], replicated
- grad_w_key: float32 [576, 192], replicated
- grad_w_value: float32 [576, 192], replicated
- grad_w_out: float32 [576, 576], replicated
- grad_mlp_gain: float32 [576], replicated
- grad_w_gate: float32 [576, 1536], replicated
- grad_w_up: float32 [576, 1536], replicated
- grad_w_down: float32 [1536, 576], replicated
The draws below stay inside these ranges and needn't reach their ends.
Inputs may be any that keep to these rules, and one draw needn't show every extreme that they name: `segment_ids`: as a function of a token's place in the pack the document number never falls and rises by at most one from one place to the next; places 0 to 8191 all form document 0. `pair_table`: A permutation: each block pair is held by exactly one device.
All inputs are finite; a program needn't handle non-finite values.
Results may differ from the reference program's by a relative error of at most 0.04.
Values may be sent and summed in bfloat16 or wider, within the bound.
A program may use at most 192 MiB of HBM per device.

```python
import math
import jax
import jax.numpy as jnp
from jax import lax

D = 576
HEADS = 9
KV_HEADS = 3
HEAD_DIM = 64
FF = 1536
TOK_DEV = 128
HALF = 64
TOKENS = 16384
N_CTX = 128


def pack_layout(key):
    pair_order = jax.random.permutation(jax.random.fold_in(key, 11), N_CTX).astype(jnp.int32)
    extra_docs = max(TOKENS // 1024, 1)
    shuffled = jax.random.permutation(jax.random.fold_in(key, 12), TOKENS // 2 - 1).astype(jnp.int32)
    starts = shuffled[:extra_docs] + TOKENS // 2 + 1
    opening = jnp.zeros((TOKENS,), jnp.int32).at[starts].set(1)
    opening = opening.at[TOKENS // 2].set(1)
    doc_by_place = jnp.cumsum(opening).astype(jnp.int32)
    slots = jnp.arange(TOKENS, dtype=jnp.int32)
    owner_dev = slots // TOK_DEV
    within = slots % TOK_DEV
    own_pair = pair_order[owner_dev]
    blocks = jnp.where(within < TOK_DEV // 2, own_pair, 2 * N_CTX - 1 - own_pair)
    places = blocks * (TOK_DEV // 2) + within % (TOK_DEV // 2)
    return (pair_order, doc_by_place[places].astype(jnp.int32))


def draw_pair_table(key, part):
    return pack_layout(key)[0]


def draw_segment_ids(key, part):
    return pack_layout(key)[1]


def levels(key, dims, pieces, low, high):
    factor_of = 1.0
    for axis_at, parts in pieces:
        draws = jax.random.uniform(jax.random.fold_in(jax.random.fold_in(key, 6), axis_at), (parts,), jnp.float32, low / len(pieces), high / len(pieces))
        factor_of = factor_of * jnp.repeat(jnp.exp(draws), dims[axis_at] // parts).reshape((-1,) + (1,) * (len(dims) - 1 - axis_at))
    return factor_of


def centred(own_key, dims, spread, limit, pieces=(), kind=jnp.bfloat16):
    drawn = spread * jax.random.normal(own_key, dims, jnp.float32)
    if pieces:
        drawn = drawn * levels(own_key, dims, pieces, -0.22, 0.18)
    return jnp.clip(drawn, -limit, limit).astype(kind)


def setup_inputs(seed: int = 0) -> dict:
    keys = jax.random.split(jax.random.key(seed), 14)
    return {
        "layer_input": centred(keys[0], (TOKENS, D), 1.0, 6.0, ((0, 128),)),
        "attn_gain": jnp.clip(1.0 + 0.1 * jax.random.normal(keys[1], (D,), jnp.float32), 0.5, 1.5),
        "w_query": centred(keys[2], (D, HEADS * HEAD_DIM), D ** -0.5, 0.25),
        "w_key": centred(keys[3], (D, KV_HEADS * HEAD_DIM), D ** -0.5, 0.25),
        "w_value": centred(keys[4], (D, KV_HEADS * HEAD_DIM), D ** -0.5, 0.25),
        "w_out": centred(keys[5], (HEADS * HEAD_DIM, D), (HEADS * HEAD_DIM // 8) ** -0.5, 0.75),
        "mlp_gain": jnp.clip(1.0 + 0.1 * jax.random.normal(keys[6], (D,), jnp.float32), 0.5, 1.5),
        "w_gate": centred(keys[7], (D, FF), D ** -0.5, 0.25),
        "w_up": centred(keys[8], (D, FF), D ** -0.5, 0.25),
        "w_down": centred(keys[9], (FF, D), FF ** -0.5, 0.15625),
        "cotangent": centred(keys[10], (TOKENS, D), 1.0, 6.0, ((0, 128),)),
        "segment_ids": draw_segment_ids(jax.random.fold_in(keys[13], 71), 0),
        "pair_table": draw_pair_table(jax.random.fold_in(keys[13], 71), 0),
    }


NORM_EPS = 1e-05
ROPE_THETA = 100000.0

@jax.custom_vjp
def low(v):
    return lax.optimization_barrier(v.astype(jnp.bfloat16)).astype(jnp.float32)

@jax.custom_vjp
def low_back(v):
    return v

def low_keep(v):
    return (low(v), None)

def low_pass(kept, grad):
    return (grad,)

def back_keep(v):
    return (v, None)

def back_low(kept, grad):
    return (low(grad),)
low.defvjp(low_keep, low_pass)
low_back.defvjp(back_keep, back_low)

def rms_scale(features, gain_vec):
    return features * lax.rsqrt(lax.optimization_barrier(jnp.mean(features * features, axis=-1, keepdims=True)) + NORM_EPS) * gain_vec

def angles(positions, head_dim):
    freq_steps = jnp.arange(head_dim // 2).astype(jnp.float32)
    frequency = ROPE_THETA ** (-2.0 * freq_steps / head_dim)
    turned = positions.astype(jnp.float32)[:, None] * frequency[None, :]
    return (jnp.cos(turned), jnp.sin(turned))

def rotate(features, cos_table, sin_table, head_dim):
    row_count = features.shape[0]
    split_heads = features.reshape(row_count, -1, head_dim)
    lower_half = split_heads[..., :head_dim // 2]
    upper_half = split_heads[..., head_dim // 2:]
    cos_wide = cos_table[:, None, :]
    sin_wide = sin_table[:, None, :]
    turned = jnp.concatenate([lower_half * cos_wide - upper_half * sin_wide, upper_half * cos_wide + lower_half * sin_wide], -1)
    return turned.reshape(row_count, -1)

def reference(layer_input, attn_gain, w_query, w_key, w_value, w_out, mlp_gain, w_gate, w_up, w_down, cotangent, segment_ids, pair_table):
    slots = jnp.arange(TOKENS, dtype=jnp.int32)
    owner_dev = slots // TOK_DEV
    within = slots % TOK_DEV
    own_pair = pair_table[owner_dev]
    blocks = jnp.where(within < HALF, own_pair, 2 * N_CTX - 1 - own_pair)
    places = (blocks * HALF + within % HALF).astype(jnp.int32)
    cos_table, sin_table = angles(places, HEAD_DIM)
    per_group = HEADS // KV_HEADS
    score_scale = HEAD_DIM ** (-0.5)
    qblock = math.gcd(TOKENS, 512)
    highest = lax.Precision.HIGHEST

    def matmul(left, right):
        return jnp.dot(left, right, precision=highest)

    def attend(q_rot, k_rot, value_rows):
        key_heads = k_rot.reshape(TOKENS, KV_HEADS, HEAD_DIM)
        value_heads = value_rows.reshape(TOKENS, KV_HEADS, HEAD_DIM)

        @jax.checkpoint
        def one_block(inputs):
            query_rows, query_segs, query_places = inputs
            query_heads = query_rows.reshape(-1, KV_HEADS, per_group, HEAD_DIM)
            raw_scores = low_back(jnp.einsum('bgrd,tgd->grbt', query_heads, key_heads, precision=highest) * score_scale)
            allowed = (query_segs[:, None] == segment_ids[None, :]) & (places[None, :] <= query_places[:, None])
            scores = jnp.where(allowed[None, None], raw_scores, -jnp.inf)
            attn_probs = low(jax.nn.softmax(scores, axis=-1))
            mixed = jnp.einsum('grbt,tgd->bgrd', attn_probs, value_heads, precision=highest)
            return mixed.reshape(-1, HEADS * HEAD_DIM)
        outputs = lax.map(one_block, (q_rot.reshape(-1, qblock, HEADS * HEAD_DIM), segment_ids.reshape(-1, qblock), places.reshape(-1, qblock)))
        return outputs.reshape(TOKENS, HEADS * HEAD_DIM)

    def layer_forward(x_float, gain_one, query_weight, key_weight, value_weight, out_weight, gain_two, gate_weight, up_weight, down_weight):
        normed = low(rms_scale(x_float, gain_one))
        queries = low_back(matmul(normed, query_weight))
        key_proj = low_back(matmul(normed, key_weight))
        value_rows = low(low_back(matmul(normed, value_weight)))
        q_rot = low(rotate(queries, cos_table, sin_table, HEAD_DIM))
        k_rot = low(rotate(key_proj, cos_table, sin_table, HEAD_DIM))
        attended = low(low_back(attend(q_rot, k_rot, value_rows)))
        hidden = x_float + low_back(matmul(attended, out_weight))
        normed_two = low(rms_scale(hidden, gain_two))
        gate_proj = low_back(matmul(normed_two, gate_weight))
        upward = low_back(matmul(normed_two, up_weight))
        active = low(jax.nn.silu(gate_proj) * upward)
        return hidden + low_back(matmul(active, down_weight))
    primals = (layer_input.astype(jnp.float32), attn_gain.astype(jnp.float32), w_query.astype(jnp.float32), w_key.astype(jnp.float32), w_value.astype(jnp.float32), w_out.astype(jnp.float32), mlp_gain.astype(jnp.float32), w_gate.astype(jnp.float32), w_up.astype(jnp.float32), w_down.astype(jnp.float32))
    result, pullback = jax.vjp(layer_forward, *primals)
    gradients = pullback(cotangent.astype(jnp.float32))
    return (result.astype(jnp.bfloat16), gradients[0], gradients[1], gradients[2], gradients[3], gradients[4], gradients[5], gradients[6], gradients[7], gradients[8], gradients[9])
```

```python
import functools
import jax
import jax.numpy as jnp
from jax import lax
from jax.experimental import pallas as pl
from jax.experimental.pallas import tpu as pltpu
from jax.sharding import PartitionSpec as P

f32 = jnp.float32
bf16 = jnp.bfloat16
D = 576
HEADS = 9
KV_HEADS = 3
HEAD_DIM = 64
PER_GROUP = HEADS // KV_HEADS
FF = 1536
NORM_EPS = 1e-05
ROPE_THETA = 100000.0
ROWS = 128
HALF = 64
N_CTX = 128
TOKENS = ROWS * N_CTX
DOCS = 18
META = 16
SLAB = ROWS + META
CHUNK = 512
PIECES = CHUNK // HALF
CHUNKS = TOKENS // CHUNK
COLS = HEADS * HALF
NEG = -1e30
SCALE = HEAD_DIM ** (-0.5)
VMEM_LIMIT = 56 * 1024 * 1024

K_AT = (0, 64, 128)
V_AT = (128, 192, 64)

GATE_AT = 0
UP_AT = GATE_AT + 12 * D
DOWN_AT = UP_AT + 12 * D
OUT_AT = DOWN_AT + 5 * FF
GAIN_AT = OUT_AT + 5 * D
BAND_ROWS = 64
FF_ROWS = 3 * N_CTX * BAND_ROWS
Q_AT = 0
KV_AT = Q_AT + 5 * D
GAIN_ONE_AT = KV_AT + 3 * D
BAND_ROWS_ONE = 16
ATT_ROWS = 3 * N_CTX * BAND_ROWS_ONE

MESH = pl.DeviceIdType.MESH
SIDE = 4
ORDERS = ((2, 1, 0), (1, 0, 2), (0, 2, 1))
STRIDES = (32, 8, 2)


def whereabouts():
    me = lax.axis_index("ctx")
    coords = (me // 32, lax.rem(me // 8, SIDE), lax.rem(me // 2, SIDE))
    return me, coords, lax.rem(me, 2)


def wrap(coord, step):
    return lax.rem(coord + (step + SIDE), SIDE)


def neighbour(me, coords, axis, step):
    return me + (wrap(coords[axis], step) - coords[axis]) * STRIDES[axis]


def greet(me, coords, core):
    barrier = pltpu.get_barrier_semaphore()
    others = [me + 1 - 2 * core]
    for axis in range(3):
        others += [neighbour(me, coords, axis, 1), neighbour(me, coords, axis, -1)]
    for other in others:
        pl.semaphore_signal(barrier, inc=1, device_id=(other,), device_id_type=MESH)
    pl.semaphore_wait(barrier, len(others))


def half_rows(rows):
    return rows // 32 * 16


class Sender:
    def __init__(self, sems):
        self.sems = sems
        self.copies = []

    def start(self, src, dst, device):
        at = len(self.copies)
        copy = pltpu.make_async_remote_copy(
            src_ref=src,
            dst_ref=dst,
            send_sem=self.sems[0].at[at],
            recv_sem=self.sems[1].at[at],
            device_id=(device,),
            device_id_type=MESH,
        )
        copy.start()
        self.copies.append(copy)
        return copy

    def finish(self):
        for copy in self.copies:
            copy.wait_send()


def at_axes(order, values):
    index = [None] * 3
    for axis, value in zip(order, values):
        index[axis] = value
    return tuple(index)


WHOLE = pl.ds(0, SIDE)


def gather_bands(own, out, sems, local_sem):
    me, coords, core = whereabouts()
    sibling = me + 1 - 2 * core
    sender = Sender(sems)
    bands = range(len(own))
    homes = []
    for band in bands:
        copy = pltpu.make_async_copy(own[band], out[band].at[coords + (core,)], local_sem.at[band])
        copy.start()
        homes.append(copy)
    for copy in homes:
        copy.wait()
    across = []

    def pass_over(band, index):
        part = out[band].at[index + (core,)]
        across.append(sender.start(part, part, sibling))

    for phase in range(3):
        subs = (None,) if phase < 2 else range(SIDE)

        def index_of(band, coord, sub):
            order = ORDERS[band % 3]
            mine = [coords[axis] for axis in order]
            values = [WHOLE] * phase + [coord] + mine[phase + 1 :]
            if sub is not None:
                values[0] = sub
            return at_axes(order, values)

        jobs = [(sub, band) for sub in subs for band in bands]
        sent, passed = {}, {}
        for sub, band in jobs:
            axis = ORDERS[band % 3][phase]
            part = out[band].at[index_of(band, coords[axis], sub) + (core,)]
            sent[sub, band] = (
                sender.start(part, part, neighbour(me, coords, axis, 1)),
                sender.start(part, part, neighbour(me, coords, axis, -1)),
            )
        if phase == 0:
            for band in bands:
                pass_over(band, coords)
        for sub, band in jobs:
            axis = ORDERS[band % 3][phase]
            rows = own[band].shape[0]
            cut = half_rows(rows)
            plus, minus = sent[sub, band]
            low = index_of(band, wrap(coords[axis], -1), sub)
            high = index_of(band, wrap(coords[axis], 1), sub)
            plus.wait_recv()
            part = out[band].at[low + (core, pl.ds(0, cut))]
            one = sender.start(part, part, neighbour(me, coords, axis, 1))
            minus.wait_recv()
            part = out[band].at[high + (core, pl.ds(cut, rows - cut))]
            two = sender.start(part, part, neighbour(me, coords, axis, -1))
            passed[sub, band] = (one, two)
            pass_over(band, low)
            pass_over(band, high)
        for sub, band in jobs:
            axis = ORDERS[band % 3][phase]
            one, two = passed[sub, band]
            one.wait_recv()
            two.wait_recv()
            pass_over(band, index_of(band, wrap(coords[axis], 2), sub))
    for copy in across:
        copy.wait_recv()
    sender.finish()


def scatter_bands(parts, done, scratch):
    n = len(parts)
    acc, sib = scratch[:n], scratch[n : 2 * n]
    landing = [scratch[2 * n + 3 * b : 2 * n + 3 * b + 3] for b in range(n)]
    send, recv, local_sem = scratch[5 * n :]
    me, coords, core = whereabouts()
    sibling = me + 1 - 2 * core
    sender = Sender((send, recv))
    bands = range(n)
    steps = (2, 1, -1, 0)
    order_of = [ORDERS[b % 3] for b in bands]

    homes, swaps = {}, {}
    for step in steps:
        for band in bands:
            order = order_of[band]
            plane = at_axes(order, (wrap(coords[order[0]], step), WHOLE, WHOLE))
            copy = pltpu.make_async_copy(
                parts[band].at[plane + (core,)], acc[band].at[plane], local_sem.at[band, step % 4]
            )
            copy.start()
            homes[band, step] = copy
        for sub in range(SIDE):
            for band in bands:
                order = order_of[band]
                line = at_axes(order, (wrap(coords[order[0]], step), sub, WHOLE))
                swaps[band, step, sub] = sender.start(
                    parts[band].at[line + (1 - core,)], sib[band].at[line], sibling
                )

    def add_swap(band, step, sub):
        order = order_of[band]
        swaps[band, step, sub].wait_recv()
        first = wrap(coords[order[0]], step)

        def body(last, carry):
            at = at_axes(order, (first, sub, last))
            acc[band][at] = acc[band][at] + sib[band][at]
            return carry

        lax.fori_loop(0, SIDE, body, 0)

    for phase in range(3):
        subs = tuple(range(SIDE)) if phase == 0 else (None,)
        jobs = [(sub, band) for sub in subs for band in bands]

        def index_of(band, step, sub):
            order = order_of[band]
            mine = [coords[axis] for axis in order]
            values = mine[:phase] + [wrap(mine[phase], step)] + [WHOLE] * (2 - phase)
            if sub is not None:
                values[1] = sub
            return at_axes(order, values)

        def land(band, slot, sub):
            return landing[band][phase].at[(slot,) if sub is None else (slot, sub)]

        def each(band, sub, body):
            if phase == 2:
                body(())
            else:

                def run(last, carry):
                    body((last,))
                    return carry

                lax.fori_loop(0, SIDE, run, 0)

        def acc_at(band, step, sub, tail):
            order = order_of[band]
            mine = [coords[axis] for axis in order]
            values = mine[:phase] + [wrap(mine[phase], step)]
            if sub is not None:
                values.append(sub)
            return at_axes(order, values + list(tail))

        def landed(slot, sub, tail):
            return (slot,) + (() if sub is None else (sub,)) + tail

        first, whole = {}, {}
        for sub, band in jobs:
            axis = order_of[band][phase]
            rows = parts[band].shape[4]
            cut = half_rows(rows)
            if phase == 0:
                if sub == 0:
                    homes[band, 2].wait()
                add_swap(band, 2, sub)
            far = index_of(band, 2, sub)
            lead = (WHOLE,) * (1 if phase < 2 else 0)
            first[sub, band] = []
            for slot, lo, size, step in ((0, 0, cut, 1), (1, cut, rows - cut, -1)):
                copy = None
                if size:
                    copy = sender.start(
                        acc[band].at[far + (pl.ds(lo, size),)],
                        land(band, slot, sub).at[lead + (pl.ds(0, size),)],
                        neighbour(me, coords, axis, step),
                    )
                first[sub, band].append(copy)
        for sub, band in jobs:
            axis = order_of[band][phase]
            rows = parts[band].shape[4]
            cut = half_rows(rows)
            for step, slot, lo, size in ((1, 0, 0, cut), (-1, 1, cut, rows - cut)):
                if phase == 0:
                    if sub == 0:
                        homes[band, step].wait()
                    add_swap(band, step, sub)
                if size:
                    first[sub, band][slot].wait_recv()

                    def body(tail, step=step, slot=slot, lo=lo, size=size):
                        at = acc_at(band, step, sub, tail) + (pl.ds(lo, size),)
                        acc[band][at] = (
                            acc[band][at]
                            + landing[band][phase][landed(slot, sub, tail) + (pl.ds(0, size),)]
                        )

                    each(band, sub, body)
                whole[sub, band, step] = sender.start(
                    acc[band].at[index_of(band, step, sub)],
                    land(band, 2 + slot, sub),
                    neighbour(me, coords, axis, step),
                )
        for sub, band in jobs:
            if phase == 0:
                if sub == 0:
                    homes[band, 0].wait()
                add_swap(band, 0, sub)
            whole[sub, band, 1].wait_recv()
            whole[sub, band, -1].wait_recv()

            def body(tail):
                at = acc_at(band, 0, sub, tail)
                total = (
                    acc[band][at].astype(f32)
                    + landing[band][phase][landed(2, sub, tail)].astype(f32)
                    + landing[band][phase][landed(3, sub, tail)].astype(f32)
                )
                if phase == 2:
                    done[band][...] = total
                else:
                    acc[band][at] = total.astype(bf16)

            each(band, sub, body)
    sender.finish()


def rms_parts(features):
    return lax.rsqrt(jnp.mean(features * features, axis=-1, keepdims=True) + NORM_EPS)


def rms_back(features, gain, grad):
    inverse = rms_parts(features)
    scaled = grad * gain
    inner = jnp.mean(scaled * features, axis=-1, keepdims=True)
    by_features = inverse * scaled - features * (inverse * inverse * inverse * inner)
    by_gain = jnp.sum(grad * features * inverse, axis=0, keepdims=True)
    return by_features, by_gain


def nt_dot(left, right):
    return lax.dot_general(left, right, (((1,), (1,)), ((), ())), preferred_element_type=f32)


def tn_dot(left, right):
    return lax.dot_general(left, right, (((0,), (0,)), ((), ())), preferred_element_type=f32)


def nn_dot(left, right):
    return jnp.dot(left, right, preferred_element_type=f32)


def turn(tile, cos_wide, sin_wide):
    lanes = lax.broadcasted_iota(jnp.int32, tile.shape, 1)
    swapped = jnp.where(
        lax.rem(lanes, HEAD_DIM) < HEAD_DIM // 2, pltpu.roll(tile, 96, 1), pltpu.roll(tile, 32, 1)
    )
    return tile * cos_wide + swapped * sin_wide


def project_kernel(
    x_ref, gain_ref, wq_ref, wk_ref, wv_ref, cos_ref, sin_ref, meta_ref,
    q_ref, n_ref, out0, out1, out2,
    own0, own1, own2, send, recv, local_sem,
):
    features = x_ref[...].astype(f32)
    normed = (features * rms_parts(features) * gain_ref[...]).astype(bf16)
    n_ref[...] = normed
    cos_wide, sin_wide = cos_ref[...], sin_ref[...]
    keys = nn_dot(normed, wk_ref[...])
    values = nn_dot(normed, wv_ref[...]).astype(bf16)
    queries = nn_dot(normed, wq_ref[...])
    own0[0:ROWS, :] = turn(keys[:, 0:128], cos_wide, sin_wide).astype(bf16)
    own0[ROWS:SLAB, :] = meta_ref[...]
    mixed = turn(jnp.concatenate([keys[:, 128:192], queries[:, 512:576]], 1), cos_wide, sin_wide)
    own1[...] = jnp.concatenate([mixed[:, 0:64].astype(bf16), values[:, 128:192]], 1)
    own2[...] = values[:, 0:128]
    for tile in range(4):
        at = slice(128 * tile, 128 * tile + 128)
        q_ref[:, at] = (turn(queries[:, at], cos_wide, sin_wide).astype(bf16).astype(f32) * SCALE).astype(bf16)
    q_ref[:, 512:576] = (mixed[:, 64:128].astype(bf16).astype(f32) * SCALE).astype(bf16)
    me, coords, core = whereabouts()
    greet(me, coords, core)
    gather_bands((own0, own1, own2), (out0, out1, out2), (send, recv), local_sem)


def project_and_gather(x, gain, wq, wk, wv, cos_wide, sin_wide, meta):
    vmem = pl.BlockSpec(memory_space=pltpu.VMEM)
    anywhere = pl.BlockSpec(memory_space=pl.ANY)
    rows = (SLAB, ROWS, ROWS)
    return pl.pallas_call(
        project_kernel,
        out_shape=(
            jax.ShapeDtypeStruct((ROWS, D), bf16),
            jax.ShapeDtypeStruct((ROWS, D), bf16),
        )
        + tuple(jax.ShapeDtypeStruct((SIDE, SIDE, SIDE, 2, r, 128), bf16) for r in rows),
        in_specs=[vmem] * 8,
        out_specs=(vmem, vmem, anywhere, anywhere, anywhere),
        scratch_shapes=[pltpu.VMEM((r, 128), bf16) for r in rows]
        + [
            pltpu.SemaphoreType.DMA((3 * 48,)),
            pltpu.SemaphoreType.DMA((3 * 48,)),
            pltpu.SemaphoreType.DMA((3,)),
        ],
        compiler_params=pltpu.CompilerParams(
            collective_id=1, has_side_effects=True, vmem_limit_bytes=VMEM_LIMIT
        ),
        name="project_and_gather",
    )(x, gain, wq, wk, wv, cos_wide, sin_wide, meta)


def needed(chunk, a_hi, b_lo, b_hi):
    return (chunk <= a_hi) | ((chunk >= b_lo) & (chunk <= b_hi))


def chunk_rows(chunk):
    return pl.ds(pl.multiple_of(chunk * CHUNK, CHUNK), CHUNK)


def wait_chunk(chunk, held, sem):
    window = held.at[chunk_rows(chunk)]
    pltpu.make_async_copy(window, window, sem.at[chunk]).wait()


def chunk_mask(chunk, place_row, start_row):
    keys = chunk * CHUNK + lax.broadcasted_iota(jnp.int32, (CHUNK, COLS), 0)
    return (keys <= place_row) & (keys >= start_row)


def layer_kernel(
    source, info,
    kv0, kv1, kv2, wo_hbm, wg_hbm, wu_hbm, wd_hbm,
    q_ref, rows_ref, x_ref, c_ref, gain_ref,
    result_ref, gh_ref, dq_ref, dkv0, dkv1, dkv2, dw0, dw1, dw2,
    held, sem, wo_ref, wg_ref, wu_ref, wd_ref, w_sem, q_spread, g_spread, mixed, top, total, att_ref,
    delta_ref, dw, dw_sem, staged, blank, out_sem, blank_sem, gain_rows,
):
    a_hi, b_lo, b_hi = info[0], info[1], info[2]
    kvs, dkvs, dws = (kv0, kv1, kv2), (dkv0, dkv1, dkv2), (dw0, dw1, dw2)

    def issue(chunk, carry):
        @pl.when(needed(chunk, a_hi, b_lo, b_hi))
        def _():
            for piece in range(PIECES):
                slot = source[chunk * PIECES + piece]
                rows = pl.ds(pl.multiple_of(chunk * CHUNK + piece * HALF, HALF), HALF)
                for band in range(3):
                    row = slot + (slot // ROWS * META if band == 0 else 0)
                    pltpu.make_async_copy(
                        kvs[band].at[pl.ds(pl.multiple_of(row, 16), HALF)],
                        held.at[rows, 128 * band : 128 * band + 128],
                        sem.at[chunk],
                    ).start()

        return carry

    lax.fori_loop(0, CHUNKS, issue, 0)
    weights = [
        pltpu.make_async_copy(src, dst, w_sem.at[i])
        for i, (src, dst) in enumerate(
            ((wo_hbm, wo_ref), (wg_hbm, wg_ref), (wu_hbm, wu_ref), (wd_hbm, wd_ref))
        )
    ]
    for copy in weights:
        copy.start()

    def spread(rows, place, windows):
        for block in range(2):
            for head in range(HEADS):
                tile = rows[block * HALF : (block + 1) * HALF, head * HEAD_DIM : (head + 1) * HEAD_DIM]
                at = windows[head // PER_GROUP]
                place[block, head * HALF : (head + 1) * HALF, at : at + HEAD_DIM] = tile

    def unspread(columns, place, block, windows):
        for head in range(HEADS):
            at = windows[head // PER_GROUP]
            tile = columns[at : at + HEAD_DIM, head * HALF : (head + 1) * HALF]
            place[block * HALF : (block + 1) * HALF, head * HEAD_DIM : (head + 1) * HEAD_DIM] = tile.T

    q_spread[...] = jnp.zeros_like(q_spread)
    g_spread[...] = jnp.zeros_like(g_spread)
    spread(q_ref[...], q_spread, K_AT)
    mixed[...] = jnp.zeros_like(mixed)
    top[...] = jnp.full_like(top, NEG)
    total[...] = jnp.zeros_like(total)
    blank[...] = jnp.zeros_like(blank)

    def mask_of(block, chunk):
        return chunk_mask(
            chunk, rows_ref[2 * block : 2 * block + 1, :], rows_ref[2 * block + 1 : 2 * block + 2, :]
        )

    def forward(block, chunk, masked):
        window = chunk_rows(chunk)
        scores = nt_dot(held[window, 0:256], q_spread[block])
        if masked:
            scores = jnp.where(mask_of(block, chunk), scores, NEG)
        old = top[block : block + 1, :]
        new = jnp.maximum(old, jnp.max(scores, axis=0, keepdims=True))
        probs = jnp.exp(scores - new)
        shrink = jnp.exp(old - new)
        top[block : block + 1, :] = new
        total[block : block + 1, :] = total[block : block + 1, :] * shrink + jnp.sum(
            probs, axis=0, keepdims=True
        )
        mixed[block] = mixed[block] * shrink + tn_dot(held[window, 128:384], probs.astype(bf16))

    def forward_step(chunk, carry):
        in_b = (chunk >= b_lo) & (chunk <= b_hi)

        @pl.when(needed(chunk, a_hi, b_lo, b_hi))
        def _():
            wait_chunk(chunk, held, sem)

        @pl.when(chunk < a_hi)
        def _():
            forward(0, chunk, False)

        @pl.when(chunk == a_hi)
        def _():
            forward(0, chunk, True)

        @pl.when(in_b)
        def _():
            forward(1, chunk, True)

        return carry

    lax.fori_loop(0, CHUNKS, forward_step, 0)
    for block in range(2):
        sums = total[block : block + 1, :]
        top[block : block + 1, :] = top[block : block + 1, :] + jnp.log(sums)
        mixed[block] = mixed[block] / sums
        unspread(mixed.at[block], att_ref, block, V_AT)

    attended = att_ref[...].astype(bf16)
    cotangent = c_ref[...]
    gain = gain_ref[...]
    for copy in weights:
        copy.wait()
    hidden = x_ref[...].astype(f32) + nn_dot(attended, wo_ref[...])
    normed = (hidden * rms_parts(hidden) * gain).astype(bf16)
    gate = nn_dot(normed, wg_ref[...])
    upward = nn_dot(normed, wu_ref[...])
    open_gate = jax.nn.sigmoid(gate)
    silu = gate * open_gate
    active = (silu * upward).astype(bf16)
    result_ref[...] = (hidden + nn_dot(active, wd_ref[...])).astype(bf16)
    grad_active = nt_dot(cotangent, wd_ref[...])
    grad_gate = (grad_active * upward * open_gate * (1.0 + gate * (1.0 - open_gate))).astype(bf16)
    grad_up = (grad_active * silu).astype(bf16)
    grad_normed = nt_dot(grad_gate, wg_ref[...]) + nt_dot(grad_up, wu_ref[...])
    by_hidden, by_gain = rms_back(hidden, gain, grad_normed)
    grad_hidden = cotangent.astype(f32) + by_hidden
    gh_ref[...] = grad_hidden
    grad_out = grad_hidden.astype(bf16)
    spread(nt_dot(grad_out, wo_ref[...]).astype(bf16), g_spread, V_AT)
    for block in range(2):
        turned = g_spread[block].astype(f32).T
        delta_ref[block : block + 1, :] = jnp.sum(turned * mixed[block], axis=0, keepdims=True)

    def pack(at, grads):
        rows = grads.shape[0]
        for tile in range(grads.shape[1] // 128):
            dw[at + tile * rows : at + (tile + 1) * rows, :] = grads[:, 128 * tile : 128 * tile + 128].astype(bf16)
        if grads.shape[1] % 128:
            tile = grads.shape[1] // 128
            dw[at + tile * rows : at + (tile + 1) * rows, 0:64] = grads[:, 128 * tile : 128 * tile + 64].astype(bf16)
            dw[at + tile * rows : at + (tile + 1) * rows, 64:128] = jnp.zeros((rows, 64), bf16)

    pack(GATE_AT, tn_dot(normed, grad_gate))
    pack(UP_AT, tn_dot(normed, grad_up))
    pack(DOWN_AT, tn_dot(active, cotangent))
    pack(OUT_AT, tn_dot(attended, grad_out))
    gain_rows[...] = jnp.zeros_like(gain_rows)
    for tile in range(4):
        gain_rows[tile : tile + 1, :] = by_gain[:, 128 * tile : 128 * tile + 128]
    gain_rows[4:5, 0:64] = by_gain[:, 512:576]
    dw[GAIN_AT : GAIN_AT + 16, :] = gain_rows[...].astype(bf16)
    dw[GAIN_AT + 16 : FF_ROWS, :] = jnp.zeros((FF_ROWS - GAIN_AT - 16, 128), bf16)
    band_rows = FF_ROWS // 3
    dw_copies = [
        pltpu.make_async_copy(dw.at[pl.ds(band * band_rows, band_rows)], dws[band], dw_sem.at[band])
        for band in range(3)
    ]
    for copy in dw_copies:
        copy.start()

    mixed[...] = jnp.zeros_like(mixed)

    def backward(block, chunk, masked, mode):
        window = chunk_rows(chunk)
        keys = held[window, 0:256]
        values = held[window, 128:384]
        scores = nt_dot(keys, q_spread[block])
        probs = jnp.exp(scores - top[block : block + 1, :])
        if masked:
            probs = jnp.where(mask_of(block, chunk), probs, 0.0)
        grad_probs = nt_dot(values, g_spread[block])
        grad_scores = (probs * (grad_probs - delta_ref[block : block + 1, :])).astype(bf16)
        mixed[block] += tn_dot(keys, grad_scores)
        dk = nn_dot(grad_scores, q_spread[block])
        dv = nn_dot(probs.astype(bf16), g_spread[block])
        parts = (dk[:, 0:128], dk[:, 128:256] + dv[:, 0:128], dv[:, 128:256])
        for band in range(3):
            at = slice(128 * band, 128 * band + 128)
            if mode == "first":
                staged[:, at] = parts[band]
            elif mode == "second":
                held[window, at] = (staged[:, at] + parts[band]).astype(bf16)
            else:
                held[window, at] = parts[band].astype(bf16)

    def zero_copy(band, row):
        return pltpu.make_async_copy(blank, dkvs[band].at[pl.ds(row, HALF)], blank_sem)

    def backward_step(chunk, carry):
        in_a = chunk <= a_hi
        in_b = (chunk >= b_lo) & (chunk <= b_hi)

        @pl.when((chunk < a_hi) & jnp.logical_not(in_b))
        def _():
            backward(0, chunk, False, "only")

        @pl.when((chunk == a_hi) & jnp.logical_not(in_b))
        def _():
            backward(0, chunk, True, "only")

        @pl.when(in_b & jnp.logical_not(in_a))
        def _():
            backward(1, chunk, True, "only")

        @pl.when(in_a & in_b)
        def _():
            backward(0, chunk, True, "first")
            backward(1, chunk, True, "second")

        use = in_a | in_b

        @pl.when(use)
        def _():
            for piece in range(PIECES):
                row = pl.multiple_of(source[chunk * PIECES + piece], HALF)
                rows = pl.ds(pl.multiple_of(chunk * CHUNK + piece * HALF, HALF), HALF)
                for band in range(3):
                    pltpu.make_async_copy(
                        held.at[rows, 128 * band : 128 * band + 128],
                        dkvs[band].at[pl.ds(row, HALF)],
                        out_sem.at[chunk],
                    ).start()

        @pl.when(jnp.logical_not(use))
        def _():
            for piece in range(PIECES):
                row = pl.multiple_of(source[chunk * PIECES + piece], HALF)
                for band in range(3):
                    zero_copy(band, row).start()

        return carry

    lax.fori_loop(0, CHUNKS, backward_step, 0)
    for block in range(2):
        unspread(mixed.at[block], dq_ref, block, K_AT)

    def drain(chunk, carry):
        use = needed(chunk, a_hi, b_lo, b_hi)

        @pl.when(use)
        def _():
            wait_chunk(chunk, held, out_sem)

        @pl.when(jnp.logical_not(use))
        def _():
            for _piece in range(PIECES):
                for band in range(3):
                    zero_copy(band, 0).wait()

        return carry

    lax.fori_loop(0, CHUNKS, drain, 0)
    for copy in dw_copies:
        copy.wait()


def layer(source, info, kvs, weights, q, row_info, x, cotangent, gain):
    vmem = pl.BlockSpec(memory_space=pltpu.VMEM)
    anywhere = pl.BlockSpec(memory_space=pl.ANY)
    return pl.pallas_call(
        layer_kernel,
        out_shape=(
            jax.ShapeDtypeStruct((ROWS, D), bf16),
            jax.ShapeDtypeStruct((ROWS, D), f32),
            jax.ShapeDtypeStruct((ROWS, D), f32),
        )
        + (jax.ShapeDtypeStruct((TOKENS, 128), bf16),) * 3
        + (jax.ShapeDtypeStruct((FF_ROWS // 3, 128), bf16),) * 3,
        grid_spec=pltpu.PrefetchScalarGridSpec(
            num_scalar_prefetch=2,
            in_specs=[anywhere] * 7 + [vmem] * 5,
            out_specs=(vmem,) * 3 + (anywhere,) * 6,
            scratch_shapes=[
                pltpu.VMEM((TOKENS, 384), bf16),
                pltpu.SemaphoreType.DMA((CHUNKS,)),
                pltpu.VMEM((D, D), bf16),
                pltpu.VMEM((D, FF), bf16),
                pltpu.VMEM((D, FF), bf16),
                pltpu.VMEM((FF, D), bf16),
                pltpu.SemaphoreType.DMA((4,)),
                pltpu.VMEM((2, COLS, 256), bf16),
                pltpu.VMEM((2, COLS, 256), bf16),
                pltpu.VMEM((2, 256, COLS), f32),
                pltpu.VMEM((2, COLS), f32),
                pltpu.VMEM((2, COLS), f32),
                pltpu.VMEM((ROWS, D), f32),
                pltpu.VMEM((2, COLS), f32),
                pltpu.VMEM((FF_ROWS, 128), bf16),
                pltpu.SemaphoreType.DMA((3,)),
                pltpu.VMEM((CHUNK, 384), f32),
                pltpu.VMEM((HALF, 128), bf16),
                pltpu.SemaphoreType.DMA((CHUNKS,)),
                pltpu.SemaphoreType.DMA,
                pltpu.VMEM((16, 128), f32),
            ],
        ),
        compiler_params=pltpu.CompilerParams(vmem_limit_bytes=VMEM_LIMIT),
        name="layer",
    )(source, info, *kvs, *weights, q, row_info, x, cotangent, gain)


SCATTERED = (ROWS, ROWS, ROWS, BAND_ROWS, BAND_ROWS, BAND_ROWS)
FINAL_ROWS = BAND_ROWS + BAND_ROWS_ONE


def scatter_scratch(rows):
    shapes = [pltpu.VMEM((SIDE, SIDE, SIDE, r, 128), bf16) for r in rows] * 2
    for r in rows:
        shapes += [
            pltpu.VMEM((4, SIDE, SIDE, r, 128), bf16),
            pltpu.VMEM((4, SIDE, r, 128), bf16),
            pltpu.VMEM((4, r, 128), bf16),
        ]
    count = len(rows) * 44
    return shapes + [
        pltpu.SemaphoreType.DMA((count,)),
        pltpu.SemaphoreType.DMA((count,)),
        pltpu.SemaphoreType.DMA((len(rows), SIDE)),
    ]


def reduce_kernel(*refs):
    dkv, dws = refs[0:3], refs[3:6]
    dq_ref, n_ref, x_ref, gh_ref, cos_ref, sin_ref, gain_ref, wq_ref, wk_ref, wv_ref = refs[6:16]
    gx_ref, outs = refs[16], refs[17:20]
    rest = refs[20:]
    done, rest = rest[:6], rest[6:]
    first, rest = rest[:33], rest[33:]
    parts, rest = rest[:3], rest[3:]
    done_one, rest = rest[:3], rest[3:]
    second, rest = rest[:18], rest[18:]
    own, rest = rest[:3], rest[3:]
    gain_rows, send, recv, local_sem = rest
    me, coords, core = whereabouts()
    greet(me, coords, core)
    scatter_bands(tuple(dkv) + tuple(dws), done, first)

    cos_wide, sin_wide = cos_ref[...], -sin_ref[...]
    tiles = [turn(dq_ref[:, 128 * t : 128 * t + 128] * SCALE, cos_wide, sin_wide).astype(bf16) for t in range(4)]
    mixed = turn(
        jnp.concatenate([done[1][:, 0:64], dq_ref[:, 512:576] * SCALE], 1), cos_wide, sin_wide
    ).astype(bf16)
    grad_q = jnp.concatenate(tiles + [mixed[:, 64:128]], 1)
    grad_k = jnp.concatenate([turn(done[0][...], cos_wide, sin_wide).astype(bf16), mixed[:, 0:64]], 1)
    grad_v = jnp.concatenate([done[2][...], done[1][:, 64:128]], 1).astype(bf16)
    normed = n_ref[...]
    features = x_ref[...].astype(f32)
    grad_normed = nt_dot(grad_q, wq_ref[...]) + nt_dot(grad_k, wk_ref[...]) + nt_dot(grad_v, wv_ref[...])
    by_x, by_gain = rms_back(features, gain_ref[...], grad_normed)
    gx_ref[...] = gh_ref[...] + by_x

    def put(at, rows16):
        block = at // 16
        band, device = divmod(block, N_CTX)
        index = (device // 32, device // 8 % 4, device // 2 % 4, device % 2)
        parts[band][index] = rows16

    def pack(at, grads):
        width = grads.shape[1]
        if width % 128:
            grads = jnp.concatenate([grads, jnp.zeros((D, 128 - width % 128), f32)], 1)
        grads = grads.astype(bf16)
        for tile in range(grads.shape[1] // 128):
            for row in range(0, D, 16):
                put(at + tile * D + row, grads[row : row + 16, 128 * tile : 128 * tile + 128])

    pack(Q_AT, tn_dot(normed, grad_q))
    pack(KV_AT, tn_dot(normed, jnp.concatenate([grad_k, grad_v], 1)))
    gain_rows[...] = jnp.zeros_like(gain_rows)
    for tile in range(4):
        gain_rows[tile : tile + 1, :] = by_gain[:, 128 * tile : 128 * tile + 128]
    gain_rows[4:5, 0:64] = by_gain[:, 512:576]
    put(GAIN_ONE_AT, gain_rows[...].astype(bf16))
    for at in range(GAIN_ONE_AT + 16, ATT_ROWS, 16):
        put(at, jnp.zeros((16, 128), bf16))
    scatter_bands(parts, done_one, second)
    for band in range(3):
        own[band][0:BAND_ROWS, :] = done[3 + band][...].astype(bf16)
        own[band][BAND_ROWS:FINAL_ROWS, :] = done_one[band][...].astype(bf16)
    gather_bands(own, outs, (send, recv), local_sem)


def reduce_all(dkvs, dws, dq, normed, x, grad_hidden, cos_wide, sin_wide, gain, wq, wk, wv):
    vmem = pl.BlockSpec(memory_space=pltpu.VMEM)
    anywhere = pl.BlockSpec(memory_space=pl.ANY)
    one = (BAND_ROWS_ONE,) * 3
    return pl.pallas_call(
        reduce_kernel,
        out_shape=(jax.ShapeDtypeStruct((ROWS, D), f32),)
        + (jax.ShapeDtypeStruct((SIDE, SIDE, SIDE, 2, FINAL_ROWS, 128), bf16),) * 3,
        in_specs=[anywhere] * 6 + [vmem] * 10,
        out_specs=(vmem,) + (anywhere,) * 3,
        scratch_shapes=[pltpu.VMEM((r, 128), f32) for r in SCATTERED]
        + scatter_scratch(SCATTERED)
        + [pltpu.VMEM((SIDE, SIDE, SIDE, 2, r, 128), bf16) for r in one]
        + [pltpu.VMEM((r, 128), f32) for r in one]
        + scatter_scratch(one)
        + [pltpu.VMEM((FINAL_ROWS, 128), bf16)] * 3
        + [
            pltpu.VMEM((16, 128), f32),
            pltpu.SemaphoreType.DMA((3 * 48,)),
            pltpu.SemaphoreType.DMA((3 * 48,)),
            pltpu.SemaphoreType.DMA((3,)),
        ],
        compiler_params=pltpu.CompilerParams(
            collective_id=2, has_side_effects=True, vmem_limit_bytes=VMEM_LIMIT
        ),
        name="reduce_all",
    )(*dkvs, *dws, dq, normed, x, grad_hidden, cos_wide, sin_wide, gain, wq, wk, wv)


def unpack_kernel(
    sums0, sums1, sums2,
    ga_ref, gq_ref, gk_ref, gv_ref, go_ref, gm_ref, gg_ref, gu_ref, gd_ref,
):
    sums = (sums0, sums1, sums2)

    def fetch(at, size):
        band, row = divmod(at, N_CTX * BAND_ROWS)
        device, row = divmod(row, BAND_ROWS)
        return sums[band][device, row : row + size, :].astype(f32)

    def fetch_one(at):
        band, row = divmod(at, N_CTX * BAND_ROWS_ONE)
        return sums[band][row // BAND_ROWS_ONE, BAND_ROWS:FINAL_ROWS, :].astype(f32)

    def fill(ref, at):
        rows, columns = ref.shape
        for tile in range((columns + 127) // 128):
            width = min(128, columns - 128 * tile)
            for row in range(0, rows, BAND_ROWS):
                piece = fetch(at + tile * rows + row, BAND_ROWS)
                ref[row : row + BAND_ROWS, 128 * tile : 128 * tile + width] = piece[:, 0:width]

    fill(gg_ref, GATE_AT)
    fill(gu_ref, UP_AT)
    fill(gd_ref, DOWN_AT)
    fill(go_ref, OUT_AT)
    for row in range(0, D, 16):
        rows = slice(row, row + 16)
        for tile in range(5):
            width = min(128, D - 128 * tile)
            gq_ref[rows, 128 * tile : 128 * tile + width] = fetch_one(Q_AT + tile * D + row)[:, 0:width]
        tiles = [fetch_one(KV_AT + tile * D + row) for tile in range(3)]
        gk_ref[rows, 0:128] = tiles[0]
        gk_ref[rows, 128:192] = tiles[1][:, 0:64]
        gv_ref[rows, :] = jnp.concatenate([tiles[1][:, 64:128], tiles[2]], 1)
    for ref, piece in ((gm_ref, fetch(GAIN_AT, 16)), (ga_ref, fetch_one(GAIN_ONE_AT))):
        for tile in range(5):
            width = min(128, D - 128 * tile)
            ref[:, 128 * tile : 128 * tile + width] = piece[tile : tile + 1, 0:width]


def unpack(sums):
    vmem = pl.BlockSpec(memory_space=pltpu.VMEM)
    shapes = ((1, D), (D, D), (D, 192), (D, 192), (D, D), (1, D), (D, FF), (D, FF), (FF, D))
    return pl.pallas_call(
        unpack_kernel,
        out_shape=tuple(jax.ShapeDtypeStruct(s, f32) for s in shapes),
        in_specs=[vmem] * 3,
        out_specs=(vmem,) * len(shapes),
        compiler_params=pltpu.CompilerParams(vmem_limit_bytes=VMEM_LIMIT),
        name="unpack",
    )(*[s.reshape(N_CTX, FINAL_ROWS, 128) for s in sums])


def on_device(
    layer_input,
    attn_gain,
    w_query,
    w_key,
    w_value,
    w_out,
    mlp_gain,
    w_gate,
    w_up,
    w_down,
    cotangent,
    segment_ids,
    pair_table,
):
    own_pair = pair_table[0]
    within = jnp.arange(ROWS, dtype=jnp.int32)
    blocks = jnp.where(within < HALF, own_pair, 2 * N_CTX - 1 - own_pair)
    places = blocks * HALF + within % HALF
    lanes = jnp.arange(128, dtype=jnp.int32)
    frequency = ROPE_THETA ** (-2.0 * (lanes % (HEAD_DIM // 2)).astype(f32) / HEAD_DIM)
    turned = places.astype(f32)[:, None] * frequency[None, :]
    cos_wide = jnp.cos(turned)
    sin_wide = jnp.sin(turned) * jnp.where(lanes % HEAD_DIM < HEAD_DIM // 2, -1.0, 1.0)[None, :]

    documents = jnp.arange(DOCS, dtype=jnp.int32)
    earlier = jnp.sum((segment_ids[None, :] < documents[:, None]).astype(f32), axis=1)
    meta = jnp.concatenate([own_pair.astype(f32)[None], earlier]).astype(bf16)
    meta = jnp.pad(meta[None, :], ((0, META - 1), (0, 128 - DOCS - 1)))
    gain_one, gain_two = attn_gain[None, :], mlp_gain[None, :]
    q_rot, normed, kv0, kv1, kv2 = project_and_gather(
        layer_input, gain_one, w_query, w_key, w_value, cos_wide, sin_wide, meta
    )
    metas = kv0.reshape(N_CTX, SLAB, 128)[:, ROWS, : DOCS + 1].astype(f32)
    pairs = metas[:, 0].astype(jnp.int32)
    starts = jnp.sum(metas[:, 1:], axis=0).astype(jnp.int32)
    numbers = jnp.arange(N_CTX, dtype=jnp.int32)
    holder = jnp.sum(jnp.where(pairs[None, :] == numbers[:, None], numbers[None, :], 0), axis=1)
    source = jnp.concatenate([holder * ROWS, holder[::-1] * ROWS + HALF])
    doc_start = jnp.sum(
        jnp.where(segment_ids[:, None] == documents[None, :], starts[None, :], 0), axis=1
    )
    row_info = jnp.tile(
        jnp.stack([places[:HALF], doc_start[:HALF], places[HALF:], doc_start[HALF:]]), (1, HEADS)
    )
    info = jnp.stack(
        [own_pair // PIECES, doc_start[HALF] // CHUNK, (2 * N_CTX - 1 - own_pair) // PIECES]
    )
    result, grad_hidden, dq, dkv0, dkv1, dkv2, dw0, dw1, dw2 = layer(
        source,
        info,
        [kv0.reshape(N_CTX * SLAB, 128), kv1.reshape(TOKENS, 128), kv2.reshape(TOKENS, 128)],
        [w_out, w_gate, w_up, w_down],
        q_rot,
        row_info,
        layer_input,
        cotangent,
        gain_two,
    )
    lead = (SIDE, SIDE, SIDE, 2)
    grad_x, *sums = reduce_all(
        [d.reshape(lead + (ROWS, 128)) for d in (dkv0, dkv1, dkv2)],
        [d.reshape(lead + (BAND_ROWS, 128)) for d in (dw0, dw1, dw2)],
        dq,
        normed,
        layer_input,
        grad_hidden,
        cos_wide,
        sin_wide,
        gain_one,
        w_query,
        w_key,
        w_value,
    )
    ga, gq, gk, gv, go, gm, gg, gu, gd = unpack(sums)
    return (result, grad_x, ga[0], gq, gk, gv, go, gm[0], gg, gu, gd)


def solution(mesh):
    return jax.shard_map(
        on_device,
        mesh=mesh,
        in_specs=(
            P("ctx", None),
            P(),
            P(),
            P(),
            P(),
            P(),
            P(),
            P(),
            P(),
            P(),
            P("ctx", None),
            P("ctx"),
            P("ctx"),
        ),
        out_specs=(P("ctx", None), P("ctx", None), P(), P(), P(), P(), P(), P(), P(), P(), P()),
        check_vma=False,
    )
```

```python
import functools
import jax
import jax.numpy as jnp
from jax import lax
from jax.experimental import pallas as pl
from jax.experimental.pallas import tpu as pltpu
from jax.sharding import PartitionSpec as P

f32 = jnp.float32
bf16 = jnp.bfloat16
D = 576
HEADS = 9
KV_HEADS = 3
HEAD_DIM = 64
PER_GROUP = HEADS // KV_HEADS
FF = 1536
NORM_EPS = 1e-05
ROPE_THETA = 100000.0
ROWS = 128
HALF = 64
N_CTX = 128
TOKENS = ROWS * N_CTX
DOCS = 18
META = 16
SLAB = ROWS + META
CHUNK = 512
PIECES = CHUNK // HALF
CHUNKS = TOKENS // CHUNK
COLS = HEADS * HALF
NEG = -1e30
SCALE = HEAD_DIM ** (-0.5)
VMEM_LIMIT = 56 * 1024 * 1024

K_AT = (0, 64, 128)
V_AT = (128, 192, 64)

GATE_AT = 0
UP_AT = GATE_AT + 12 * D
DOWN_AT = UP_AT + 12 * D
OUT_AT = DOWN_AT + 12 * D
GAIN_AT = OUT_AT + 5 * D
BAND_ROWS = 64
FF_ROWS = 3 * N_CTX * BAND_ROWS
Q_AT = 0
KV_AT = Q_AT + 5 * D
GAIN_ONE_AT = KV_AT + 5 * 384
BAND_ROWS_ONE = 16
ATT_ROWS = 3 * N_CTX * BAND_ROWS_ONE

MESH = pl.DeviceIdType.MESH
SIDE = 4
ORDERS = ((2, 1, 0), (1, 0, 2), (0, 2, 1))
STRIDES = (32, 8, 2)


def whereabouts():
    me = lax.axis_index("ctx")
    coords = (me // 32, lax.rem(me // 8, SIDE), lax.rem(me // 2, SIDE))
    return me, coords, lax.rem(me, 2)


def wrap(coord, step):
    return lax.rem(coord + (step + SIDE), SIDE)


def neighbour(me, coords, axis, step):
    return me + (wrap(coords[axis], step) - coords[axis]) * STRIDES[axis]


def greet(me, coords, core):
    barrier = pltpu.get_barrier_semaphore()
    others = [me + 1 - 2 * core]
    for axis in range(3):
        others += [neighbour(me, coords, axis, step) for step in (1, -1, 2)]
    for other in others:
        pl.semaphore_signal(barrier, inc=1, device_id=(other,), device_id_type=MESH)
    pl.semaphore_wait(barrier, len(others))


def half_rows(rows):
    return rows // 32 * 16


class Pool:
    def __init__(self, sems):
        self.sems = sems
        self.used = 0

    def new(self):
        self.used += 1
        return self.sems.at[self.used - 1]


def send(src, dst, device, send_sem, recv_sem):
    pltpu.make_async_remote_copy(
        src_ref=src,
        dst_ref=dst,
        send_sem=send_sem,
        recv_sem=recv_sem,
        device_id=(device,),
        device_id_type=MESH,
    ).start()


def wait_for(ref, sem):
    pltpu.make_async_copy(ref, ref, sem).wait()


def at_axes(order, values):
    index = [None] * 3
    for axis, value in zip(order, values):
        index[axis] = value
    return tuple(index)


WHOLE = pl.ds(0, SIDE)


def gather_steps(own, out, pool, ring=True):
    me, coords, core = whereabouts()
    sibling = me + 1 - 2 * core
    bands = range(len(own))
    orders = [ORDERS[band % 3] for band in bands]
    lines = (0, 1, -1, 2)
    steps = (1, -1, 2)

    def place(band, *values):
        return out[band].at[at_axes(orders[band], values) + (core,)]

    def mine(band, phase, step=0):
        return wrap(coords[orders[band][phase]], step)

    def device(band, phase, step):
        return neighbour(me, coords, orders[band][phase], step)

    homes = [pool.new() for band in bands]
    sent = [[pool.new() for phase in range(3)] for band in bands]
    across = [(pool.new(), pool.new()) for band in bands]
    came = [[pool.new() for phase in range(3)] for band in bands]
    ends = {}
    for step in steps:
        for phase in (1, 0):
            for band in bands:
                part = place(band, *(mine(band, p) for p in range(3)))
                send(own[band], part, device(band, phase, step), sent[band][0], came[band][phase])
    for band in bands:
        part = place(band, *(mine(band, p) for p in range(3)))
        pltpu.make_async_copy(own[band], part, homes[band]).start()

    def send_line(band, line):
        part = place(band, mine(band, 0, line), WHOLE, mine(band, 2))
        if ring:
            ends[band, line] = (pool.new(), pool.new(), pool.new())
            send(part, part, device(band, 2, 1), sent[band][2], ends[band, line][0])
            send(part, part, device(band, 2, -1), sent[band][2], ends[band, line][1])
        else:
            if line == 0:
                ends[band] = pool.new()
            for step in steps:
                send(part, part, device(band, 2, step), sent[band][2], ends[band])

    yield
    for band in bands:
        wait_for(own[band], homes[band])
        wait_for(out[band].at[0, 0, 0:3, 0], came[band][1])
        send_line(band, 0)
    for band in bands:
        wait_for(out[band].at[0, 0, 0:3, 0], came[band][0])
        for line in lines[1:]:
            part = place(band, mine(band, 0, line), mine(band, 1), mine(band, 2))
            for step in steps:
                send(part, part, device(band, 1, step), sent[band][1], came[band][2])
    yield
    for band in bands:
        wait_for(out[band].at[0, 0:3, 0:3, 0], came[band][2])
        for line in lines[1:]:
            send_line(band, line)
    for band in bands:
        part = place(band, WHOLE, WHOLE, mine(band, 2))
        send(part, part, sibling, *across[band])
    if ring:
        for line in lines:
            yield
            for band in bands:
                rows = own[band].shape[0]
                cut = half_rows(rows)
                for side, step, lo, size in ((0, -1, 0, cut), (1, 1, cut, rows - cut)):
                    part = place(band, mine(band, 0, line), WHOLE, mine(band, 2, step))
                    wait_for(part, ends[band, line][side])
                    half = part.at[:, pl.ds(lo, size)]
                    send(half, half, device(band, 2, -step), sent[band][2], ends[band, line][2])
                    send(part, part, sibling, *across[band])
        for line in lines:
            yield
            for band in bands:
                part = place(band, mine(band, 0, line), WHOLE, mine(band, 2, 2))
                wait_for(part, ends[band, line][2])
                send(part, part, sibling, *across[band])
    else:
        yield
        for band in bands:
            wait_for(out[band].at[0:3, :, :, 0], ends[band])
            for step in steps:
                part = place(band, WHOLE, WHOLE, mine(band, 2, step))
                send(part, part, sibling, *across[band])
    yield
    for band in bands:
        wait_for(out[band].at[:, :, :, 0], across[band][1])
        wait_for(out[band].at[:, :, :, 0], across[band][0])
        wait_for(out[band].at[0, 0:2, 0:3, 0], sent[band][0])
        wait_for(out[band].at[0, 0:3, 0:3, 0], sent[band][1])
        wait_for(out[band].at[0:3, :, :, 0], sent[band][2])


GATHER_SEMS = 3 * (1 + 3 + 2 + 3 + 12)
GATHER_SEMS_ONE = 3 * (1 + 3 + 2 + 3 + 1)


def run(steps):
    for _ in steps:
        pass


def scatter_scratch(rows, ring):
    shapes = [pltpu.VMEM((SIDE, SIDE, SIDE, rows, 128), bf16)] * 6
    for _ in range(3):
        shapes += [
            pltpu.VMEM((3, SIDE, SIDE, rows, 128), bf16),
            pltpu.VMEM((3, SIDE, rows, 128), bf16),
            pltpu.VMEM((3, rows, 128), bf16),
        ]
    return shapes + [pltpu.SemaphoreType.DMA((3 * (4 + 16 + 4 + 8 + 2 if ring else 4 + 1 + 1 + 3),))]


SCATTER_REFS = 16


def scatter_steps(parts, done, scratch, ring):
    acc, sib = scratch[0:3], scratch[3:6]
    landing = [scratch[6 + 3 * b : 9 + 3 * b] for b in range(3)]
    pool = Pool(scratch[15])
    me, coords, core = whereabouts()
    sibling = me + 1 - 2 * core
    bands = range(3)
    steps = (2, 1, -1, 0)
    rows = acc[0].shape[3]
    cut = half_rows(rows)
    sent = [[pool.new() for phase in range(4)] for band in bands]
    homes, swaps = {}, {}
    if ring:
        for step in steps:
            for band in bands:
                order = ORDERS[band]
                plane = at_axes(order, (wrap(coords[order[0]], step), WHOLE, WHOLE))
                homes[band, step] = pool.new()
                top = 0
                for part in parts[band]:
                    size = part.shape[4]
                    pltpu.make_async_copy(
                        part.at[plane + (core,)],
                        acc[band].at[plane + (pl.ds(top, size),)],
                        homes[band, step],
                    ).start()
                    top += size
            for sub in range(SIDE):
                for band in bands:
                    order = ORDERS[band]
                    line = at_axes(order, (wrap(coords[order[0]], step), sub, WHOLE))
                    swaps[band, step, sub] = pool.new()
                    top = 0
                    for part in parts[band]:
                        size = part.shape[4]
                        send(
                            part.at[line + (1 - core,)],
                            sib[band].at[line + (pl.ds(top, size),)],
                            sibling,
                            sent[band][3],
                            swaps[band, step, sub],
                        )
                        top += size
    else:
        for band in bands:
            homes[band], swaps[band] = pool.new(), pool.new()
            (part,) = parts[band]
            pltpu.make_async_copy(part.at[:, :, :, core], acc[band], homes[band]).start()
            send(part.at[:, :, :, 1 - core], sib[band], sibling, sent[band][3], swaps[band])

    def add_swap(band, step, sub):
        order = ORDERS[band]
        first = wrap(coords[order[0]], step)
        if sub == 0:
            plane = acc[band].at[at_axes(order, (first, WHOLE, WHOLE))]
            wait_for(plane, homes[band, step])
        wait_for(sib[band].at[at_axes(order, (first, sub, WHOLE))], swaps[band, step, sub])

        def body(last, carry):
            at = at_axes(order, (first, sub, last))
            acc[band][at] = acc[band][at] + sib[band][at]
            return carry

        lax.fori_loop(0, SIDE, body, 0)

    jobs = [(sub, band) for sub in range(SIDE) for band in bands]

    def line_at(band, step, sub):
        order = ORDERS[band]
        return at_axes(order, (wrap(coords[order[0]], step), sub, WHOLE))

    def sum_up(band, index_of, landed):
        def body(last, carry):
            at = index_of(last)
            total = acc[band][at].astype(f32)
            for ref in landed(last):
                total = total + ref.astype(f32)
            acc[band][at] = total.astype(bf16)
            return carry

        lax.fori_loop(0, SIDE, body, 0)

    if ring:
        passing, ending = {}, {}
        for sub, band in jobs:
            if band == 0:
                yield
            axis = ORDERS[band][0]
            add_swap(band, 2, sub)
            far = acc[band].at[line_at(band, 2, sub)]
            passing[sub, band], ending[sub, band] = pool.new(), pool.new()
            for slot, lo, size, step in ((0, 0, cut, 1), (0, cut, rows - cut, -1)):
                send(
                    far.at[:, pl.ds(lo, size)],
                    landing[band][0].at[slot, sub, :, pl.ds(lo, size)],
                    neighbour(me, coords, axis, step),
                    sent[band][0],
                    passing[sub, band],
                )
        for sub, band in jobs:
            if band == 0:
                yield
            axis = ORDERS[band][0]
            add_swap(band, 1, sub)
            add_swap(band, -1, sub)
            wait_for(landing[band][0].at[0, sub], passing[sub, band])
            for slot, lo, size, step in ((1, 0, cut, 1), (2, cut, rows - cut, -1)):

                def body(last, carry, lo=lo, size=size, step=step):
                    order = ORDERS[band]
                    at = at_axes(order, (wrap(coords[order[0]], step), sub, last)) + (pl.ds(lo, size),)
                    acc[band][at] = acc[band][at] + landing[band][0][0, sub, last, lo : lo + size]
                    return carry

                lax.fori_loop(0, SIDE, body, 0)
                send(
                    acc[band].at[line_at(band, step, sub)],
                    landing[band][0].at[slot, sub],
                    neighbour(me, coords, axis, step),
                    sent[band][0],
                    ending[sub, band],
                )
        for sub, band in jobs:
            if band == 0:
                yield
            order = ORDERS[band]
            add_swap(band, 0, sub)
            wait_for(landing[band][0].at[1:3, sub], ending[sub, band])
            sum_up(
                band,
                lambda last: at_axes(order, (coords[order[0]], sub, last)),
                lambda last: [landing[band][0][slot, sub, last] for slot in (1, 2)],
            )
    else:
        came = [pool.new() for band in bands]
        yield
        for band in bands:
            axis = ORDERS[band][0]
            wait_for(acc[band], homes[band])
            wait_for(sib[band], swaps[band])
            acc[band][...] = acc[band][...] + sib[band][...]
            for slot, step in enumerate((2, 1, -1)):
                plane = at_axes(ORDERS[band], (wrap(coords[axis], step), WHOLE, WHOLE))
                send(
                    acc[band].at[plane],
                    landing[band][0].at[slot],
                    neighbour(me, coords, axis, step),
                    sent[band][0],
                    came[band],
                )
        yield
        for band in bands:
            plane = at_axes(ORDERS[band], (coords[ORDERS[band][0]], WHOLE, WHOLE))
            wait_for(landing[band][0], came[band])
            total = acc[band][plane].astype(f32)
            for slot in range(3):
                total = total + landing[band][0][slot].astype(f32)
            acc[band][plane] = total.astype(bf16)
    came = [pool.new() for band in bands]
    for slot, step in enumerate((2, 1, -1)):
        for band in bands:
            order = ORDERS[band]
            line = at_axes(order, (coords[order[0]], wrap(coords[order[1]], step), WHOLE))
            send(
                acc[band].at[line],
                landing[band][1].at[slot],
                neighbour(me, coords, order[1], step),
                sent[band][1],
                came[band],
            )
    yield
    ends = [pool.new() for band in bands]
    for band in bands:
        order = ORDERS[band]
        wait_for(landing[band][1], came[band])
        sum_up(
            band,
            lambda last: at_axes(order, (coords[order[0]], coords[order[1]], last)),
            lambda last: [landing[band][1][slot, last] for slot in range(3)],
        )
        for slot, step in enumerate((2, 1, -1)):
            at = at_axes(order, (coords[order[0]], coords[order[1]], wrap(coords[order[2]], step)))
            send(
                acc[band].at[at],
                landing[band][2].at[slot],
                neighbour(me, coords, order[2], step),
                sent[band][2],
                ends[band],
            )
    yield
    for band in bands:
        wait_for(landing[band][2], ends[band])
        total = acc[band][coords].astype(f32)
        for slot in range(3):
            total = total + landing[band][2][slot].astype(f32)
        done[band][...] = total
    for band in bands:
        wait_for(acc[band].at[0:3], sent[band][0])
        wait_for(acc[band].at[0, 0:3], sent[band][1])
        wait_for(acc[band].at[0, 0, 0:3], sent[band][2])
        wait_for(acc[band], sent[band][3])


def rms_parts(features):
    return lax.rsqrt(jnp.mean(features * features, axis=-1, keepdims=True) + NORM_EPS)


def rms_back(features, gain, grad):
    inverse = rms_parts(features)
    scaled = grad * gain
    inner = jnp.mean(scaled * features, axis=-1, keepdims=True)
    by_features = inverse * scaled - features * (inverse * inverse * inverse * inner)
    by_gain = jnp.sum(grad * features * inverse, axis=0, keepdims=True)
    return by_features, by_gain


def nt_dot(left, right):
    return lax.dot_general(left, right, (((1,), (1,)), ((), ())), preferred_element_type=f32)


def tn_dot(left, right):
    return lax.dot_general(left, right, (((0,), (0,)), ((), ())), preferred_element_type=f32)


def nn_dot(left, right):
    return jnp.dot(left, right, preferred_element_type=f32)


def turn(tile, cos_wide, sin_wide):
    lanes = lax.broadcasted_iota(jnp.int32, tile.shape, 1)
    swapped = jnp.where(
        lax.rem(lanes, HEAD_DIM) < HEAD_DIM // 2, pltpu.roll(tile, 96, 1), pltpu.roll(tile, 32, 1)
    )
    return tile * cos_wide + swapped * sin_wide


def project_kernel(
    pair_ref, x_ref, gain_ref, wq_ref, wk_ref, wv_ref, cos_ref, sin_ref, seg_ref,
    q_ref, n_ref, out0, out1, out2,
    own0, own1, own2, sems,
):
    me, coords, core = whereabouts()
    features = x_ref[...].astype(f32).T
    normed = (features * rms_parts(features) * gain_ref[...].reshape(1, D)).astype(bf16)
    n_ref[...] = normed
    cos_wide, sin_wide = cos_ref[...], sin_ref[...]
    keys = nt_dot(normed, wk_ref[...])
    values = nt_dot(normed, wv_ref[...]).astype(bf16)
    queries = nn_dot(normed, wq_ref[...])
    own0[0:ROWS, :] = turn(keys[:, 0:128], cos_wide, sin_wide).astype(bf16)
    segments = jnp.broadcast_to(seg_ref[...].astype(f32), (ROWS, ROWS)).T
    lanes = lax.broadcasted_iota(jnp.int32, (ROWS, ROWS), 1)
    earlier = jnp.sum(jnp.where(segments < (lanes - 1).astype(f32), 1.0, 0.0), axis=0, keepdims=True)
    meta = jnp.where(lanes[0:1] == 0, pair_ref[0].astype(f32), earlier)
    own0[ROWS:SLAB, :] = jnp.broadcast_to(meta, (META, 128)).astype(bf16)
    mixed = turn(jnp.concatenate([keys[:, 128:192], queries[:, 512:576]], 1), cos_wide, sin_wide)
    own1[...] = jnp.concatenate([mixed[:, 0:64].astype(bf16), values[:, 128:192]], 1)
    own2[...] = values[:, 0:128]
    greet(me, coords, core)
    steps = gather_steps((own0, own1, own2), (out0, out1, out2), Pool(sems))
    next(steps)
    for tile in range(4):
        at = slice(128 * tile, 128 * tile + 128)
        q_ref[:, at] = (turn(queries[:, at], cos_wide, sin_wide).astype(bf16).astype(f32) * SCALE).astype(bf16)
    q_ref[:, 512:576] = (mixed[:, 64:128].astype(bf16).astype(f32) * SCALE).astype(bf16)
    run(steps)


def project_and_gather(pair, x, gain, wq, wk, wv, cos_wide, sin_wide, segments):
    vmem = pl.BlockSpec(memory_space=pltpu.VMEM)
    anywhere = pl.BlockSpec(memory_space=pl.ANY)
    rows = (SLAB, ROWS, ROWS)
    return pl.pallas_call(
        project_kernel,
        out_shape=(
            jax.ShapeDtypeStruct((ROWS, D), bf16),
            jax.ShapeDtypeStruct((ROWS, D), bf16),
        )
        + tuple(jax.ShapeDtypeStruct((SIDE, SIDE, SIDE, 2, r, 128), bf16) for r in rows),
        in_specs=[pl.BlockSpec(memory_space=pltpu.SMEM)] + [vmem] * 8,
        out_specs=(vmem, vmem, anywhere, anywhere, anywhere),
        scratch_shapes=[pltpu.VMEM((r, 128), bf16) for r in rows]
        + [pltpu.SemaphoreType.DMA((GATHER_SEMS,))],
        compiler_params=pltpu.CompilerParams(
            collective_id=1, has_side_effects=True, vmem_limit_bytes=VMEM_LIMIT
        ),
        name="project_and_gather",
    )(pair, x, gain, wq, wk, wv, cos_wide, sin_wide, segments)


def needed(chunk, a_hi, b_lo, b_hi):
    return (chunk <= a_hi) | ((chunk >= b_lo) & (chunk <= b_hi))


def chunk_rows(chunk, count=1):
    return pl.ds(pl.multiple_of(chunk * CHUNK, CHUNK), count * CHUNK)


def wait_chunk(chunk, held, sem):
    window = held.at[chunk_rows(chunk)]
    pltpu.make_async_copy(window, window, sem.at[chunk]).wait()


def chunk_mask(chunk, place_row, start_row):
    keys = chunk * CHUNK + lax.broadcasted_iota(jnp.int32, (CHUNK, COLS), 0)
    return (keys <= place_row) & (keys >= start_row)


def layer_kernel(
    pair_ref,
    kv0, kv1, kv2, wo_hbm, wg_hbm, wu_hbm, wd_hbm,
    q_ref, seg_ref, x_ref, c_ref, gain_ref,
    result_ref, gh_ref, dq_ref, dkv0, dkv1, dkv2, dw0, dw1, dw2,
    held, sem, wo_ref, wg_ref, wu_ref, wd_ref, w_sem, q_spread, g_spread, mixed, top, total, att_ref,
    delta_ref, dw, dw_sem, staged, blank, out_sem, blank_sem, gain_rows,
    rows_ref, meta_ref, meta_sem, table_ref, table,
):
    kvs, dkvs, dws = (kv0, kv1, kv2), (dkv0, dkv1, dkv2), (dw0, dw1, dw2)
    weights = [
        pltpu.make_async_copy(src, dst, w_sem.at[i])
        for i, (src, dst) in enumerate(
            ((wo_hbm, wo_ref), (wg_hbm, wg_ref), (wu_hbm, wu_ref), (wd_hbm, wd_ref))
        )
    ]
    metas = pltpu.make_async_copy(kv0.at[:, pl.ds(ROWS, META)], meta_ref, meta_sem.at[0])
    metas.start()
    for copy in weights:
        copy.start()
    pair = pair_ref[0]
    metas.wait()
    columns = meta_ref[:, 0, :].astype(f32)
    starts = jnp.sum(columns, axis=0, keepdims=True)
    numbers = lax.broadcasted_iota(jnp.int32, (N_CTX, N_CTX), 0).astype(f32)
    lanes = lax.broadcasted_iota(jnp.int32, (N_CTX, N_CTX), 1).astype(f32)
    holders = jnp.sum(jnp.where(columns[:, 0:1] == lanes, numbers, 0.0), axis=0, keepdims=True)
    segments = seg_ref[...].astype(f32)
    row_starts = jnp.zeros((1, ROWS), f32)
    for document in range(DOCS):
        row_starts = jnp.where(
            segments == float(document), starts[:, document + 1 : document + 2], row_starts
        )
    for block in range(2):
        first = pair if block == 0 else 2 * N_CTX - 1 - pair
        places = first * HALF + lax.rem(lax.broadcasted_iota(jnp.int32, (1, COLS), 1), HALF)
        rows_ref[2 * block : 2 * block + 1, :] = places
        mine = row_starts[:, block * HALF : (block + 1) * HALF].astype(jnp.int32)
        rows_ref[2 * block + 1 : 2 * block + 2, :] = jnp.concatenate([mine] * HEADS, 1)
    table_ref[...] = jnp.zeros_like(table_ref)
    table_ref[0:1, :] = holders.astype(jnp.int32)
    table_ref[1:2, :] = row_starts.astype(jnp.int32)
    tables = pltpu.make_async_copy(table_ref, table, meta_sem.at[1])
    tables.start()
    tables.wait()
    a_hi, b_lo, b_hi = pair // PIECES, table[1, HALF] // CHUNK, (2 * N_CTX - 1 - pair) // PIECES

    def slot_of(block_number):
        low = table[0, jnp.minimum(block_number, 2 * N_CTX - 1 - block_number)]
        return low * ROWS + jnp.where(block_number < N_CTX, 0, HALF)


    def issue(chunk, carry):
        @pl.when(needed(chunk, a_hi, b_lo, b_hi))
        def _():
            for piece in range(PIECES):
                slot = slot_of(chunk * PIECES + piece)
                rows = pl.ds(pl.multiple_of(chunk * CHUNK + piece * HALF, HALF), HALF)
                device, top = slot // ROWS, pl.multiple_of(lax.rem(slot, ROWS), HALF)
                for band in range(3):
                    pltpu.make_async_copy(
                        kvs[band].at[device, pl.ds(top, HALF)],
                        held.at[rows, 128 * band : 128 * band + 128],
                        sem.at[chunk],
                    ).start()

        return carry

    lax.fori_loop(0, CHUNKS, issue, 0)

    def spread(rows, place, windows):
        for block in range(2):
            for head in range(HEADS):
                tile = rows[block * HALF : (block + 1) * HALF, head * HEAD_DIM : (head + 1) * HEAD_DIM]
                at = windows[head // PER_GROUP]
                place[block, head * HALF : (head + 1) * HALF, at : at + HEAD_DIM] = tile

    def unspread(columns, place, block, windows):
        for head in range(HEADS):
            at = windows[head // PER_GROUP]
            tile = columns[at : at + HEAD_DIM, head * HALF : (head + 1) * HALF]
            place[block * HALF : (block + 1) * HALF, head * HEAD_DIM : (head + 1) * HEAD_DIM] = tile.T

    blank[...] = jnp.zeros_like(blank)

    def zero_copy(band, row):
        return pltpu.make_async_copy(blank, dkvs[band].at[pl.ds(row, HALF)], blank_sem)

    def clear(chunk, carry):
        @pl.when(jnp.logical_not(needed(chunk, a_hi, b_lo, b_hi)))
        def _():
            for piece in range(PIECES):
                row = pl.multiple_of(slot_of(chunk * PIECES + piece), HALF)
                for band in range(3):
                    zero_copy(band, row).start()

        return carry

    lax.fori_loop(0, CHUNKS, clear, 0)
    q_spread[...] = jnp.zeros_like(q_spread)
    g_spread[...] = jnp.zeros_like(g_spread)
    spread(q_ref[...], q_spread, K_AT)
    mixed[...] = jnp.zeros_like(mixed)
    top[...] = jnp.full_like(top, NEG)
    total[...] = jnp.zeros_like(total)

    def mask_of(block, chunk):
        return chunk_mask(
            chunk, rows_ref[2 * block : 2 * block + 1, :], rows_ref[2 * block + 1 : 2 * block + 2, :]
        )

    def forward(block, chunk, masked, count=1):
        window = chunk_rows(chunk, count)
        scores = nt_dot(held[window, 0:256], q_spread[block])
        if masked:
            scores = jnp.where(mask_of(block, chunk), scores, NEG)
        old = top[block : block + 1, :]
        new = jnp.maximum(old, jnp.max(scores, axis=0, keepdims=True))
        probs = jnp.exp(scores - new)
        shrink = jnp.exp(old - new)
        top[block : block + 1, :] = new
        total[block : block + 1, :] = total[block : block + 1, :] * shrink + jnp.sum(
            probs, axis=0, keepdims=True
        )
        values = held[window, 128:384].T[64:256]
        mixed[block, 64:256] = mixed[block, 64:256] * shrink + nn_dot(values, probs.astype(bf16))

    def forward_step(chunk, carry):
        in_b = (chunk >= b_lo) & (chunk <= b_hi)

        @pl.when(needed(chunk, a_hi, b_lo, b_hi))
        def _():
            wait_chunk(chunk, held, sem)

        @pl.when(chunk <= a_hi)
        def _():
            forward(0, chunk, True)

        @pl.when(in_b)
        def _():
            forward(1, chunk, True)

        return carry

    def forward_pair(pair_of, carry):
        wait_chunk(2 * pair_of, held, sem)
        wait_chunk(2 * pair_of + 1, held, sem)
        forward(0, 2 * pair_of, False, 2)
        return carry

    plain = jnp.minimum(a_hi, b_lo) // 2
    lax.fori_loop(0, plain, forward_pair, 0)
    lax.fori_loop(2 * plain, b_hi + 1, forward_step, 0)
    for block in range(2):
        sums = total[block : block + 1, :]
        top[block : block + 1, :] = top[block : block + 1, :] + jnp.log(sums)
        mixed[block] = mixed[block] / sums
        unspread(mixed.at[block], att_ref, block, V_AT)

    attended = att_ref[...].astype(bf16)
    cotangent = c_ref[...].astype(f32).T.astype(bf16)
    gain = gain_ref[...].reshape(1, D)
    for copy in weights:
        copy.wait()
    hidden = x_ref[...].astype(f32).T + nn_dot(attended, wo_ref[...])
    normed = (hidden * rms_parts(hidden) * gain).astype(bf16)
    gate = nn_dot(normed, wg_ref[...])
    upward = nn_dot(normed, wu_ref[...])
    open_gate = jax.nn.sigmoid(gate)
    silu = gate * open_gate
    active = (silu * upward).astype(bf16)
    result_ref[...] = (hidden + nt_dot(active, wd_ref[...])).T.astype(bf16)
    grad_active = nn_dot(cotangent, wd_ref[...])
    grad_gate = (grad_active * upward * open_gate * (1.0 + gate * (1.0 - open_gate))).astype(bf16)
    grad_up = (grad_active * silu).astype(bf16)
    grad_normed = nt_dot(grad_gate, wg_ref[...]) + nt_dot(grad_up, wu_ref[...])
    by_hidden, by_gain = rms_back(hidden, gain, grad_normed)
    grad_hidden = cotangent.astype(f32) + by_hidden
    gh_ref[...] = grad_hidden
    grad_out = grad_hidden.astype(bf16)
    spread(nt_dot(grad_out, wo_ref[...]).astype(bf16), g_spread, V_AT)
    for block in range(2):
        turned = g_spread[block].astype(f32).T
        delta_ref[block : block + 1, :] = jnp.sum(turned * mixed[block], axis=0, keepdims=True)

    def pack(at, grads):
        rows = grads.shape[0]
        for tile in range(grads.shape[1] // 128):
            dw[at + tile * rows : at + (tile + 1) * rows, :] = grads[:, 128 * tile : 128 * tile + 128].astype(bf16)
        if grads.shape[1] % 128:
            tile = grads.shape[1] // 128
            dw[at + tile * rows : at + (tile + 1) * rows, 0:64] = grads[:, 128 * tile : 128 * tile + 64].astype(bf16)
            dw[at + tile * rows : at + (tile + 1) * rows, 64:128] = jnp.zeros((rows, 64), bf16)

    pack(GATE_AT, tn_dot(normed, grad_gate))
    pack(UP_AT, tn_dot(normed, grad_up))
    pack(DOWN_AT, tn_dot(cotangent, active))
    pack(OUT_AT, tn_dot(attended, grad_out))
    gain_rows[...] = jnp.zeros_like(gain_rows)
    for tile in range(4):
        gain_rows[tile : tile + 1, :] = by_gain[:, 128 * tile : 128 * tile + 128]
    gain_rows[4:5, 0:64] = by_gain[:, 512:576]
    dw[GAIN_AT : GAIN_AT + 16, :] = gain_rows[...].astype(bf16)
    dw[GAIN_AT + 16 : FF_ROWS, :] = jnp.zeros((FF_ROWS - GAIN_AT - 16, 128), bf16)
    band_rows = FF_ROWS // 3
    dw_copies = [
        pltpu.make_async_copy(dw.at[pl.ds(band * band_rows, band_rows)], dws[band], dw_sem.at[band])
        for band in range(3)
    ]
    for copy in dw_copies:
        copy.start()

    mixed[...] = jnp.zeros_like(mixed)

    def backward(block, chunk, masked, mode, count=1):
        window = chunk_rows(chunk, count)
        keys = held[window, 0:256]
        values = held[window, 128:384]
        scores = nt_dot(keys, q_spread[block])
        probs = jnp.exp(scores - top[block : block + 1, :])
        if masked:
            probs = jnp.where(mask_of(block, chunk), probs, 0.0)
        grad_probs = nt_dot(values, g_spread[block])
        grad_scores = (probs * (grad_probs - delta_ref[block : block + 1, :])).astype(bf16)
        mixed[block, 0:192] += nn_dot(keys.T[0:192], grad_scores)
        dk = nn_dot(grad_scores, q_spread[block])
        dv = nn_dot(probs.astype(bf16), g_spread[block])
        parts = (dk[:, 0:128], dk[:, 128:256] + dv[:, 0:128], dv[:, 128:256])
        for band in range(3):
            at = slice(128 * band, 128 * band + 128)
            if mode == "first":
                staged[:, at] = parts[band]
            elif mode == "second":
                held[window, at] = (staged[:, at] + parts[band]).astype(bf16)
            else:
                held[window, at] = parts[band].astype(bf16)

    def put_back(chunk):
        for piece in range(PIECES):
            row = pl.multiple_of(slot_of(chunk * PIECES + piece), HALF)
            rows = pl.ds(pl.multiple_of(chunk * CHUNK + piece * HALF, HALF), HALF)
            for band in range(3):
                pltpu.make_async_copy(
                    held.at[rows, 128 * band : 128 * band + 128],
                    dkvs[band].at[pl.ds(row, HALF)],
                    out_sem.at[chunk],
                ).start()

    def backward_step(chunk, carry):
        in_a = chunk <= a_hi
        in_b = (chunk >= b_lo) & (chunk <= b_hi)

        @pl.when(in_a & jnp.logical_not(in_b))
        def _():
            backward(0, chunk, True, "only")

        @pl.when(in_b & jnp.logical_not(in_a))
        def _():
            backward(1, chunk, True, "only")

        @pl.when(in_a & in_b)
        def _():
            backward(0, chunk, True, "first")
            backward(1, chunk, True, "second")

        @pl.when(in_a | in_b)
        def _():
            put_back(chunk)

        return carry

    def backward_pair(pair_of, carry):
        backward(0, 2 * pair_of, False, "only", 2)
        put_back(2 * pair_of)
        put_back(2 * pair_of + 1)
        return carry

    lax.fori_loop(0, plain, backward_pair, 0)
    lax.fori_loop(2 * plain, b_hi + 1, backward_step, 0)
    for block in range(2):
        unspread(mixed.at[block], dq_ref, block, K_AT)

    def drain(chunk, carry):
        use = needed(chunk, a_hi, b_lo, b_hi)

        @pl.when(use)
        def _():
            wait_chunk(chunk, held, out_sem)

        @pl.when(jnp.logical_not(use))
        def _():
            for _piece in range(PIECES):
                for band in range(3):
                    zero_copy(band, 0).wait()

        return carry

    lax.fori_loop(0, CHUNKS, drain, 0)
    for copy in dw_copies:
        copy.wait()


def layer(pair, kvs, weights, q, segments, x, cotangent, gain):
    vmem = pl.BlockSpec(memory_space=pltpu.VMEM)
    anywhere = pl.BlockSpec(memory_space=pl.ANY)
    return pl.pallas_call(
        layer_kernel,
        out_shape=(
            jax.ShapeDtypeStruct((D, ROWS), bf16),
            jax.ShapeDtypeStruct((ROWS, D), f32),
            jax.ShapeDtypeStruct((ROWS, D), f32),
        )
        + (jax.ShapeDtypeStruct((TOKENS, 128), bf16),) * 3
        + (jax.ShapeDtypeStruct((FF_ROWS // 3, 128), bf16),) * 3,
        grid_spec=pltpu.PrefetchScalarGridSpec(
            num_scalar_prefetch=1,
            in_specs=[anywhere] * 7 + [vmem] * 5,
            out_specs=(vmem,) * 3 + (anywhere,) * 6,
            scratch_shapes=[
                pltpu.VMEM((TOKENS, 384), bf16),
                pltpu.SemaphoreType.DMA((CHUNKS,)),
                pltpu.VMEM((D, D), bf16),
                pltpu.VMEM((D, FF), bf16),
                pltpu.VMEM((D, FF), bf16),
                pltpu.VMEM((D, FF), bf16),
                pltpu.SemaphoreType.DMA((4,)),
                pltpu.VMEM((2, COLS, 256), bf16),
                pltpu.VMEM((2, COLS, 256), bf16),
                pltpu.VMEM((2, 256, COLS), f32),
                pltpu.VMEM((2, COLS), f32),
                pltpu.VMEM((2, COLS), f32),
                pltpu.VMEM((ROWS, D), f32),
                pltpu.VMEM((2, COLS), f32),
                pltpu.VMEM((FF_ROWS, 128), bf16),
                pltpu.SemaphoreType.DMA((3,)),
                pltpu.VMEM((CHUNK, 384), f32),
                pltpu.VMEM((HALF, 128), bf16),
                pltpu.SemaphoreType.DMA((CHUNKS,)),
                pltpu.SemaphoreType.DMA,
                pltpu.VMEM((16, 128), f32),
                pltpu.VMEM((4, COLS), jnp.int32),
                pltpu.VMEM((N_CTX, META, 128), bf16),
                pltpu.SemaphoreType.DMA((2,)),
                pltpu.VMEM((8, 128), jnp.int32),
                pltpu.SMEM((8, 128), jnp.int32),
            ],
        ),
        compiler_params=pltpu.CompilerParams(vmem_limit_bytes=VMEM_LIMIT),
        name="layer",
    )(pair, *kvs, *weights, q, segments, x, cotangent, gain)


def reduce_kernel(*refs):
    dkv, dws = refs[0:3], refs[3:6]
    dq_ref, n_ref, x_ref, gh_ref, cos_ref, sin_ref, gain_ref, wq_ref, wk_ref, wv_ref = refs[6:16]
    gx_ref, outs, outs_one = refs[16], refs[17:20], refs[20:23]
    rest = refs[23:]
    done, done_ff, done_one, rest = rest[0:3], rest[3:6], rest[6:9], rest[9:]
    first, rest = rest[:SCATTER_REFS], rest[SCATTER_REFS:]
    second, rest = rest[:SCATTER_REFS], rest[SCATTER_REFS:]
    third, rest = rest[:SCATTER_REFS], rest[SCATTER_REFS:]
    parts, own, own_one, rest = rest[0:3], rest[3:6], rest[6:9], rest[9:]
    gain_rows, sems, sems_one = rest
    me, coords, core = whereabouts()
    greet(me, coords, core)

    def feed_forward():
        yield from scatter_steps([(dw,) for dw in dws], done_ff, second, True)
        for band in range(3):
            own[band][...] = done_ff[band][...].astype(bf16)
        yield from gather_steps(own, outs, Pool(sems))

    def small():
        yield from scatter_steps([(part,) for part in parts], done_one, third, False)
        for band in range(3):
            own_one[band][...] = done_one[band][...].astype(bf16)
        yield from gather_steps(own_one, outs_one, Pool(sems_one), False)

    def advance(steps, count):
        for _ in range(count):
            next(steps)

    scatter = scatter_steps([(d,) for d in dkv], done, first, True)
    other = feed_forward()
    advance(scatter, 1)
    advance(other, 1)
    advance(scatter, 12)
    advance(other, SIDE)
    run(scatter)

    cos_wide, sin_wide = cos_ref[...], -sin_ref[...]
    tiles = [turn(dq_ref[:, 128 * t : 128 * t + 128] * SCALE, cos_wide, sin_wide).astype(bf16) for t in range(4)]
    mixed = turn(
        jnp.concatenate([done[1][0:ROWS, 0:64], dq_ref[:, 512:576] * SCALE], 1), cos_wide, sin_wide
    ).astype(bf16)
    grad_q = jnp.concatenate(tiles + [mixed[:, 64:128]], 1)
    grad_k = jnp.concatenate(
        [turn(done[0][0:ROWS, :], cos_wide, sin_wide).astype(bf16), mixed[:, 0:64]], 1
    )
    grad_v = jnp.concatenate([done[2][0:ROWS, :], done[1][0:ROWS, 64:128]], 1).astype(bf16)
    normed = n_ref[...]
    features = x_ref[...].astype(f32).T
    grad_normed = nt_dot(grad_q, wq_ref[...]) + nn_dot(grad_k, wk_ref[...]) + nn_dot(grad_v, wv_ref[...])
    by_x, by_gain = rms_back(features, gain_ref[...].reshape(1, D), grad_normed)

    def put(at, rows16):
        block = at // 16
        band, device = divmod(block, N_CTX)
        index = (device // 32, device // 8 % 4, device // 2 % 4, device % 2)
        parts[band][index] = rows16

    def pack(at, grads):
        height, width = grads.shape
        grads = jnp.concatenate([grads, jnp.zeros((height, 128 - width % 128), f32)], 1).astype(bf16)
        for tile in range(grads.shape[1] // 128):
            for row in range(0, height, 16):
                put(at + tile * height + row, grads[row : row + 16, 128 * tile : 128 * tile + 128])

    pack(Q_AT, tn_dot(normed, grad_q))
    pack(KV_AT, tn_dot(jnp.concatenate([grad_k, grad_v], 1), normed))
    gain_rows[...] = jnp.zeros_like(gain_rows)
    for tile in range(4):
        gain_rows[tile : tile + 1, :] = by_gain[:, 128 * tile : 128 * tile + 128]
    gain_rows[4:5, 0:64] = by_gain[:, 512:576]
    put(GAIN_ONE_AT, gain_rows[...].astype(bf16))
    for at in range(GAIN_ONE_AT + 16, ATT_ROWS, 16):
        put(at, jnp.zeros((16, 128), bf16))

    chain = small()
    advance(chain, 1)
    gx_ref[...] = gh_ref[...] + by_x
    turns = [(chain, 1), (other, 2)]
    while turns:
        for steps, count in list(turns):
            try:
                advance(steps, count)
            except StopIteration:
                turns.remove((steps, count))


def reduce_all(dkvs, dws, dq, normed, x, grad_hidden, cos_wide, sin_wide, gain, wq, wk, wv):
    vmem = pl.BlockSpec(memory_space=pltpu.VMEM)
    anywhere = pl.BlockSpec(memory_space=pl.ANY)
    one = BAND_ROWS_ONE
    return pl.pallas_call(
        reduce_kernel,
        out_shape=(jax.ShapeDtypeStruct((ROWS, D), f32),)
        + (jax.ShapeDtypeStruct((SIDE, SIDE, SIDE, 2, BAND_ROWS, 128), bf16),) * 3
        + (jax.ShapeDtypeStruct((SIDE, SIDE, SIDE, 2, one, 128), bf16),) * 3,
        in_specs=[anywhere] * 6 + [vmem] * 10,
        out_specs=(vmem,) + (anywhere,) * 6,
        scratch_shapes=[pltpu.VMEM((ROWS, 128), f32)] * 3
        + [pltpu.VMEM((BAND_ROWS, 128), f32)] * 3
        + [pltpu.VMEM((one, 128), f32)] * 3
        + scatter_scratch(ROWS, True)
        + scatter_scratch(BAND_ROWS, True)
        + scatter_scratch(one, False)
        + [pltpu.VMEM((SIDE, SIDE, SIDE, 2, one, 128), bf16)] * 3
        + [pltpu.VMEM((BAND_ROWS, 128), bf16)] * 3
        + [pltpu.VMEM((one, 128), bf16)] * 3
        + [
            pltpu.VMEM((16, 128), f32),
            pltpu.SemaphoreType.DMA((GATHER_SEMS,)),
            pltpu.SemaphoreType.DMA((GATHER_SEMS_ONE,)),
        ],
        compiler_params=pltpu.CompilerParams(
            collective_id=2, has_side_effects=True, vmem_limit_bytes=VMEM_LIMIT
        ),
        name="reduce_all",
    )(*dkvs, *dws, dq, normed, x, grad_hidden, cos_wide, sin_wide, gain, wq, wk, wv)


FF_PARTS = ((GATE_AT, D, FF), (UP_AT, D, FF), (DOWN_AT, D, FF), (OUT_AT, D, D))


def unpack_kernel(
    sums0, sums1, sums2, ones0, ones1, ones2, gx_ref,
    xt_ref, ga_ref, gq_ref, gk_ref, gv_ref, gm_ref, gg_hbm, gu_hbm, gd_hbm, go_hbm,
    held, held_one, full0, full1, full2, full3, sem_in, sem_one, sem_out,
):
    sums = (sums0, sums1, sums2)
    fulls = (full0, full1, full2, full3)
    spots = (gg_hbm, gu_hbm, gd_hbm, go_hbm)
    band_blocks = N_CTX
    copies = []
    edges = [0]
    for at, rows, columns in FF_PARTS:
        edges.append((at + (columns + 127) // 128 * rows) // BAND_ROWS)
    edges[-1] = 3 * band_blocks
    for part in range(4):
        mine = []
        lo = edges[part]
        while lo < edges[part + 1]:
            band = lo // band_blocks
            hi = min(edges[part + 1], (band + 1) * band_blocks)
            mine.append(
                pltpu.make_async_copy(
                    sums[band].at[pl.ds(lo - band * band_blocks, hi - lo)],
                    held.at[pl.ds(lo, hi - lo)],
                    sem_in.at[part, len(mine)],
                )
            )
            mine[-1].start()
            lo = hi
        copies.append(mine)
    small = [
        pltpu.make_async_copy(ref, held_one.at[band], sem_one.at[band])
        for band, ref in enumerate((ones0, ones1, ones2))
    ]
    for copy in small:
        copy.start()
    xt_ref[...] = gx_ref[...].T
    outs = []
    for part, (at, rows, columns) in enumerate(FF_PARTS):
        for copy in copies[part]:
            copy.wait()
        for tile in range((columns + 127) // 128):
            width = min(128, columns - 128 * tile)
            for row in range(0, rows, BAND_ROWS):
                piece = held[(at + tile * rows + row) // BAND_ROWS].astype(f32)
                fulls[part][row : row + BAND_ROWS, 128 * tile : 128 * tile + width] = piece[:, 0:width]
        outs.append(pltpu.make_async_copy(fulls[part], spots[part], sem_out.at[part]))
        outs[-1].start()
    for copy in small:
        copy.wait()

    def fetch_one(at):
        band, block = divmod(at // BAND_ROWS_ONE, N_CTX)
        return held_one[band, block].astype(f32)

    for tile in range(5):
        width = min(128, D - 128 * tile)
        lanes = slice(128 * tile, 128 * tile + width)
        for row in range(0, D, 16):
            gq_ref[row : row + 16, lanes] = fetch_one(Q_AT + tile * D + row)[:, 0:width]
        for row in range(0, 192, 16):
            gk_ref[row : row + 16, lanes] = fetch_one(KV_AT + tile * 384 + row)[:, 0:width]
            gv_ref[row : row + 16, lanes] = fetch_one(KV_AT + tile * 384 + 192 + row)[:, 0:width]
        ga_ref[lanes] = fetch_one(GAIN_ONE_AT)[tile, 0:width]
        gm_ref[lanes] = held[GAIN_AT // BAND_ROWS].astype(f32)[tile, 0:width]
    for copy in outs:
        copy.wait()


def unpack(sums, ones, grad_x):
    vmem = pl.BlockSpec(memory_space=pltpu.VMEM)
    anywhere = pl.BlockSpec(memory_space=pl.ANY)
    shapes = ((D, ROWS), (D,), (D, D), (192, D), (192, D), (D,), (D, FF), (D, FF), (D, FF), (D, D))
    return pl.pallas_call(
        unpack_kernel,
        out_shape=tuple(jax.ShapeDtypeStruct(s, f32) for s in shapes),
        in_specs=[anywhere] * 6 + [vmem],
        out_specs=(vmem,) * 6 + (anywhere,) * 4,
        scratch_shapes=[
            pltpu.VMEM((3 * N_CTX, BAND_ROWS, 128), bf16),
            pltpu.VMEM((3, N_CTX, BAND_ROWS_ONE, 128), bf16),
            pltpu.VMEM((D, FF), f32),
            pltpu.VMEM((D, FF), f32),
            pltpu.VMEM((D, FF), f32),
            pltpu.VMEM((D, D), f32),
            pltpu.SemaphoreType.DMA((4, 2)),
            pltpu.SemaphoreType.DMA((3,)),
            pltpu.SemaphoreType.DMA((4,)),
        ],
        compiler_params=pltpu.CompilerParams(vmem_limit_bytes=VMEM_LIMIT),
        name="unpack",
    )(
        *[s.reshape(N_CTX, BAND_ROWS, 128) for s in sums],
        *[s.reshape(N_CTX, BAND_ROWS_ONE, 128) for s in ones],
        grad_x,
    )


def on_device(
    layer_input,
    attn_gain,
    w_query,
    w_key,
    w_value,
    w_out,
    mlp_gain,
    w_gate,
    w_up,
    w_down,
    cotangent,
    segment_ids,
    pair_table,
):
    own_pair = pair_table[0]
    within = jnp.arange(ROWS, dtype=jnp.int32)
    blocks = jnp.where(within < HALF, own_pair, 2 * N_CTX - 1 - own_pair)
    places = blocks * HALF + within % HALF
    lanes = jnp.arange(128, dtype=jnp.int32)
    frequency = ROPE_THETA ** (-2.0 * (lanes % (HEAD_DIM // 2)).astype(f32) / HEAD_DIM)
    turned = places.astype(f32)[:, None] * frequency[None, :]
    cos_wide = jnp.cos(turned)
    sin_wide = jnp.sin(turned) * jnp.where(lanes % HEAD_DIM < HEAD_DIM // 2, -1.0, 1.0)[None, :]

    segments = segment_ids[None, :]
    x_turned = layer_input.T
    wk_turned, wv_turned = w_key.T, w_value.T
    q_rot, normed, *kvs = project_and_gather(
        pair_table, x_turned, attn_gain, w_query, wk_turned, wv_turned, cos_wide, sin_wide, segments
    )
    result, grad_hidden, dq, *rest = layer(
        pair_table,
        [kv.reshape(N_CTX, kv.shape[4], 128) for kv in kvs],
        [w_out, w_gate, w_up, w_down.T],
        q_rot,
        segments,
        x_turned,
        cotangent.T,
        mlp_gain,
    )
    lead = (SIDE, SIDE, SIDE, 2)
    grad_x, *sums = reduce_all(
        [d.reshape(lead + (ROWS, 128)) for d in rest[0:3]],
        [d.reshape(lead + (BAND_ROWS, 128)) for d in rest[3:6]],
        dq,
        normed,
        x_turned,
        grad_hidden,
        cos_wide,
        sin_wide,
        attn_gain,
        w_query,
        wk_turned,
        wv_turned,
    )
    gx, ga, gq, gk, gv, gm, gg, gu, gd, go = unpack(sums[0:3], sums[3:6], grad_x)
    return (result.T, gx.T, ga, gq, gk.T, gv.T, go, gm, gg, gu, gd.T)


def solution(mesh):
    return jax.shard_map(
        on_device,
        mesh=mesh,
        in_specs=(
            P("ctx", None),
            P(),
            P(),
            P(),
            P(),
            P(),
            P(),
            P(),
            P(),
            P(),
            P("ctx", None),
            P("ctx"),
            P("ctx"),
        ),
        out_specs=(P("ctx", None), P("ctx", None), P(), P(), P(), P(), P(), P(), P(), P(), P()),
        check_vma=False,
    )
```

```python
import functools
import jax
import jax.numpy as jnp
from jax import lax
from jax.experimental import pallas as pl
from jax.experimental.pallas import tpu as pltpu
from jax.sharding import PartitionSpec as P

f32 = jnp.float32
bf16 = jnp.bfloat16
D = 576
HEADS = 9
KV_HEADS = 3
HEAD_DIM = 64
PER_GROUP = HEADS // KV_HEADS
FF = 1536
NORM_EPS = 1e-05
ROPE_THETA = 100000.0
ROWS = 128
HALF = 64
N_CTX = 128
TOKENS = ROWS * N_CTX
DOCS = 18
META = 16
CHUNK = 512
PIECES = CHUNK // HALF
CHUNKS = TOKENS // CHUNK
BLANK = 4096
COLS = HEADS * HALF
NEG = -1e30
SCALE = HEAD_DIM ** (-0.5)
VMEM_LIMIT = 56 * 1024 * 1024

K_AT = (0, 64, 128)
V_AT = (128, 192, 64)

GATE_AT = 0
UP_AT = GATE_AT + 12 * D
DOWN_AT = UP_AT + 12 * D
OUT_AT = DOWN_AT + 12 * D
GAIN_AT = OUT_AT + 5 * D
BAND_ROWS = 64
FF_ROWS = 3 * N_CTX * BAND_ROWS
Q_AT = 0
KV_AT = Q_AT + 5 * D
GAIN_ONE_AT = KV_AT + 5 * 384
BAND_ROWS_ONE = 16
FINAL_ROWS = BAND_ROWS + BAND_ROWS_ONE
ATT_ROWS = 3 * N_CTX * BAND_ROWS_ONE

MESH = pl.DeviceIdType.MESH
SIDE = 4
ORDERS = ((2, 1, 0), (1, 0, 2), (0, 2, 1))
STRIDES = (32, 8, 2)


def whereabouts():
    me = lax.axis_index("ctx")
    coords = (me // 32, lax.rem(me // 8, SIDE), lax.rem(me // 2, SIDE))
    return me, coords, lax.rem(me, 2)


def wrap(coord, step):
    return lax.rem(coord + (step + SIDE), SIDE)


def neighbour(me, coords, axis, step):
    return me + (wrap(coords[axis], step) - coords[axis]) * STRIDES[axis]


PARTNERS = 10


def greet(me, coords, core):
    others = [me + 1 - 2 * core]
    for axis in range(3):
        others += [neighbour(me, coords, axis, step) for step in (1, -1, 2)]
    for other in others:
        pl.semaphore_signal(
            pltpu.get_barrier_semaphore(), inc=1, device_id=(other,), device_id_type=MESH
        )


def meet():
    pl.semaphore_wait(pltpu.get_barrier_semaphore(), PARTNERS)


def half_rows(rows):
    return rows // 32 * 16


class Pool:
    def __init__(self, sems):
        self.sems = sems
        self.used = 0

    def new(self):
        self.used += 1
        return self.sems.at[self.used - 1]


def send(src, dst, device, send_sem, recv_sem):
    pltpu.make_async_remote_copy(
        src_ref=src,
        dst_ref=dst,
        send_sem=send_sem,
        recv_sem=recv_sem,
        device_id=(device,),
        device_id_type=MESH,
    ).start()


def wait_for(ref, sem):
    pltpu.make_async_copy(ref, ref, sem).wait()


def at_axes(order, values):
    index = [None] * 3
    for axis, value in zip(order, values):
        index[axis] = value
    return tuple(index)


WHOLE = pl.ds(0, SIDE)


def gather_steps(own, out, pool):
    me, coords, core = whereabouts()
    sibling = me + 1 - 2 * core
    bands = range(len(own))
    orders = [ORDERS[band % 3] for band in bands]
    lines = (0, 1, -1, 2)
    steps = (1, -1, 2)

    def place(band, *values):
        return out[band].at[at_axes(orders[band], values) + (core,)]

    def mine(band, phase, step=0):
        return wrap(coords[orders[band][phase]], step)

    def device(band, phase, step):
        return neighbour(me, coords, orders[band][phase], step)

    def blocks(*shape):
        return out[0].at[tuple(pl.ds(0, size) for size in shape)]

    home, came, gone = pool.new(), [pool.new() for phase in range(3)], [pool.new(), pool.new()]
    ringed = [pool.new() for band in bands]
    across = [(pool.new(), pool.new()) for band in bands]
    ends = {line: (pool.new(), pool.new(), pool.new()) for line in lines}
    for step in steps:
        for phase in (1, 0):
            for band in bands:
                part = place(band, *(mine(band, p) for p in range(3)))
                send(own[band], part, device(band, phase, step), gone[0], came[phase])
    for band in bands:
        part = place(band, *(mine(band, p) for p in range(3)))
        pltpu.make_async_copy(own[band], part, home).start()

    def send_line(band, line):
        part = place(band, mine(band, 0, line), WHOLE, mine(band, 2))
        send(part, part, device(band, 2, 1), ringed[band], ends[line][0])
        send(part, part, device(band, 2, -1), ringed[band], ends[line][1])

    yield
    wait_for(blocks(1, 1, 3, 1), home)
    wait_for(blocks(1, 3, 3, 1), came[1])
    for band in bands:
        send_line(band, 0)
    wait_for(blocks(1, 3, 3, 1), came[0])
    for band in bands:
        for line in lines[1:]:
            part = place(band, mine(band, 0, line), mine(band, 1), mine(band, 2))
            for step in steps:
                send(part, part, device(band, 1, step), gone[1], came[2])
    yield
    wait_for(blocks(3, 3, 3, 1), came[2])
    for line in lines[1:]:
        for band in bands:
            send_line(band, line)
    for band in bands:
        part = place(band, WHOLE, WHOLE, mine(band, 2))
        send(part, part, sibling, *across[band])
    for line in lines:
        yield
        for side, step in ((0, -1), (1, 1)):
            wait_for(blocks(1, 3, 4, 1), ends[line][side])
            for band in bands:
                rows = own[band].shape[0]
                cut = half_rows(rows)
                part = place(band, mine(band, 0, line), WHOLE, mine(band, 2, step))
                half = part.at[:, pl.ds(0, cut) if side == 0 else pl.ds(cut, rows - cut)]
                send(half, half, device(band, 2, -step), ringed[band], ends[line][2])
                send(part, part, sibling, *across[band])
    for line in lines:
        yield
        wait_for(blocks(1, 3, 4, 1), ends[line][2])
        for band in bands:
            part = place(band, mine(band, 0, line), WHOLE, mine(band, 2, 2))
            send(part, part, sibling, *across[band])
    yield
    for band in bands:
        wait_for(out[band].at[:, :, :, 0], across[band][1])
        wait_for(out[band].at[:, :, :, 0], across[band][0])
        wait_for(out[band].at[0:3, :, :, 0], ringed[band])
    wait_for(blocks(3, 3, 1, 2), gone[0])
    wait_for(blocks(3, 3, 3, 1), gone[1])


GATHER_SEMS = 1 + 3 + 2 + 3 + 6 + 12


def gather_small_steps(own, out, pool):
    me, coords, core = whereabouts()
    sibling = me + 1 - 2 * core
    bands = range(len(own))
    homes = [pool.new() for band in bands]
    for band in bands:
        pltpu.make_async_copy(own[band], out[band].at[coords + (core,)], homes[band]).start()
    sent = []
    for phase in range(3):
        came = [pool.new() for band in bands]
        gone = [pool.new() for band in bands]
        for band in bands:
            order = ORDERS[band % 3]
            mine = [coords[axis] for axis in order]
            part = out[band].at[at_axes(order, [WHOLE] * phase + mine[phase:]) + (core,)]
            for step in (1, -1, 2):
                send(
                    own[band] if phase == 0 else part,
                    part,
                    neighbour(me, coords, order[phase], step),
                    gone[band],
                    came[band],
                )
        yield
        for band in bands:
            if phase == 0:
                wait_for(own[band], homes[band])
            three = (0, 0, pl.ds(0, 3), 0), (0, pl.ds(0, 3), WHOLE, 0), (pl.ds(0, 3), WHOLE, WHOLE, 0)
            wait_for(out[band].at[three[phase]], came[band])
            sent.append((out[band].at[three[phase]], gone[band]))
    across = [(pool.new(), pool.new()) for band in bands]
    for band in bands:
        part = out[band].at[:, :, :, core]
        send(part, part, sibling, *across[band])
    yield
    for band in bands:
        wait_for(out[band].at[:, :, :, 0], across[band][1])
        wait_for(out[band].at[:, :, :, 0], across[band][0])
    for ref, sem in sent:
        wait_for(ref, sem)


GATHER_SMALL_SEMS = 1 + 3 * 2 + 2


def run(steps):
    for _ in steps:
        pass


def scatter_scratch(rows, ring):
    shapes = [pltpu.VMEM((SIDE, SIDE, SIDE, rows, 128), bf16)] * 6
    for _ in range(3):
        shapes += [
            pltpu.VMEM((3, SIDE, SIDE, rows, 128), bf16),
            pltpu.VMEM((3, SIDE, rows, 128), bf16),
            pltpu.VMEM((3, rows, 128), bf16),
        ]
    return shapes + [pltpu.SemaphoreType.DMA((6 + 2 + 4 + 16 + 8 + 2 if ring else 6 + 2 + 6 + 3 + 2,))]


SCATTER_REFS = 16


def scatter_steps(parts, done, scratch, ring):
    acc, sib = scratch[0:3], scratch[3:6]
    landing = [scratch[6 + 3 * b : 9 + 3 * b] for b in range(3)]
    pool = Pool(scratch[15])
    me, coords, core = whereabouts()
    sibling = me + 1 - 2 * core
    bands = range(3)
    steps = (2, 1, -1, 0)
    rows = acc[0].shape[3]
    cut = half_rows(rows)
    def blocks(*shape):
        return acc[0].at[tuple(pl.ds(0, size) for size in shape)]

    sent = [[pool.new(), None, None, pool.new()] for band in bands]
    for phase in (1, 2):
        shared = pool.new()
        for band in bands:
            sent[band][phase] = shared
    homes, swaps = {}, {}
    if ring:
        for step in steps:
            for band in bands:
                order = ORDERS[band]
                plane = at_axes(order, (wrap(coords[order[0]], step), WHOLE, WHOLE))
                if band == 0:
                    homes[step] = pool.new()
                top = 0
                for part in parts[band]:
                    size = part.shape[4]
                    pltpu.make_async_copy(
                        part.at[plane + (core,)],
                        acc[band].at[plane + (pl.ds(top, size),)],
                        homes[step],
                    ).start()
                    top += size
            for sub in range(SIDE):
                for band in bands:
                    order = ORDERS[band]
                    line = at_axes(order, (wrap(coords[order[0]], step), sub, WHOLE))
                    if band == 0:
                        swaps[step, sub] = pool.new()
                    top = 0
                    for part in parts[band]:
                        size = part.shape[4]
                        send(
                            part.at[line + (1 - core,)],
                            sib[band].at[line + (pl.ds(top, size),)],
                            sibling,
                            sent[band][3],
                            swaps[step, sub],
                        )
                        top += size
    else:
        for band in bands:
            homes[band], swaps[band] = pool.new(), pool.new()
            (part,) = parts[band]
            pltpu.make_async_copy(part.at[:, :, :, core], acc[band], homes[band]).start()
            send(part.at[:, :, :, 1 - core], sib[band], sibling, sent[band][3], swaps[band])

    def add_swap(band, step, sub):
        order = ORDERS[band]
        first = wrap(coords[order[0]], step)
        if band == 0:
            if sub == 0:
                wait_for(blocks(3, 4, 4), homes[step])
            wait_for(blocks(1, 3, 4), swaps[step, sub])

        line = at_axes(order, (first, sub, WHOLE))
        acc[band][line] = acc[band][line] + sib[band][line]

    jobs = [(sub, band) for sub in range(SIDE) for band in bands]

    def line_at(band, step, sub):
        order = ORDERS[band]
        return at_axes(order, (wrap(coords[order[0]], step), sub, WHOLE))

    def sum_up(band, region, landed):
        total = acc[band][region].astype(f32)
        for ref in landed:
            total = total + ref[...].astype(f32)
        acc[band][region] = total.astype(bf16)

    if ring:
        passing, ending = {}, {}
        for sub in range(SIDE):
            yield
            passing[sub], ending[sub] = pool.new(), pool.new()
            for band in bands:
                axis = ORDERS[band][0]
                add_swap(band, 2, sub)
                far = acc[band].at[line_at(band, 2, sub)]
                for lo, size, step in ((0, cut, 1), (cut, rows - cut, -1)):
                    send(
                        far.at[:, pl.ds(lo, size)],
                        landing[band][0].at[0, sub, :, pl.ds(lo, size)],
                        neighbour(me, coords, axis, step),
                        sent[band][0],
                        passing[sub],
                    )
        for sub in range(SIDE):
            yield
            for step in (1, -1):
                for band in bands:
                    add_swap(band, step, sub)
            wait_for(blocks(1, 3, 4), passing[sub])
            for band in bands:
                order = ORDERS[band]
                for slot, lo, size, step in ((1, 0, cut, 1), (2, cut, rows - cut, -1)):
                    half = line_at(band, step, sub) + (pl.ds(lo, size),)
                    acc[band][half] = acc[band][half] + landing[band][0][0, sub, :, lo : lo + size]
                    send(
                        acc[band].at[line_at(band, step, sub)],
                        landing[band][0].at[slot, sub],
                        neighbour(me, coords, order[0], step),
                        sent[band][0],
                        ending[sub],
                    )
        for sub in range(SIDE):
            yield
            for band in bands:
                add_swap(band, 0, sub)
            wait_for(blocks(2, 3, 4), ending[sub])
            for band in bands:
                order = ORDERS[band]
                sum_up(
                    band, line_at(band, 0, sub), [landing[band][0].at[slot, sub] for slot in (1, 2)]
                )
    else:
        came = [pool.new() for band in bands]
        yield
        for band in bands:
            axis = ORDERS[band][0]
            wait_for(acc[band], homes[band])
            wait_for(sib[band], swaps[band])
            acc[band][...] = acc[band][...] + sib[band][...]
            for slot, step in enumerate((2, 1, -1)):
                plane = at_axes(ORDERS[band], (wrap(coords[axis], step), WHOLE, WHOLE))
                send(
                    acc[band].at[plane],
                    landing[band][0].at[slot],
                    neighbour(me, coords, axis, step),
                    sent[band][0],
                    came[band],
                )
        yield
        for band in bands:
            plane = at_axes(ORDERS[band], (coords[ORDERS[band][0]], WHOLE, WHOLE))
            wait_for(landing[band][0], came[band])
            total = acc[band][plane].astype(f32)
            for slot in range(3):
                total = total + landing[band][0][slot].astype(f32)
            acc[band][plane] = total.astype(bf16)
    came = pool.new()
    for slot, step in enumerate((2, 1, -1)):
        for band in bands:
            order = ORDERS[band]
            line = at_axes(order, (coords[order[0]], wrap(coords[order[1]], step), WHOLE))
            send(
                acc[band].at[line],
                landing[band][1].at[slot],
                neighbour(me, coords, order[1], step),
                sent[band][1],
                came,
            )
    yield
    ends = pool.new()
    wait_for(blocks(3, 3, 4), came)
    for band in bands:
        order = ORDERS[band]
        line = at_axes(order, (coords[order[0]], coords[order[1]], WHOLE))
        sum_up(band, line, [landing[band][1].at[slot] for slot in range(3)])
        for slot, step in enumerate((2, 1, -1)):
            at = at_axes(order, (coords[order[0]], coords[order[1]], wrap(coords[order[2]], step)))
            send(
                acc[band].at[at],
                landing[band][2].at[slot],
                neighbour(me, coords, order[2], step),
                sent[band][2],
                ends,
            )
    yield
    wait_for(blocks(1, 3, 3), ends)
    for band in bands:
        total = acc[band][coords].astype(f32)
        for slot in range(3):
            total = total + landing[band][2][slot].astype(f32)
        done[band][...] = total
    for band in bands:
        wait_for(acc[band].at[0:3], sent[band][0])
        wait_for(acc[band], sent[band][3])
    wait_for(blocks(3, 3, 4), sent[0][1])
    wait_for(blocks(1, 3, 3), sent[0][2])


def rms_parts(features):
    return lax.rsqrt(jnp.mean(features * features, axis=-1, keepdims=True) + NORM_EPS)


def rms_back(features, gain, grad):
    inverse = rms_parts(features)
    scaled = grad * gain
    inner = jnp.mean(scaled * features, axis=-1, keepdims=True)
    by_features = inverse * scaled - features * (inverse * inverse * inverse * inner)
    by_gain = jnp.sum(grad * features * inverse, axis=0, keepdims=True)
    return by_features, by_gain


def nt_dot(left, right):
    return lax.dot_general(left, right, (((1,), (1,)), ((), ())), preferred_element_type=f32)


def tn_dot(left, right):
    return lax.dot_general(left, right, (((0,), (0,)), ((), ())), preferred_element_type=f32)


def nn_dot(left, right):
    return jnp.dot(left, right, preferred_element_type=f32)


def turn(tile, cos_wide, sin_wide):
    lanes = lax.broadcasted_iota(jnp.int32, tile.shape, 1)
    swapped = jnp.where(
        lax.rem(lanes, HEAD_DIM) < HEAD_DIM // 2, pltpu.roll(tile, 96, 1), pltpu.roll(tile, 32, 1)
    )
    return tile * cos_wide + swapped * sin_wide


def project_kernel(
    pair_ref, x_ref, gain_ref, wq_ref, wk_ref, wv_ref, cos_ref, sin_ref, seg_ref,
    q_ref, n_ref, table_ref, out0, out1, out2,
    own0, own1, own2, own_meta, metas, sems, meta_sems,
):
    me, coords, core = whereabouts()
    greet(me, coords, core)
    segments = jnp.broadcast_to(seg_ref[...].astype(f32), (ROWS, ROWS)).T
    lanes = lax.broadcasted_iota(jnp.int32, (ROWS, ROWS), 1)
    earlier = jnp.sum(jnp.where(segments < (lanes - 1).astype(f32), 1.0, 0.0), axis=0, keepdims=True)
    meta = jnp.where(lanes[0:1] == 0, pair_ref[0].astype(f32), earlier)
    own_meta[...] = jnp.broadcast_to(meta, (META, 128)).astype(bf16)
    features = x_ref[...].astype(f32).T
    normed = (features * rms_parts(features) * gain_ref[...].reshape(1, D)).astype(bf16)
    n_ref[...] = normed
    cos_wide, sin_wide = cos_ref[...], sin_ref[...]
    keys = nt_dot(normed, wk_ref[...])
    values = nt_dot(normed, wv_ref[...]).astype(bf16)
    queries = nn_dot(normed, wq_ref[...])
    own0[...] = turn(keys[:, 0:128], cos_wide, sin_wide).astype(bf16)
    mixed = turn(jnp.concatenate([keys[:, 128:192], queries[:, 512:576]], 1), cos_wide, sin_wide)
    own1[...] = jnp.concatenate([mixed[:, 0:64].astype(bf16), values[:, 128:192]], 1)
    own2[...] = values[:, 0:128]
    meet()
    steps = gather_steps((own0, own1, own2), (out0, out1, out2), Pool(sems))
    small = gather_small_steps((own_meta,), (metas,), Pool(meta_sems))
    next(small)
    next(steps)
    next(small)
    for tile in range(4):
        at = slice(128 * tile, 128 * tile + 128)
        q_ref[:, at] = (turn(queries[:, at], cos_wide, sin_wide).astype(bf16).astype(f32) * SCALE).astype(bf16)
    q_ref[:, 512:576] = (mixed[:, 64:128].astype(bf16).astype(f32) * SCALE).astype(bf16)
    next(steps)
    next(small)
    for _ in range(3):
        next(steps)
    next(small)
    for _ in range(3):
        next(steps)
    run(small)
    columns = metas[:, :, :, :, 0, :].astype(f32).reshape(N_CTX, 128)
    starts = jnp.sum(columns, axis=0, keepdims=True)
    numbers = lax.broadcasted_iota(jnp.int32, (N_CTX, N_CTX), 0).astype(f32)
    holders = jnp.sum(
        jnp.where(columns[:, 0:1] == lanes.astype(f32), numbers, 0.0), axis=0, keepdims=True
    )
    segment_row = seg_ref[...].astype(f32)
    row_starts = jnp.zeros((1, ROWS), f32)
    for document in range(DOCS):
        row_starts = jnp.where(
            segment_row == float(document), starts[:, document + 1 : document + 2], row_starts
        )
    table_ref[...] = jnp.concatenate(
        [holders, row_starts, jnp.zeros((6, 128), f32)], 0
    ).astype(jnp.int32)
    run(steps)


def project_and_gather(pair, x, gain, wq, wk, wv, cos_wide, sin_wide, segments):
    vmem = pl.BlockSpec(memory_space=pltpu.VMEM)
    anywhere = pl.BlockSpec(memory_space=pl.ANY)
    return pl.pallas_call(
        project_kernel,
        out_shape=(
            jax.ShapeDtypeStruct((ROWS, D), bf16),
            jax.ShapeDtypeStruct((ROWS, D), bf16),
            jax.ShapeDtypeStruct((8, 128), jnp.int32),
        )
        + (jax.ShapeDtypeStruct((SIDE, SIDE, SIDE, 2, ROWS, 128), bf16),) * 3,
        in_specs=[pl.BlockSpec(memory_space=pltpu.SMEM)] + [vmem] * 8,
        out_specs=(vmem, vmem, vmem, anywhere, anywhere, anywhere),
        scratch_shapes=[pltpu.VMEM((ROWS, 128), bf16)] * 3
        + [
            pltpu.VMEM((META, 128), bf16),
            pltpu.VMEM((SIDE, SIDE, SIDE, 2, META, 128), bf16),
            pltpu.SemaphoreType.DMA((GATHER_SEMS,)),
            pltpu.SemaphoreType.DMA((GATHER_SMALL_SEMS,)),
        ],
        compiler_params=pltpu.CompilerParams(
            collective_id=1, has_side_effects=True, vmem_limit_bytes=VMEM_LIMIT
        ),
        name="project_and_gather",
    )(pair, x, gain, wq, wk, wv, cos_wide, sin_wide, segments)


def needed(chunk, a_hi, b_lo, b_hi):
    return (chunk <= a_hi) | ((chunk >= b_lo) & (chunk <= b_hi))


def chunk_rows(chunk, count=1):
    return pl.ds(pl.multiple_of(chunk * CHUNK, CHUNK), count * CHUNK)


def wait_chunk(chunk, held, sem):
    window = held.at[chunk_rows(chunk)]
    pltpu.make_async_copy(window, window, sem.at[chunk]).wait()


def chunk_mask(chunk, place_row, start_row):
    keys = chunk * CHUNK + lax.broadcasted_iota(jnp.int32, (CHUNK, COLS), 0)
    return (keys <= place_row) & (keys >= start_row)


def layer_kernel(
    pair_ref, table,
    kv0, kv1, kv2, wo_hbm, wg_hbm, wu_hbm, wd_hbm,
    q_ref, starts_ref, x_ref, c_ref, gain_ref,
    result_ref, gh_ref, dq_ref, dkv0, dkv1, dkv2, dw0, dw1, dw2,
    held, sem, wo_ref, wg_ref, wu_ref, wd_ref, w_sem, q_spread, g_spread, mixed, top, total, att_ref,
    delta_ref, dw, dw_sem, staged, blank, out_sem, blank_sem, gain_rows,
    rows_ref,
):
    kvs, dkvs, dws = (kv0, kv1, kv2), (dkv0, dkv1, dkv2), (dw0, dw1, dw2)
    weights = [
        pltpu.make_async_copy(src, dst, w_sem.at[i])
        for i, (src, dst) in enumerate(
            ((wo_hbm, wo_ref), (wg_hbm, wg_ref), (wu_hbm, wu_ref), (wd_hbm, wd_ref))
        )
    ]
    for copy in weights:
        copy.start()
    pair = pair_ref[0]
    row_starts = starts_ref[1:2, :]
    for block in range(2):
        first = pair if block == 0 else 2 * N_CTX - 1 - pair
        places = first * HALF + lax.rem(lax.broadcasted_iota(jnp.int32, (1, COLS), 1), HALF)
        rows_ref[2 * block : 2 * block + 1, :] = places
        mine = row_starts[:, block * HALF : (block + 1) * HALF]
        rows_ref[2 * block + 1 : 2 * block + 2, :] = jnp.concatenate([mine] * HEADS, 1)
    a_hi, b_lo, b_hi = pair // PIECES, table[1, HALF] // CHUNK, (2 * N_CTX - 1 - pair) // PIECES

    def slot_of(block_number):
        low = table[0, jnp.minimum(block_number, 2 * N_CTX - 1 - block_number)]
        return low * ROWS + jnp.where(block_number < N_CTX, 0, HALF)


    def issue(chunk, carry):
        @pl.when(needed(chunk, a_hi, b_lo, b_hi))
        def _():
            for piece in range(PIECES):
                slot = slot_of(chunk * PIECES + piece)
                rows = pl.ds(pl.multiple_of(chunk * CHUNK + piece * HALF, HALF), HALF)
                device, top = slot // ROWS, pl.multiple_of(lax.rem(slot, ROWS), HALF)
                for band in range(3):
                    pltpu.make_async_copy(
                        kvs[band].at[device, pl.ds(top, HALF)],
                        held.at[rows, 128 * band : 128 * band + 128],
                        sem.at[chunk],
                    ).start()

        return carry

    lax.fori_loop(0, CHUNKS, issue, 0)

    def spread(rows, place, windows):
        for block in range(2):
            for head in range(HEADS):
                tile = rows[block * HALF : (block + 1) * HALF, head * HEAD_DIM : (head + 1) * HEAD_DIM]
                at = windows[head // PER_GROUP]
                place[block, head * HALF : (head + 1) * HALF, at : at + HEAD_DIM] = tile

    def unspread(columns, place, block, windows):
        for head in range(HEADS):
            at = windows[head // PER_GROUP]
            tile = columns[at : at + HEAD_DIM, head * HALF : (head + 1) * HALF]
            place[block * HALF : (block + 1) * HALF, head * HEAD_DIM : (head + 1) * HEAD_DIM] = tile.T

    blank[...] = jnp.zeros_like(blank)

    clears = [
        pltpu.make_async_copy(blank, dkvs[band].at[pl.ds(row, BLANK)], blank_sem.at[band, row // BLANK])
        for band in range(3)
        for row in range(0, TOKENS, BLANK)
    ]
    for copy in clears:
        copy.start()
    q_spread[...] = jnp.zeros_like(q_spread)
    g_spread[...] = jnp.zeros_like(g_spread)
    spread(q_ref[...], q_spread, K_AT)
    mixed[...] = jnp.zeros_like(mixed)
    top[...] = jnp.full_like(top, NEG)
    total[...] = jnp.zeros_like(total)

    def mask_of(block, chunk):
        return chunk_mask(
            chunk, rows_ref[2 * block : 2 * block + 1, :], rows_ref[2 * block + 1 : 2 * block + 2, :]
        )

    def forward(block, chunk, masked, count=1):
        window = chunk_rows(chunk, count)
        scores = nt_dot(held[window, 0:256], q_spread[block])
        if masked:
            scores = jnp.where(mask_of(block, chunk), scores, NEG)
        old = top[block : block + 1, :]
        new = jnp.maximum(old, jnp.max(scores, axis=0, keepdims=True))
        probs = jnp.exp(scores - new)
        shrink = jnp.exp(old - new)
        top[block : block + 1, :] = new
        total[block : block + 1, :] = total[block : block + 1, :] * shrink + jnp.sum(
            probs, axis=0, keepdims=True
        )
        values = held[window, 128:384].T[64:256]
        mixed[block, 64:256] = mixed[block, 64:256] * shrink + nn_dot(values, probs.astype(bf16))

    def forward_step(chunk, carry):
        in_b = (chunk >= b_lo) & (chunk <= b_hi)

        @pl.when(needed(chunk, a_hi, b_lo, b_hi))
        def _():
            wait_chunk(chunk, held, sem)

        @pl.when(chunk <= a_hi)
        def _():
            forward(0, chunk, True)

        @pl.when(in_b)
        def _():
            forward(1, chunk, True)

        return carry

    def forward_pair(pair_of, carry):
        wait_chunk(2 * pair_of, held, sem)
        wait_chunk(2 * pair_of + 1, held, sem)
        forward(0, 2 * pair_of, False, 2)
        return carry

    plain = jnp.minimum(a_hi, b_lo) // 2
    lax.fori_loop(0, plain, forward_pair, 0)
    lax.fori_loop(2 * plain, b_hi + 1, forward_step, 0)
    for block in range(2):
        sums = total[block : block + 1, :]
        top[block : block + 1, :] = top[block : block + 1, :] + jnp.log(sums)
        mixed[block] = mixed[block] / sums
        unspread(mixed.at[block], att_ref, block, V_AT)

    attended = att_ref[...].astype(bf16)
    cotangent = c_ref[...].astype(f32).T.astype(bf16)
    gain = gain_ref[...].reshape(1, D)
    for copy in weights:
        copy.wait()
    hidden = x_ref[...].astype(f32).T + nn_dot(attended, wo_ref[...])
    normed = (hidden * rms_parts(hidden) * gain).astype(bf16)
    gate = nn_dot(normed, wg_ref[...])
    upward = nn_dot(normed, wu_ref[...])
    open_gate = jax.nn.sigmoid(gate)
    silu = gate * open_gate
    active = (silu * upward).astype(bf16)
    result_ref[...] = (hidden + nt_dot(active, wd_ref[...])).T.astype(bf16)
    grad_active = nn_dot(cotangent, wd_ref[...])
    grad_gate = (grad_active * upward * open_gate * (1.0 + gate * (1.0 - open_gate))).astype(bf16)
    grad_up = (grad_active * silu).astype(bf16)
    grad_normed = nt_dot(grad_gate, wg_ref[...]) + nt_dot(grad_up, wu_ref[...])
    by_hidden, by_gain = rms_back(hidden, gain, grad_normed)
    grad_hidden = cotangent.astype(f32) + by_hidden
    gh_ref[...] = grad_hidden
    grad_out = grad_hidden.astype(bf16)
    spread(nt_dot(grad_out, wo_ref[...]).astype(bf16), g_spread, V_AT)
    for block in range(2):
        turned = g_spread[block].astype(f32).T
        delta_ref[block : block + 1, :] = jnp.sum(turned * mixed[block], axis=0, keepdims=True)

    def pack(at, grads):
        rows = grads.shape[0]
        for tile in range(grads.shape[1] // 128):
            dw[at + tile * rows : at + (tile + 1) * rows, :] = grads[:, 128 * tile : 128 * tile + 128].astype(bf16)
        if grads.shape[1] % 128:
            tile = grads.shape[1] // 128
            dw[at + tile * rows : at + (tile + 1) * rows, 0:64] = grads[:, 128 * tile : 128 * tile + 64].astype(bf16)
            dw[at + tile * rows : at + (tile + 1) * rows, 64:128] = jnp.zeros((rows, 64), bf16)

    pack(GATE_AT, tn_dot(normed, grad_gate))
    pack(UP_AT, tn_dot(normed, grad_up))
    pack(DOWN_AT, tn_dot(cotangent, active))
    pack(OUT_AT, tn_dot(attended, grad_out))
    gain_rows[...] = jnp.zeros_like(gain_rows)
    for tile in range(4):
        gain_rows[tile : tile + 1, :] = by_gain[:, 128 * tile : 128 * tile + 128]
    gain_rows[4:5, 0:64] = by_gain[:, 512:576]
    dw[GAIN_AT : GAIN_AT + 16, :] = gain_rows[...].astype(bf16)
    dw[GAIN_AT + 16 : FF_ROWS, :] = jnp.zeros((FF_ROWS - GAIN_AT - 16, 128), bf16)
    band_rows = FF_ROWS // 3
    dw_copies = [
        pltpu.make_async_copy(dw.at[pl.ds(band * band_rows, band_rows)], dws[band], dw_sem.at[band])
        for band in range(3)
    ]
    for copy in dw_copies:
        copy.start()

    for copy in clears:
        copy.wait()
    mixed[...] = jnp.zeros_like(mixed)

    def backward(block, chunk, masked, mode, count=1):
        window = chunk_rows(chunk, count)
        keys = held[window, 0:256]
        values = held[window, 128:384]
        scores = nt_dot(keys, q_spread[block])
        probs = jnp.exp(scores - top[block : block + 1, :])
        if masked:
            probs = jnp.where(mask_of(block, chunk), probs, 0.0)
        grad_probs = nt_dot(values, g_spread[block])
        grad_scores = (probs * (grad_probs - delta_ref[block : block + 1, :])).astype(bf16)
        mixed[block, 0:192] += nn_dot(keys.T[0:192], grad_scores)
        dk = nn_dot(grad_scores, q_spread[block])
        dv = nn_dot(probs.astype(bf16), g_spread[block])
        parts = (dk[:, 0:128], dk[:, 128:256] + dv[:, 0:128], dv[:, 128:256])
        for band in range(3):
            at = slice(128 * band, 128 * band + 128)
            if mode == "first":
                staged[:, at] = parts[band]
            elif mode == "second":
                held[window, at] = (staged[:, at] + parts[band]).astype(bf16)
            else:
                held[window, at] = parts[band].astype(bf16)

    def put_back(chunk):
        for piece in range(PIECES):
            row = pl.multiple_of(slot_of(chunk * PIECES + piece), HALF)
            rows = pl.ds(pl.multiple_of(chunk * CHUNK + piece * HALF, HALF), HALF)
            for band in range(3):
                pltpu.make_async_copy(
                    held.at[rows, 128 * band : 128 * band + 128],
                    dkvs[band].at[pl.ds(row, HALF)],
                    out_sem.at[chunk],
                ).start()

    def backward_step(chunk, carry):
        in_a = chunk <= a_hi
        in_b = (chunk >= b_lo) & (chunk <= b_hi)

        @pl.when(in_a & jnp.logical_not(in_b))
        def _():
            backward(0, chunk, True, "only")

        @pl.when(in_b & jnp.logical_not(in_a))
        def _():
            backward(1, chunk, True, "only")

        @pl.when(in_a & in_b)
        def _():
            backward(0, chunk, True, "first")
            backward(1, chunk, True, "second")

        @pl.when(in_a | in_b)
        def _():
            put_back(chunk)

        return carry

    def backward_pair(pair_of, carry):
        backward(0, 2 * pair_of, False, "only", 2)
        put_back(2 * pair_of)
        put_back(2 * pair_of + 1)
        return carry

    lax.fori_loop(0, plain, backward_pair, 0)
    lax.fori_loop(2 * plain, b_hi + 1, backward_step, 0)
    for block in range(2):
        unspread(mixed.at[block], dq_ref, block, K_AT)

    def drain(chunk, carry):
        use = needed(chunk, a_hi, b_lo, b_hi)

        @pl.when(use)
        def _():
            wait_chunk(chunk, held, out_sem)

        return carry

    lax.fori_loop(0, CHUNKS, drain, 0)
    for copy in dw_copies:
        copy.wait()


def layer(pair, table, kvs, weights, q, x, cotangent, gain):
    vmem = pl.BlockSpec(memory_space=pltpu.VMEM)
    anywhere = pl.BlockSpec(memory_space=pl.ANY)
    return pl.pallas_call(
        layer_kernel,
        out_shape=(
            jax.ShapeDtypeStruct((D, ROWS), bf16),
            jax.ShapeDtypeStruct((ROWS, D), f32),
            jax.ShapeDtypeStruct((ROWS, D), f32),
        )
        + (jax.ShapeDtypeStruct((TOKENS, 128), bf16),) * 3
        + (jax.ShapeDtypeStruct((FF_ROWS // 3, 128), bf16),) * 3,
        grid_spec=pltpu.PrefetchScalarGridSpec(
            num_scalar_prefetch=2,
            in_specs=[anywhere] * 7 + [vmem] * 5,
            out_specs=(vmem,) * 3 + (anywhere,) * 6,
            scratch_shapes=[
                pltpu.VMEM((TOKENS, 384), bf16),
                pltpu.SemaphoreType.DMA((CHUNKS,)),
                pltpu.VMEM((D, D), bf16),
                pltpu.VMEM((D, FF), bf16),
                pltpu.VMEM((D, FF), bf16),
                pltpu.VMEM((D, FF), bf16),
                pltpu.SemaphoreType.DMA((4,)),
                pltpu.VMEM((2, COLS, 256), bf16),
                pltpu.VMEM((2, COLS, 256), bf16),
                pltpu.VMEM((2, 256, COLS), f32),
                pltpu.VMEM((2, COLS), f32),
                pltpu.VMEM((2, COLS), f32),
                pltpu.VMEM((ROWS, D), f32),
                pltpu.VMEM((2, COLS), f32),
                pltpu.VMEM((FF_ROWS, 128), bf16),
                pltpu.SemaphoreType.DMA((3,)),
                pltpu.VMEM((CHUNK, 384), f32),
                pltpu.VMEM((BLANK, 128), bf16),
                pltpu.SemaphoreType.DMA((CHUNKS,)),
                pltpu.SemaphoreType.DMA((3, TOKENS // BLANK)),
                pltpu.VMEM((16, 128), f32),
                pltpu.VMEM((4, COLS), jnp.int32),
            ],
        ),
        compiler_params=pltpu.CompilerParams(vmem_limit_bytes=VMEM_LIMIT),
        name="layer",
    )(pair, table, *kvs, *weights, q, table, x, cotangent, gain)


def reduce_kernel(*refs):
    dkv, dws = refs[0:3], refs[3:6]
    dq_ref, n_ref, x_ref, gh_ref, cos_ref, sin_ref, gain_ref, wq_ref, wk_ref, wv_ref = refs[6:16]
    gx_ref, outs = refs[16], refs[17:20]
    rest = refs[20:]
    done, done_ff, done_one, rest = rest[0:3], rest[3:6], rest[6:9], rest[9:]
    first, rest = rest[:SCATTER_REFS], rest[SCATTER_REFS:]
    second, rest = rest[:SCATTER_REFS], rest[SCATTER_REFS:]
    third, rest = rest[:SCATTER_REFS], rest[SCATTER_REFS:]
    parts, own, rest = rest[0:3], rest[3:6], rest[6:]
    gain_rows, sems = rest
    me, coords, core = whereabouts()
    greet(me, coords, core)
    meet()

    def advance(steps, count):
        for _ in range(count):
            next(steps)

    scatter = scatter_steps([(d,) for d in dkv], done, first, True)
    other = scatter_steps([(dw,) for dw in dws], done_ff, second, True)
    advance(scatter, 1)
    advance(other, 1)
    advance(scatter, 12)

    cos_wide, sin_wide = cos_ref[...], -sin_ref[...]
    normed = n_ref[...]
    features = x_ref[...].astype(f32).T
    tiles = [turn(dq_ref[:, 128 * t : 128 * t + 128] * SCALE, cos_wide, sin_wide).astype(bf16) for t in range(4)]
    last = turn(
        jnp.concatenate([dq_ref[:, 512:576], jnp.zeros((ROWS, 64), f32)], 1) * SCALE, cos_wide, sin_wide
    ).astype(bf16)
    grad_q = jnp.concatenate(tiles + [last[:, 0:64]], 1)
    grad_normed = nt_dot(grad_q, wq_ref[...])

    def put(at, rows16):
        block = at // 16
        band, device = divmod(block, N_CTX)
        index = (device // 32, device // 8 % 4, device // 2 % 4, device % 2)
        parts[band][index] = rows16

    def pack(at, grads):
        height, width = grads.shape
        grads = jnp.concatenate([grads, jnp.zeros((height, 128 - width % 128), f32)], 1).astype(bf16)
        for tile in range(grads.shape[1] // 128):
            for row in range(0, height, 16):
                put(at + tile * height + row, grads[row : row + 16, 128 * tile : 128 * tile + 128])

    pack(Q_AT, tn_dot(normed, grad_q))
    for at in range(GAIN_ONE_AT + 16, ATT_ROWS, 16):
        put(at, jnp.zeros((16, 128), bf16))
    gain_rows[...] = jnp.zeros_like(gain_rows)
    advance(other, SIDE)
    run(scatter)

    last = turn(
        jnp.concatenate([done[1][:, 0:64], jnp.zeros((ROWS, 64), f32)], 1), cos_wide, sin_wide
    ).astype(bf16)
    grad_k = jnp.concatenate([turn(done[0][...], cos_wide, sin_wide).astype(bf16), last[:, 0:64]], 1)
    grad_v = jnp.concatenate([done[2][...], done[1][:, 64:128]], 1).astype(bf16)
    pack(KV_AT, tn_dot(jnp.concatenate([grad_k, grad_v], 1), normed))
    grad_normed = grad_normed + nn_dot(grad_k, wk_ref[...]) + nn_dot(grad_v, wv_ref[...])
    by_x, by_gain = rms_back(features, gain_ref[...].reshape(1, D), grad_normed)
    for tile in range(4):
        gain_rows[tile : tile + 1, :] = by_gain[:, 128 * tile : 128 * tile + 128]
    gain_rows[4:5, 0:64] = by_gain[:, 512:576]
    put(GAIN_ONE_AT, gain_rows[...].astype(bf16))

    small = scatter_steps([(part,) for part in parts], done_one, third, False)
    advance(small, 1)
    gx_ref[...] = gh_ref[...] + by_x
    turns = [(other, 3), (small, 1)]
    while turns:
        for steps, count in list(turns):
            try:
                advance(steps, count)
            except StopIteration:
                turns.remove((steps, count))
    for band in range(3):
        own[band][0:BAND_ROWS, :] = done_ff[band][...].astype(bf16)
        own[band][BAND_ROWS:FINAL_ROWS, :] = done_one[band][...].astype(bf16)
    run(gather_steps(own, outs, Pool(sems)))


def reduce_all(dkvs, dws, dq, normed, x, grad_hidden, cos_wide, sin_wide, gain, wq, wk, wv):
    vmem = pl.BlockSpec(memory_space=pltpu.VMEM)
    anywhere = pl.BlockSpec(memory_space=pl.ANY)
    one = BAND_ROWS_ONE
    return pl.pallas_call(
        reduce_kernel,
        out_shape=(jax.ShapeDtypeStruct((ROWS, D), f32),)
        + (jax.ShapeDtypeStruct((SIDE, SIDE, SIDE, 2, FINAL_ROWS, 128), bf16),) * 3,
        in_specs=[anywhere] * 6 + [vmem] * 10,
        out_specs=(vmem,) + (anywhere,) * 3,
        scratch_shapes=[pltpu.VMEM((ROWS, 128), f32)] * 3
        + [pltpu.VMEM((BAND_ROWS, 128), f32)] * 3
        + [pltpu.VMEM((one, 128), f32)] * 3
        + scatter_scratch(ROWS, True)
        + scatter_scratch(BAND_ROWS, True)
        + scatter_scratch(one, False)
        + [pltpu.VMEM((SIDE, SIDE, SIDE, 2, one, 128), bf16)] * 3
        + [pltpu.VMEM((FINAL_ROWS, 128), bf16)] * 3
        + [pltpu.VMEM((16, 128), f32), pltpu.SemaphoreType.DMA((GATHER_SEMS,))],
        compiler_params=pltpu.CompilerParams(
            collective_id=2, has_side_effects=True, vmem_limit_bytes=VMEM_LIMIT
        ),
        name="reduce_all",
    )(*dkvs, *dws, dq, normed, x, grad_hidden, cos_wide, sin_wide, gain, wq, wk, wv)


FF_PARTS = ((GATE_AT, D, FF), (UP_AT, D, FF), (DOWN_AT, D, FF), (OUT_AT, D, D))


def unpack_kernel(
    sums0, sums1, sums2, gx_ref,
    xt_ref, ga_ref, gq_ref, gk_ref, gv_ref, gm_ref, gg_hbm, gu_hbm, gd_hbm, go_hbm,
    held, held_one, full0, full1, full2, full3, sem_in, sem_one, sem_out,
):
    sums = (sums0, sums1, sums2)
    fulls = (full0, full1, full2, full3)
    spots = (gg_hbm, gu_hbm, gd_hbm, go_hbm)
    band_blocks = N_CTX
    copies = []
    edges = [0]
    for at, rows, columns in FF_PARTS:
        edges.append((at + (columns + 127) // 128 * rows) // BAND_ROWS)
    edges[-1] = 3 * band_blocks
    for part in range(4):
        mine = []
        lo = edges[part]
        while lo < edges[part + 1]:
            band = lo // band_blocks
            hi = min(edges[part + 1], (band + 1) * band_blocks)
            mine.append(
                pltpu.make_async_copy(
                    sums[band].at[pl.ds(lo - band * band_blocks, hi - lo), pl.ds(0, BAND_ROWS)],
                    held.at[pl.ds(lo, hi - lo)],
                    sem_in.at[part, len(mine)],
                )
            )
            mine[-1].start()
            lo = hi
        copies.append(mine)
    small = [
        pltpu.make_async_copy(
            sums[band].at[:, pl.ds(BAND_ROWS, BAND_ROWS_ONE)], held_one.at[band], sem_one.at[band]
        )
        for band in range(3)
    ]
    for copy in small:
        copy.start()
    xt_ref[...] = gx_ref[...].T
    outs = []
    for part, (at, rows, columns) in enumerate(FF_PARTS):
        for copy in copies[part]:
            copy.wait()
        for tile in range((columns + 127) // 128):
            width = min(128, columns - 128 * tile)
            for row in range(0, rows, BAND_ROWS):
                piece = held[(at + tile * rows + row) // BAND_ROWS].astype(f32)
                fulls[part][row : row + BAND_ROWS, 128 * tile : 128 * tile + width] = piece[:, 0:width]
        outs.append(pltpu.make_async_copy(fulls[part], spots[part], sem_out.at[part]))
        outs[-1].start()
    for copy in small:
        copy.wait()

    def fetch_one(at):
        band, block = divmod(at // BAND_ROWS_ONE, N_CTX)
        return held_one[band, block].astype(f32)

    for tile in range(5):
        width = min(128, D - 128 * tile)
        lanes = slice(128 * tile, 128 * tile + width)
        for row in range(0, D, 16):
            gq_ref[row : row + 16, lanes] = fetch_one(Q_AT + tile * D + row)[:, 0:width]
        for row in range(0, 192, 16):
            gk_ref[row : row + 16, lanes] = fetch_one(KV_AT + tile * 384 + row)[:, 0:width]
            gv_ref[row : row + 16, lanes] = fetch_one(KV_AT + tile * 384 + 192 + row)[:, 0:width]
        ga_ref[lanes] = fetch_one(GAIN_ONE_AT)[tile, 0:width]
        gm_ref[lanes] = held[GAIN_AT // BAND_ROWS].astype(f32)[tile, 0:width]
    for copy in outs:
        copy.wait()


def unpack(sums, grad_x):
    vmem = pl.BlockSpec(memory_space=pltpu.VMEM)
    anywhere = pl.BlockSpec(memory_space=pl.ANY)
    shapes = ((D, ROWS), (D,), (D, D), (192, D), (192, D), (D,), (D, FF), (D, FF), (D, FF), (D, D))
    return pl.pallas_call(
        unpack_kernel,
        out_shape=tuple(jax.ShapeDtypeStruct(s, f32) for s in shapes),
        in_specs=[anywhere] * 3 + [vmem],
        out_specs=(vmem,) * 6 + (anywhere,) * 4,
        scratch_shapes=[
            pltpu.VMEM((3 * N_CTX, BAND_ROWS, 128), bf16),
            pltpu.VMEM((3, N_CTX, BAND_ROWS_ONE, 128), bf16),
            pltpu.VMEM((D, FF), f32),
            pltpu.VMEM((D, FF), f32),
            pltpu.VMEM((D, FF), f32),
            pltpu.VMEM((D, D), f32),
            pltpu.SemaphoreType.DMA((4, 2)),
            pltpu.SemaphoreType.DMA((3,)),
            pltpu.SemaphoreType.DMA((4,)),
        ],
        compiler_params=pltpu.CompilerParams(vmem_limit_bytes=VMEM_LIMIT),
        name="unpack",
    )(
        *[s.reshape(N_CTX, FINAL_ROWS, 128) for s in sums],
        grad_x,
    )


def on_device(
    layer_input,
    attn_gain,
    w_query,
    w_key,
    w_value,
    w_out,
    mlp_gain,
    w_gate,
    w_up,
    w_down,
    cotangent,
    segment_ids,
    pair_table,
):
    own_pair = pair_table[0]
    within = jnp.arange(ROWS, dtype=jnp.int32)
    blocks = jnp.where(within < HALF, own_pair, 2 * N_CTX - 1 - own_pair)
    places = blocks * HALF + within % HALF
    lanes = jnp.arange(128, dtype=jnp.int32)
    frequency = ROPE_THETA ** (-2.0 * (lanes % (HEAD_DIM // 2)).astype(f32) / HEAD_DIM)
    turned = places.astype(f32)[:, None] * frequency[None, :]
    cos_wide = jnp.cos(turned)
    sin_wide = jnp.sin(turned) * jnp.where(lanes % HEAD_DIM < HEAD_DIM // 2, -1.0, 1.0)[None, :]

    segments = segment_ids[None, :]
    x_turned = layer_input.T
    wk_turned, wv_turned = w_key.T, w_value.T
    q_rot, normed, table, *kvs = project_and_gather(
        pair_table, x_turned, attn_gain, w_query, wk_turned, wv_turned, cos_wide, sin_wide, segments
    )
    result, grad_hidden, dq, *rest = layer(
        pair_table,
        table,
        [kv.reshape(N_CTX, ROWS, 128) for kv in kvs],
        [w_out, w_gate, w_up, w_down.T],
        q_rot,
        x_turned,
        cotangent.T,
        mlp_gain,
    )
    lead = (SIDE, SIDE, SIDE, 2)
    grad_x, *sums = reduce_all(
        [d.reshape(lead + (ROWS, 128)) for d in rest[0:3]],
        [d.reshape(lead + (BAND_ROWS, 128)) for d in rest[3:6]],
        dq,
        normed,
        x_turned,
        grad_hidden,
        cos_wide,
        sin_wide,
        attn_gain,
        w_query,
        wk_turned,
        wv_turned,
    )
    gx, ga, gq, gk, gv, gm, gg, gu, gd, go = unpack(sums, grad_x)
    return (result.T, gx.T, ga, gq, gk.T, gv.T, go, gm, gg, gu, gd.T)


def solution(mesh):
    return jax.shard_map(
        on_device,
        mesh=mesh,
        in_specs=(
            P("ctx", None),
            P(),
            P(),
            P(),
            P(),
            P(),
            P(),
            P(),
            P(),
            P(),
            P("ctx", None),
            P("ctx"),
            P("ctx"),
        ),
        out_specs=(P("ctx", None), P("ctx", None), P(), P(), P(), P(), P(), P(), P(), P(), P()),
        check_vma=False,
    )
```

```python
import functools
import jax
import jax.numpy as jnp
from jax import lax
from jax.experimental import pallas as pl
from jax.experimental.pallas import tpu as pltpu
from jax.sharding import PartitionSpec as P

f32 = jnp.float32
bf16 = jnp.bfloat16
D = 576
HEADS = 9
KV_HEADS = 3
HEAD_DIM = 64
PER_GROUP = HEADS // KV_HEADS
FF = 1536
NORM_EPS = 1e-05
ROPE_THETA = 100000.0
ROWS = 128
HALF = 64
N_CTX = 128
TOKENS = ROWS * N_CTX
DOCS = 18
META = 16
CHUNK = 512
PIECES = CHUNK // HALF
CHUNKS = TOKENS // CHUNK
BLANK = 4096
COLS = HEADS * HALF
NEG = -1e30
SCALE = HEAD_DIM ** (-0.5)
VMEM_LIMIT = 56 * 1024 * 1024

K_AT = (0, 64, 128)
V_AT = (128, 192, 64)

GATE_AT = 0
UP_AT = GATE_AT + 12 * D
DOWN_AT = UP_AT + 12 * D
OUT_AT = DOWN_AT + 12 * D
GAIN_AT = OUT_AT + 5 * D
BAND_ROWS = 64
FF_ROWS = 3 * N_CTX * BAND_ROWS
Q_AT = 0
KV_AT = Q_AT + 5 * D
GAIN_ONE_AT = KV_AT + 5 * 384
BAND_ROWS_ONE = 16
FINAL_ROWS = BAND_ROWS + BAND_ROWS_ONE
ATT_ROWS = 3 * N_CTX * BAND_ROWS_ONE

MESH = pl.DeviceIdType.MESH
SIDE = 4
ORDERS = ((2, 1, 0), (1, 0, 2), (0, 2, 1))
STRIDES = (32, 8, 2)


def whereabouts():
    me = lax.axis_index("ctx")
    coords = (me // 32, lax.rem(me // 8, SIDE), lax.rem(me // 2, SIDE))
    return me, coords, lax.rem(me, 2)


def wrap(coord, step):
    return lax.rem(coord + (step + SIDE), SIDE)


def neighbour(me, coords, axis, step):
    return me + (wrap(coords[axis], step) - coords[axis]) * STRIDES[axis]


PARTNERS = 10


def greet(me, coords, core):
    others = [me + 1 - 2 * core]
    for axis in range(3):
        others += [neighbour(me, coords, axis, step) for step in (1, -1, 2)]
    for other in others:
        pl.semaphore_signal(
            pltpu.get_barrier_semaphore(), inc=1, device_id=(other,), device_id_type=MESH
        )


def meet():
    pl.semaphore_wait(pltpu.get_barrier_semaphore(), PARTNERS)


def half_rows(rows):
    return rows // 32 * 16


class Pool:
    def __init__(self, sems):
        self.sems = sems
        self.used = 0

    def new(self):
        self.used += 1
        return self.sems.at[self.used - 1]


def send(src, dst, device, send_sem, recv_sem):
    pltpu.make_async_remote_copy(
        src_ref=src,
        dst_ref=dst,
        send_sem=send_sem,
        recv_sem=recv_sem,
        device_id=(device,),
        device_id_type=MESH,
    ).start()


def wait_for(ref, sem):
    pltpu.make_async_copy(ref, ref, sem).wait()


def at_axes(order, values):
    index = [None] * 3
    for axis, value in zip(order, values):
        index[axis] = value
    return tuple(index)


WHOLE = pl.ds(0, SIDE)


def gather_steps(own, out, pool):
    me, coords, core = whereabouts()
    sibling = me + 1 - 2 * core
    bands = range(len(own))
    orders = [ORDERS[band % 3] for band in bands]
    lines = (0, 1, -1, 2)
    steps = (1, -1, 2)

    def place(band, *values):
        return out[band].at[at_axes(orders[band], values) + (core,)]

    def mine(band, phase, step=0):
        return wrap(coords[orders[band][phase]], step)

    def device(band, phase, step):
        return neighbour(me, coords, orders[band][phase], step)

    def blocks(*shape):
        return out[0].at[tuple(pl.ds(0, size) for size in shape)]

    home, came, gone = pool.new(), [pool.new() for phase in range(3)], [pool.new(), pool.new()]
    ringed = [pool.new() for band in bands]
    across = [(pool.new(), pool.new()) for band in bands]
    ends = {line: (pool.new(), pool.new(), pool.new()) for line in lines}
    for step in steps:
        for phase in (1, 0):
            for band in bands:
                part = place(band, *(mine(band, p) for p in range(3)))
                send(own[band], part, device(band, phase, step), gone[0], came[phase])
    for band in bands:
        part = place(band, *(mine(band, p) for p in range(3)))
        pltpu.make_async_copy(own[band], part, home).start()

    def send_line(band, line):
        part = place(band, mine(band, 0, line), WHOLE, mine(band, 2))
        send(part, part, device(band, 2, 1), ringed[band], ends[line][0])
        send(part, part, device(band, 2, -1), ringed[band], ends[line][1])

    yield
    wait_for(blocks(1, 1, 3, 1), home)
    wait_for(blocks(1, 3, 3, 1), came[1])
    for band in bands:
        send_line(band, 0)
    wait_for(blocks(1, 3, 3, 1), came[0])
    for band in bands:
        for line in lines[1:]:
            part = place(band, mine(band, 0, line), mine(band, 1), mine(band, 2))
            for step in steps:
                send(part, part, device(band, 1, step), gone[1], came[2])
    yield
    wait_for(blocks(3, 3, 3, 1), came[2])
    for line in lines[1:]:
        for band in bands:
            send_line(band, line)
    for band in bands:
        part = place(band, WHOLE, WHOLE, mine(band, 2))
        send(part, part, sibling, *across[band])
    for line in lines:
        yield
        for side, step in ((0, -1), (1, 1)):
            wait_for(blocks(1, 3, 4, 1), ends[line][side])
            for band in bands:
                rows = own[band].shape[0]
                cut = half_rows(rows)
                part = place(band, mine(band, 0, line), WHOLE, mine(band, 2, step))
                half = part.at[:, pl.ds(0, cut) if side == 0 else pl.ds(cut, rows - cut)]
                send(half, half, device(band, 2, -step), ringed[band], ends[line][2])
                send(part, part, sibling, *across[band])
    for line in lines:
        yield
        wait_for(blocks(1, 3, 4, 1), ends[line][2])
        for band in bands:
            part = place(band, mine(band, 0, line), WHOLE, mine(band, 2, 2))
            send(part, part, sibling, *across[band])
    yield
    for band in bands:
        wait_for(out[band].at[:, :, :, 0], across[band][1])
        wait_for(out[band].at[:, :, :, 0], across[band][0])
        wait_for(out[band].at[0:3, :, :, 0], ringed[band])
    wait_for(blocks(3, 3, 1, 2), gone[0])
    wait_for(blocks(3, 3, 3, 1), gone[1])


GATHER_SEMS = 1 + 3 + 2 + 3 + 6 + 12


def gather_small_steps(own, out, pool):
    me, coords, core = whereabouts()
    sibling = me + 1 - 2 * core
    bands = range(len(own))
    homes = [pool.new() for band in bands]
    for band in bands:
        pltpu.make_async_copy(own[band], out[band].at[coords + (core,)], homes[band]).start()
    sent = []
    for phase in range(3):
        came = [pool.new() for band in bands]
        gone = [pool.new() for band in bands]
        for band in bands:
            order = ORDERS[band % 3]
            mine = [coords[axis] for axis in order]
            part = out[band].at[at_axes(order, [WHOLE] * phase + mine[phase:]) + (core,)]
            for step in (1, -1, 2):
                send(
                    own[band] if phase == 0 else part,
                    part,
                    neighbour(me, coords, order[phase], step),
                    gone[band],
                    came[band],
                )
        yield
        for band in bands:
            if phase == 0:
                wait_for(own[band], homes[band])
            three = (0, 0, pl.ds(0, 3), 0), (0, pl.ds(0, 3), WHOLE, 0), (pl.ds(0, 3), WHOLE, WHOLE, 0)
            wait_for(out[band].at[three[phase]], came[band])
            sent.append((out[band].at[three[phase]], gone[band]))
    across = [(pool.new(), pool.new()) for band in bands]
    for band in bands:
        part = out[band].at[:, :, :, core]
        send(part, part, sibling, *across[band])
    yield
    for band in bands:
        wait_for(out[band].at[:, :, :, 0], across[band][1])
        wait_for(out[band].at[:, :, :, 0], across[band][0])
    for ref, sem in sent:
        wait_for(ref, sem)


GATHER_SMALL_SEMS = 1 + 3 * 2 + 2


def run(steps):
    for _ in steps:
        pass


def scatter_scratch(rows, ring):
    shapes = [pltpu.VMEM((SIDE, SIDE, SIDE, rows, 128), bf16)] * 6
    for _ in range(3):
        shapes += [
            pltpu.VMEM((3, SIDE, SIDE, rows, 128), bf16),
            pltpu.VMEM((3, SIDE, rows, 128), bf16),
            pltpu.VMEM((3, rows, 128), bf16),
        ]
    return shapes + [pltpu.SemaphoreType.DMA((6 + 2 + 4 + 16 + 8 + 2 if ring else 6 + 2 + 6 + 3 + 2,))]


SCATTER_REFS = 16


def scatter_steps(parts, done, scratch, ring):
    acc, sib = scratch[0:3], scratch[3:6]
    landing = [scratch[6 + 3 * b : 9 + 3 * b] for b in range(3)]
    pool = Pool(scratch[15])
    me, coords, core = whereabouts()
    sibling = me + 1 - 2 * core
    bands = range(3)
    steps = (2, 1, -1, 0)
    rows = acc[0].shape[3]
    cut = half_rows(rows)
    def blocks(*shape):
        return acc[0].at[tuple(pl.ds(0, size) for size in shape)]

    sent = [[pool.new(), None, None, pool.new()] for band in bands]
    for phase in (1, 2):
        shared = pool.new()
        for band in bands:
            sent[band][phase] = shared
    homes, swaps = {}, {}

    def line_at(band, step, sub):
        order = ORDERS[band]
        return at_axes(order, (wrap(coords[order[0]], step), wrap(coords[order[1]], steps[sub]), WHOLE))

    if ring:
        for step in steps:
            for band in bands:
                order = ORDERS[band]
                plane = at_axes(order, (wrap(coords[order[0]], step), WHOLE, WHOLE))
                if band == 0:
                    homes[step] = pool.new()
                top = 0
                for part in parts[band]:
                    size = part.shape[4]
                    pltpu.make_async_copy(
                        part.at[plane + (core,)],
                        acc[band].at[plane + (pl.ds(top, size),)],
                        homes[step],
                    ).start()
                    top += size
            for sub in range(SIDE):
                for band in bands:
                    line = line_at(band, step, sub)
                    if band == 0:
                        swaps[step, sub] = pool.new()
                    top = 0
                    for part in parts[band]:
                        size = part.shape[4]
                        send(
                            part.at[line + (1 - core,)],
                            sib[band].at[line + (pl.ds(top, size),)],
                            sibling,
                            sent[band][3],
                            swaps[step, sub],
                        )
                        top += size
    else:
        for band in bands:
            homes[band], swaps[band] = pool.new(), pool.new()
            (part,) = parts[band]
            pltpu.make_async_copy(part.at[:, :, :, core], acc[band], homes[band]).start()
            send(part.at[:, :, :, 1 - core], sib[band], sibling, sent[band][3], swaps[band])

    def add_swap(band, step, sub):
        if band == 0:
            if sub == 0:
                wait_for(blocks(3, 4, 4), homes[step])
            wait_for(blocks(1, 3, 4), swaps[step, sub])

        line = line_at(band, step, sub)
        acc[band][line] = acc[band][line] + sib[band][line]

    def sum_up(band, region, landed):
        total = acc[band][region].astype(f32)
        for ref in landed:
            total = total + ref[...].astype(f32)
        acc[band][region] = total.astype(bf16)

    second = pool.new()

    def send_second(band, sub):
        if steps[sub]:
            send(
                acc[band].at[line_at(band, 0, sub)],
                landing[band][1].at[sub],
                neighbour(me, coords, ORDERS[band][1], steps[sub]),
                sent[band][1],
                second,
            )

    if ring:
        passing, ending = {}, {}
        for sub in range(SIDE):
            yield
            passing[sub], ending[sub] = pool.new(), pool.new()
            for band in bands:
                axis = ORDERS[band][0]
                add_swap(band, 2, sub)
                far = acc[band].at[line_at(band, 2, sub)]
                for lo, size, step in ((0, cut, 1), (cut, rows - cut, -1)):
                    send(
                        far.at[:, pl.ds(lo, size)],
                        landing[band][0].at[0, sub, :, pl.ds(lo, size)],
                        neighbour(me, coords, axis, step),
                        sent[band][0],
                        passing[sub],
                    )
        for sub in range(SIDE):
            yield
            for step in (1, -1):
                for band in bands:
                    add_swap(band, step, sub)
            wait_for(blocks(1, 3, 4), passing[sub])
            for band in bands:
                order = ORDERS[band]
                for slot, lo, size, step in ((1, 0, cut, 1), (2, cut, rows - cut, -1)):
                    half = line_at(band, step, sub) + (pl.ds(lo, size),)
                    acc[band][half] = acc[band][half] + landing[band][0][0, sub, :, lo : lo + size]
                    send(
                        acc[band].at[line_at(band, step, sub)],
                        landing[band][0].at[slot, sub],
                        neighbour(me, coords, order[0], step),
                        sent[band][0],
                        ending[sub],
                    )
        for sub in range(SIDE):
            yield
            for band in bands:
                add_swap(band, 0, sub)
            wait_for(blocks(2, 3, 4), ending[sub])
            for band in bands:
                order = ORDERS[band]
                sum_up(
                    band, line_at(band, 0, sub), [landing[band][0].at[slot, sub] for slot in (1, 2)]
                )
                send_second(band, sub)
    else:
        came = [pool.new() for band in bands]
        yield
        for band in bands:
            axis = ORDERS[band][0]
            wait_for(acc[band], homes[band])
            wait_for(sib[band], swaps[band])
            acc[band][...] = acc[band][...] + sib[band][...]
            for slot, step in enumerate((2, 1, -1)):
                plane = at_axes(ORDERS[band], (wrap(coords[axis], step), WHOLE, WHOLE))
                send(
                    acc[band].at[plane],
                    landing[band][0].at[slot],
                    neighbour(me, coords, axis, step),
                    sent[band][0],
                    came[band],
                )
        yield
        for band in bands:
            plane = at_axes(ORDERS[band], (coords[ORDERS[band][0]], WHOLE, WHOLE))
            wait_for(landing[band][0], came[band])
            total = acc[band][plane].astype(f32)
            for slot in range(3):
                total = total + landing[band][0][slot].astype(f32)
            acc[band][plane] = total.astype(bf16)
    if not ring:
        for sub in range(SIDE):
            for band in bands:
                send_second(band, sub)
    yield
    ends = pool.new()
    wait_for(blocks(3, 3, 4), second)
    for band in bands:
        order = ORDERS[band]
        line = at_axes(order, (coords[order[0]], coords[order[1]], WHOLE))
        sum_up(band, line, [landing[band][1].at[slot] for slot in range(3)])
        for slot, step in enumerate((2, 1, -1)):
            at = at_axes(order, (coords[order[0]], coords[order[1]], wrap(coords[order[2]], step)))
            send(
                acc[band].at[at],
                landing[band][2].at[slot],
                neighbour(me, coords, order[2], step),
                sent[band][2],
                ends,
            )
    yield
    wait_for(blocks(1, 3, 3), ends)
    for band in bands:
        total = acc[band][coords].astype(f32)
        for slot in range(3):
            total = total + landing[band][2][slot].astype(f32)
        done[band][...] = total
    for band in bands:
        wait_for(acc[band].at[0:3], sent[band][0])
        wait_for(acc[band], sent[band][3])
    wait_for(blocks(3, 3, 4), sent[0][1])
    wait_for(blocks(1, 3, 3), sent[0][2])


def rms_parts(features):
    return lax.rsqrt(jnp.mean(features * features, axis=-1, keepdims=True) + NORM_EPS)


def rms_back(features, gain, grad):
    inverse = rms_parts(features)
    scaled = grad * gain
    inner = jnp.mean(scaled * features, axis=-1, keepdims=True)
    by_features = inverse * scaled - features * (inverse * inverse * inverse * inner)
    by_gain = jnp.sum(grad * features * inverse, axis=0, keepdims=True)
    return by_features, by_gain


def nt_dot(left, right):
    return lax.dot_general(left, right, (((1,), (1,)), ((), ())), preferred_element_type=f32)


def tn_dot(left, right):
    return lax.dot_general(left, right, (((0,), (0,)), ((), ())), preferred_element_type=f32)


def nn_dot(left, right):
    return jnp.dot(left, right, preferred_element_type=f32)


def turn(tile, cos_wide, sin_wide):
    lanes = lax.broadcasted_iota(jnp.int32, tile.shape, 1)
    swapped = jnp.where(
        lax.rem(lanes, HEAD_DIM) < HEAD_DIM // 2, pltpu.roll(tile, 96, 1), pltpu.roll(tile, 32, 1)
    )
    return tile * cos_wide + swapped * sin_wide


def project_kernel(
    pair_ref, x_ref, gain_ref, wq_ref, wk_ref, wv_ref, cos_ref, sin_ref, seg_ref,
    q_ref, n_ref, table_ref, out0, out1, out2,
    own0, own1, own2, own_meta, metas, sems, meta_sems,
):
    me, coords, core = whereabouts()
    greet(me, coords, core)
    segments = jnp.broadcast_to(seg_ref[...].astype(f32), (ROWS, ROWS)).T
    lanes = lax.broadcasted_iota(jnp.int32, (ROWS, ROWS), 1)
    earlier = jnp.sum(jnp.where(segments < (lanes - 1).astype(f32), 1.0, 0.0), axis=0, keepdims=True)
    meta = jnp.where(lanes[0:1] == 0, pair_ref[0].astype(f32), earlier)
    own_meta[...] = jnp.broadcast_to(meta, (META, 128)).astype(bf16)
    features = x_ref[...].astype(f32).T
    normed = (features * rms_parts(features) * gain_ref[...].reshape(1, D)).astype(bf16)
    n_ref[...] = normed
    cos_wide, sin_wide = cos_ref[...], sin_ref[...]
    keys = nt_dot(normed, wk_ref[...])
    values = nt_dot(normed, wv_ref[...]).astype(bf16)
    queries = nn_dot(normed, wq_ref[...])
    own0[...] = turn(keys[:, 0:128], cos_wide, sin_wide).astype(bf16)
    mixed = turn(jnp.concatenate([keys[:, 128:192], queries[:, 512:576]], 1), cos_wide, sin_wide)
    own1[...] = jnp.concatenate([mixed[:, 0:64].astype(bf16), values[:, 128:192]], 1)
    own2[...] = values[:, 0:128]
    meet()
    steps = gather_steps((own0, own1, own2), (out0, out1, out2), Pool(sems))
    small = gather_small_steps((own_meta,), (metas,), Pool(meta_sems))
    next(small)
    next(steps)
    next(small)
    for tile in range(4):
        at = slice(128 * tile, 128 * tile + 128)
        q_ref[:, at] = (turn(queries[:, at], cos_wide, sin_wide).astype(bf16).astype(f32) * SCALE).astype(bf16)
    q_ref[:, 512:576] = (mixed[:, 64:128].astype(bf16).astype(f32) * SCALE).astype(bf16)
    next(steps)
    next(small)
    for _ in range(3):
        next(steps)
    next(small)
    for _ in range(3):
        next(steps)
    run(small)
    columns = metas[:, :, :, :, 0, :].astype(f32).reshape(N_CTX, 128)
    starts = jnp.sum(columns, axis=0, keepdims=True)
    numbers = lax.broadcasted_iota(jnp.int32, (N_CTX, N_CTX), 0).astype(f32)
    holders = jnp.sum(
        jnp.where(columns[:, 0:1] == lanes.astype(f32), numbers, 0.0), axis=0, keepdims=True
    )
    segment_row = seg_ref[...].astype(f32)
    row_starts = jnp.zeros((1, ROWS), f32)
    for document in range(DOCS):
        row_starts = jnp.where(
            segment_row == float(document), starts[:, document + 1 : document + 2], row_starts
        )
    table_ref[...] = jnp.concatenate(
        [holders, row_starts, jnp.zeros((6, 128), f32)], 0
    ).astype(jnp.int32)
    run(steps)


def project_and_gather(pair, x, gain, wq, wk, wv, cos_wide, sin_wide, segments):
    vmem = pl.BlockSpec(memory_space=pltpu.VMEM)
    anywhere = pl.BlockSpec(memory_space=pl.ANY)
    return pl.pallas_call(
        project_kernel,
        out_shape=(
            jax.ShapeDtypeStruct((ROWS, D), bf16),
            jax.ShapeDtypeStruct((ROWS, D), bf16),
            jax.ShapeDtypeStruct((8, 128), jnp.int32),
        )
        + (jax.ShapeDtypeStruct((SIDE, SIDE, SIDE, 2, ROWS, 128), bf16),) * 3,
        in_specs=[pl.BlockSpec(memory_space=pltpu.SMEM)] + [vmem] * 8,
        out_specs=(vmem, vmem, vmem, anywhere, anywhere, anywhere),
        scratch_shapes=[pltpu.VMEM((ROWS, 128), bf16)] * 3
        + [
            pltpu.VMEM((META, 128), bf16),
            pltpu.VMEM((SIDE, SIDE, SIDE, 2, META, 128), bf16),
            pltpu.SemaphoreType.DMA((GATHER_SEMS,)),
            pltpu.SemaphoreType.DMA((GATHER_SMALL_SEMS,)),
        ],
        compiler_params=pltpu.CompilerParams(
            collective_id=1, has_side_effects=True, vmem_limit_bytes=VMEM_LIMIT
        ),
        name="project_and_gather",
    )(pair, x, gain, wq, wk, wv, cos_wide, sin_wide, segments)


def needed(chunk, a_hi, b_lo, b_hi):
    return (chunk <= a_hi) | ((chunk >= b_lo) & (chunk <= b_hi))


def chunk_rows(chunk, count=1):
    return pl.ds(pl.multiple_of(chunk * CHUNK, CHUNK), count * CHUNK)


def wait_chunk(chunk, held, sem):
    window = held.at[chunk_rows(chunk)]
    pltpu.make_async_copy(window, window, sem.at[chunk]).wait()


def chunk_mask(chunk, count, place_row, start_row):
    keys = chunk * CHUNK + lax.broadcasted_iota(jnp.int32, (count * CHUNK, COLS), 0)
    return (keys <= place_row) & (keys >= start_row)


def layer_kernel(
    pair_ref, table,
    kv0, kv1, kv2, wo_hbm, wg_hbm, wu_hbm, wd_hbm,
    q_ref, starts_ref, x_ref, c_ref, gain_ref,
    result_ref, gh_ref, dq_ref, dkv0, dkv1, dkv2, dw0, dw1, dw2,
    held, sem, wo_ref, wg_ref, wu_ref, wd_ref, w_sem, q_spread, g_spread, mixed, top, total, att_ref,
    delta_ref, dw, dw_sem, staged, blank, out_sem, blank_sem, gain_rows,
    rows_ref,
):
    kvs, dkvs, dws = (kv0, kv1, kv2), (dkv0, dkv1, dkv2), (dw0, dw1, dw2)
    weights = [
        pltpu.make_async_copy(src, dst, w_sem.at[i])
        for i, (src, dst) in enumerate(
            ((wo_hbm, wo_ref), (wg_hbm, wg_ref), (wu_hbm, wu_ref), (wd_hbm, wd_ref))
        )
    ]
    pair = pair_ref[0]
    row_starts = starts_ref[1:2, :]
    for block in range(2):
        first = pair if block == 0 else 2 * N_CTX - 1 - pair
        places = first * HALF + lax.rem(lax.broadcasted_iota(jnp.int32, (1, COLS), 1), HALF)
        rows_ref[2 * block : 2 * block + 1, :] = places
        mine = row_starts[:, block * HALF : (block + 1) * HALF]
        rows_ref[2 * block + 1 : 2 * block + 2, :] = jnp.concatenate([mine] * HEADS, 1)
    a_hi, b_lo, b_hi = pair // PIECES, table[1, HALF] // CHUNK, (2 * N_CTX - 1 - pair) // PIECES

    def slot_of(block_number):
        low = table[0, jnp.minimum(block_number, 2 * N_CTX - 1 - block_number)]
        return low * ROWS + jnp.where(block_number < N_CTX, 0, HALF)


    def issue(chunk, carry):
        @pl.when(needed(chunk, a_hi, b_lo, b_hi))
        def _():
            for piece in range(PIECES):
                slot = slot_of(chunk * PIECES + piece)
                rows = pl.ds(pl.multiple_of(chunk * CHUNK + piece * HALF, HALF), HALF)
                device, top = slot // ROWS, pl.multiple_of(lax.rem(slot, ROWS), HALF)
                for band in range(3):
                    pltpu.make_async_copy(
                        kvs[band].at[device, pl.ds(top, HALF)],
                        held.at[rows, 128 * band : 128 * band + 128],
                        sem.at[chunk],
                    ).start()

        return carry

    lax.fori_loop(0, CHUNKS, issue, 0)
    for copy in weights:
        copy.start()

    def spread(rows, place, windows):
        for block in range(2):
            for head in range(HEADS):
                tile = rows[block * HALF : (block + 1) * HALF, head * HEAD_DIM : (head + 1) * HEAD_DIM]
                at = windows[head // PER_GROUP]
                place[block, head * HALF : (head + 1) * HALF, at : at + HEAD_DIM] = tile

    def unspread(columns, place, block, windows):
        for head in range(HEADS):
            at = windows[head // PER_GROUP]
            tile = columns[at : at + HEAD_DIM, head * HALF : (head + 1) * HALF]
            place[block * HALF : (block + 1) * HALF, head * HEAD_DIM : (head + 1) * HEAD_DIM] = tile.T

    blank[...] = jnp.zeros_like(blank)

    clears = [
        pltpu.make_async_copy(blank, dkvs[band].at[pl.ds(row, BLANK)], blank_sem.at[band, row // BLANK])
        for band in range(3)
        for row in range(0, TOKENS, BLANK)
    ]
    q_spread[...] = jnp.zeros_like(q_spread)
    g_spread[...] = jnp.zeros_like(g_spread)
    spread(q_ref[...], q_spread, K_AT)
    mixed[...] = jnp.zeros_like(mixed)
    top[...] = jnp.full_like(top, NEG)
    total[...] = jnp.zeros_like(total)

    def mask_of(block, chunk, count):
        return chunk_mask(
            chunk, count, rows_ref[2 * block : 2 * block + 1, :], rows_ref[2 * block + 1 : 2 * block + 2, :]
        )

    def forward(block, chunk, masked, count=1):
        window = chunk_rows(chunk, count)
        scores = nt_dot(held[window, 0:256], q_spread[block])
        if masked:
            scores = jnp.where(mask_of(block, chunk, count), scores, NEG)
        old = top[block : block + 1, :]
        new = jnp.maximum(old, jnp.max(scores, axis=0, keepdims=True))
        probs = jnp.exp(scores - new)
        shrink = jnp.exp(old - new)
        top[block : block + 1, :] = new
        total[block : block + 1, :] = total[block : block + 1, :] * shrink + jnp.sum(
            probs, axis=0, keepdims=True
        )
        values = held[window, 128:384].T[64:256]
        mixed[block, 64:256] = mixed[block, 64:256] * shrink + nn_dot(values, probs.astype(bf16))

    def forward_step(chunk, carry):
        in_b = (chunk >= b_lo) & (chunk <= b_hi)

        @pl.when(needed(chunk, a_hi, b_lo, b_hi))
        def _():
            wait_chunk(chunk, held, sem)

        @pl.when(chunk <= a_hi)
        def _():
            forward(0, chunk, True)

        @pl.when(in_b)
        def _():
            forward(1, chunk, True)

        return carry

    def forward_pair(pair_of, carry):
        wait_chunk(2 * pair_of, held, sem)
        wait_chunk(2 * pair_of + 1, held, sem)
        forward(0, 2 * pair_of, False, 2)
        return carry

    plain = jnp.minimum(a_hi, b_lo) // 2
    tail = 2 * plain
    paired = (a_hi == tail + 1) & (b_lo > a_hi)
    ahead = jnp.where(paired, tail + 2, tail)
    lax.fori_loop(0, plain, forward_pair, 0)

    @pl.when(paired)
    def _():
        wait_chunk(tail, held, sem)
        wait_chunk(tail + 1, held, sem)
        forward(0, tail, True, 2)

    lax.fori_loop(ahead, b_hi + 1, forward_step, 0)
    for block in range(2):
        sums = total[block : block + 1, :]
        top[block : block + 1, :] = top[block : block + 1, :] + jnp.log(sums)
        mixed[block] = mixed[block] / sums
        unspread(mixed.at[block], att_ref, block, V_AT)

    for copy in clears:
        copy.start()

    attended = att_ref[...].astype(bf16)
    cotangent = c_ref[...].astype(f32).T.astype(bf16)
    gain = gain_ref[...].reshape(1, D)
    for copy in weights:
        copy.wait()
    hidden = x_ref[...].astype(f32).T + nn_dot(attended, wo_ref[...])
    normed = (hidden * rms_parts(hidden) * gain).astype(bf16)
    gate = nn_dot(normed, wg_ref[...])
    upward = nn_dot(normed, wu_ref[...])
    open_gate = jax.nn.sigmoid(gate)
    silu = gate * open_gate
    active = (silu * upward).astype(bf16)
    result_ref[...] = (hidden + nt_dot(active, wd_ref[...])).T.astype(bf16)
    grad_active = nn_dot(cotangent, wd_ref[...])
    grad_gate = (grad_active * upward * open_gate * (1.0 + gate * (1.0 - open_gate))).astype(bf16)
    grad_up = (grad_active * silu).astype(bf16)
    grad_normed = nt_dot(grad_gate, wg_ref[...]) + nt_dot(grad_up, wu_ref[...])
    by_hidden, by_gain = rms_back(hidden, gain, grad_normed)
    grad_hidden = cotangent.astype(f32) + by_hidden
    gh_ref[...] = grad_hidden
    grad_out = grad_hidden.astype(bf16)
    spread(nt_dot(grad_out, wo_ref[...]).astype(bf16), g_spread, V_AT)
    for block in range(2):
        turned = g_spread[block].astype(f32).T
        delta_ref[block : block + 1, :] = jnp.sum(turned * mixed[block], axis=0, keepdims=True)

    def pack(at, grads):
        rows = grads.shape[0]
        for tile in range(grads.shape[1] // 128):
            dw[at + tile * rows : at + (tile + 1) * rows, :] = grads[:, 128 * tile : 128 * tile + 128].astype(bf16)
        if grads.shape[1] % 128:
            tile = grads.shape[1] // 128
            dw[at + tile * rows : at + (tile + 1) * rows, 0:64] = grads[:, 128 * tile : 128 * tile + 64].astype(bf16)
            dw[at + tile * rows : at + (tile + 1) * rows, 64:128] = jnp.zeros((rows, 64), bf16)

    pack(GATE_AT, tn_dot(normed, grad_gate))
    pack(UP_AT, tn_dot(normed, grad_up))
    pack(DOWN_AT, tn_dot(cotangent, active))
    pack(OUT_AT, tn_dot(attended, grad_out))
    gain_rows[...] = jnp.zeros_like(gain_rows)
    for tile in range(4):
        gain_rows[tile : tile + 1, :] = by_gain[:, 128 * tile : 128 * tile + 128]
    gain_rows[4:5, 0:64] = by_gain[:, 512:576]
    dw[GAIN_AT : GAIN_AT + 16, :] = gain_rows[...].astype(bf16)
    dw[GAIN_AT + 16 : FF_ROWS, :] = jnp.zeros((FF_ROWS - GAIN_AT - 16, 128), bf16)
    band_rows = FF_ROWS // 3
    dw_copies = [
        pltpu.make_async_copy(dw.at[pl.ds(band * band_rows, band_rows)], dws[band], dw_sem.at[band])
        for band in range(3)
    ]
    for copy in dw_copies:
        copy.start()

    for copy in clears:
        copy.wait()
    mixed[...] = jnp.zeros_like(mixed)

    def backward(block, chunk, masked, mode, count=1):
        window = chunk_rows(chunk, count)
        keys = held[window, 0:256]
        values = held[window, 128:384]
        scores = nt_dot(keys, q_spread[block])
        probs = jnp.exp(scores - top[block : block + 1, :])
        if masked:
            probs = jnp.where(mask_of(block, chunk, count), probs, 0.0)
        grad_probs = nt_dot(values, g_spread[block])
        grad_scores = (probs * (grad_probs - delta_ref[block : block + 1, :])).astype(bf16)
        mixed[block, 0:192] += nn_dot(keys.T[0:192], grad_scores)
        dk = nn_dot(grad_scores, q_spread[block])
        dv = nn_dot(probs.astype(bf16), g_spread[block])
        parts = (dk[:, 0:128], dk[:, 128:256] + dv[:, 0:128], dv[:, 128:256])
        for band in range(3):
            at = slice(128 * band, 128 * band + 128)
            if mode == "first":
                staged[:, at] = parts[band]
            elif mode == "second":
                held[window, at] = (staged[:, at] + parts[band]).astype(bf16)
            else:
                held[window, at] = parts[band].astype(bf16)

    def put_back(chunk):
        for piece in range(PIECES):
            row = pl.multiple_of(slot_of(chunk * PIECES + piece), HALF)
            rows = pl.ds(pl.multiple_of(chunk * CHUNK + piece * HALF, HALF), HALF)
            for band in range(3):
                pltpu.make_async_copy(
                    held.at[rows, 128 * band : 128 * band + 128],
                    dkvs[band].at[pl.ds(row, HALF)],
                    out_sem.at[chunk],
                ).start()

    def backward_step(chunk, carry):
        in_a = chunk <= a_hi
        in_b = (chunk >= b_lo) & (chunk <= b_hi)

        @pl.when(in_a & jnp.logical_not(in_b))
        def _():
            backward(0, chunk, True, "only")

        @pl.when(in_b & jnp.logical_not(in_a))
        def _():
            backward(1, chunk, True, "only")

        @pl.when(in_a & in_b)
        def _():
            backward(0, chunk, True, "first")
            backward(1, chunk, True, "second")

        @pl.when(in_a | in_b)
        def _():
            put_back(chunk)

        return carry

    def backward_pair(pair_of, carry):
        backward(0, 2 * pair_of, False, "only", 2)
        put_back(2 * pair_of)
        put_back(2 * pair_of + 1)
        return carry

    lax.fori_loop(0, plain, backward_pair, 0)

    @pl.when(paired)
    def _():
        backward(0, tail, True, "only", 2)
        put_back(tail)
        put_back(tail + 1)

    lax.fori_loop(ahead, b_hi + 1, backward_step, 0)
    for block in range(2):
        unspread(mixed.at[block], dq_ref, block, K_AT)

    def drain(chunk, carry):
        use = needed(chunk, a_hi, b_lo, b_hi)

        @pl.when(use)
        def _():
            wait_chunk(chunk, held, out_sem)

        return carry

    lax.fori_loop(0, CHUNKS, drain, 0)
    for copy in dw_copies:
        copy.wait()


def layer(pair, table, kvs, weights, q, x, cotangent, gain):
    vmem = pl.BlockSpec(memory_space=pltpu.VMEM)
    anywhere = pl.BlockSpec(memory_space=pl.ANY)
    return pl.pallas_call(
        layer_kernel,
        out_shape=(
            jax.ShapeDtypeStruct((D, ROWS), bf16),
            jax.ShapeDtypeStruct((ROWS, D), f32),
            jax.ShapeDtypeStruct((ROWS, D), f32),
        )
        + (jax.ShapeDtypeStruct((TOKENS, 128), bf16),) * 3
        + (jax.ShapeDtypeStruct((FF_ROWS // 3, 128), bf16),) * 3,
        grid_spec=pltpu.PrefetchScalarGridSpec(
            num_scalar_prefetch=2,
            in_specs=[anywhere] * 7 + [vmem] * 5,
            out_specs=(vmem,) * 3 + (anywhere,) * 6,
            scratch_shapes=[
                pltpu.VMEM((TOKENS, 384), bf16),
                pltpu.SemaphoreType.DMA((CHUNKS,)),
                pltpu.VMEM((D, D), bf16),
                pltpu.VMEM((D, FF), bf16),
                pltpu.VMEM((D, FF), bf16),
                pltpu.VMEM((D, FF), bf16),
                pltpu.SemaphoreType.DMA((4,)),
                pltpu.VMEM((2, COLS, 256), bf16),
                pltpu.VMEM((2, COLS, 256), bf16),
                pltpu.VMEM((2, 256, COLS), f32),
                pltpu.VMEM((2, COLS), f32),
                pltpu.VMEM((2, COLS), f32),
                pltpu.VMEM((ROWS, D), f32),
                pltpu.VMEM((2, COLS), f32),
                pltpu.VMEM((FF_ROWS, 128), bf16),
                pltpu.SemaphoreType.DMA((3,)),
                pltpu.VMEM((CHUNK, 384), f32),
                pltpu.VMEM((BLANK, 128), bf16),
                pltpu.SemaphoreType.DMA((CHUNKS,)),
                pltpu.SemaphoreType.DMA((3, TOKENS // BLANK)),
                pltpu.VMEM((16, 128), f32),
                pltpu.VMEM((4, COLS), jnp.int32),
            ],
        ),
        compiler_params=pltpu.CompilerParams(vmem_limit_bytes=VMEM_LIMIT),
        name="layer",
    )(pair, table, *kvs, *weights, q, table, x, cotangent, gain)


def reduce_kernel(*refs):
    dkv, dws = refs[0:3], refs[3:6]
    dq_ref, n_ref, x_ref, gh_ref, cos_ref, sin_ref, gain_ref, wq_ref, wk_ref, wv_ref = refs[6:16]
    gx_ref, outs = refs[16], refs[17:20]
    rest = refs[20:]
    done, done_ff, done_one, rest = rest[0:3], rest[3:6], rest[6:9], rest[9:]
    first, rest = rest[:SCATTER_REFS], rest[SCATTER_REFS:]
    second, rest = rest[:SCATTER_REFS], rest[SCATTER_REFS:]
    third, rest = rest[:SCATTER_REFS], rest[SCATTER_REFS:]
    parts, own, rest = rest[0:3], rest[3:6], rest[6:]
    gain_rows, sems = rest
    me, coords, core = whereabouts()
    greet(me, coords, core)
    meet()

    def advance(steps, count):
        for _ in range(count):
            next(steps)

    scatter = scatter_steps([(d,) for d in dkv], done, first, True)
    other = scatter_steps([(dw,) for dw in dws], done_ff, second, True)
    advance(scatter, 1)
    advance(other, 1)
    advance(scatter, 12)

    cos_wide, sin_wide = cos_ref[...], -sin_ref[...]
    normed = n_ref[...]
    features = x_ref[...].astype(f32).T
    tiles = [turn(dq_ref[:, 128 * t : 128 * t + 128] * SCALE, cos_wide, sin_wide).astype(bf16) for t in range(4)]
    last = turn(
        jnp.concatenate([dq_ref[:, 512:576], jnp.zeros((ROWS, 64), f32)], 1) * SCALE, cos_wide, sin_wide
    ).astype(bf16)
    grad_q = jnp.concatenate(tiles + [last[:, 0:64]], 1)
    grad_normed = nt_dot(grad_q, wq_ref[...])

    def put(at, rows16):
        block = at // 16
        band, device = divmod(block, N_CTX)
        index = (device // 32, device // 8 % 4, device // 2 % 4, device % 2)
        parts[band][index] = rows16

    def pack(at, grads):
        height, width = grads.shape
        grads = jnp.concatenate([grads, jnp.zeros((height, 128 - width % 128), f32)], 1).astype(bf16)
        for tile in range(grads.shape[1] // 128):
            for row in range(0, height, 16):
                put(at + tile * height + row, grads[row : row + 16, 128 * tile : 128 * tile + 128])

    pack(Q_AT, tn_dot(normed, grad_q))
    for at in range(GAIN_ONE_AT + 16, ATT_ROWS, 16):
        put(at, jnp.zeros((16, 128), bf16))
    gain_rows[...] = jnp.zeros_like(gain_rows)
    advance(other, SIDE)
    advance(scatter, 1)
    advance(other, SIDE)
    run(scatter)

    last = turn(
        jnp.concatenate([done[1][:, 0:64], jnp.zeros((ROWS, 64), f32)], 1), cos_wide, sin_wide
    ).astype(bf16)
    grad_k = jnp.concatenate([turn(done[0][...], cos_wide, sin_wide).astype(bf16), last[:, 0:64]], 1)
    grad_v = jnp.concatenate([done[2][...], done[1][:, 64:128]], 1).astype(bf16)
    pack(KV_AT, tn_dot(jnp.concatenate([grad_k, grad_v], 1), normed))
    grad_normed = grad_normed + nn_dot(grad_k, wk_ref[...]) + nn_dot(grad_v, wv_ref[...])
    by_x, by_gain = rms_back(features, gain_ref[...].reshape(1, D), grad_normed)
    for tile in range(4):
        gain_rows[tile : tile + 1, :] = by_gain[:, 128 * tile : 128 * tile + 128]
    gain_rows[4:5, 0:64] = by_gain[:, 512:576]
    put(GAIN_ONE_AT, gain_rows[...].astype(bf16))

    small = scatter_steps([(part,) for part in parts], done_one, third, False)
    advance(small, 1)
    gx_ref[...] = gh_ref[...] + by_x
    turns = [(other, 2), (small, 1)]
    while turns:
        for steps, count in list(turns):
            try:
                advance(steps, count)
            except StopIteration:
                turns.remove((steps, count))
    for band in range(3):
        own[band][0:BAND_ROWS, :] = done_ff[band][...].astype(bf16)
        own[band][BAND_ROWS:FINAL_ROWS, :] = done_one[band][...].astype(bf16)
    run(gather_steps(own, outs, Pool(sems)))


def reduce_all(dkvs, dws, dq, normed, x, grad_hidden, cos_wide, sin_wide, gain, wq, wk, wv):
    vmem = pl.BlockSpec(memory_space=pltpu.VMEM)
    anywhere = pl.BlockSpec(memory_space=pl.ANY)
    one = BAND_ROWS_ONE
    return pl.pallas_call(
        reduce_kernel,
        out_shape=(jax.ShapeDtypeStruct((ROWS, D), f32),)
        + (jax.ShapeDtypeStruct((SIDE, SIDE, SIDE, 2, FINAL_ROWS, 128), bf16),) * 3,
        in_specs=[anywhere] * 6 + [vmem] * 10,
        out_specs=(vmem,) + (anywhere,) * 3,
        scratch_shapes=[pltpu.VMEM((ROWS, 128), f32)] * 3
        + [pltpu.VMEM((BAND_ROWS, 128), f32)] * 3
        + [pltpu.VMEM((one, 128), f32)] * 3
        + scatter_scratch(ROWS, True)
        + scatter_scratch(BAND_ROWS, True)
        + scatter_scratch(one, False)
        + [pltpu.VMEM((SIDE, SIDE, SIDE, 2, one, 128), bf16)] * 3
        + [pltpu.VMEM((FINAL_ROWS, 128), bf16)] * 3
        + [pltpu.VMEM((16, 128), f32), pltpu.SemaphoreType.DMA((GATHER_SEMS,))],
        compiler_params=pltpu.CompilerParams(
            collective_id=2, has_side_effects=True, vmem_limit_bytes=VMEM_LIMIT
        ),
        name="reduce_all",
    )(*dkvs, *dws, dq, normed, x, grad_hidden, cos_wide, sin_wide, gain, wq, wk, wv)


FF_PARTS = ((GATE_AT, D, FF), (UP_AT, D, FF), (DOWN_AT, D, FF), (OUT_AT, D, D))


def unpack_kernel(
    sums0, sums1, sums2, gx_ref,
    ga_ref, gm_ref, xt_hbm, gq_hbm, gk_hbm, gv_hbm, gg_hbm, gu_hbm, gd_hbm, go_hbm,
    held, held_one, full0, full1, full2, full3, xt_ref, gq_ref, gk_ref, gv_ref, sem_in, sem_one, sem_out,
):
    sums = (sums0, sums1, sums2)
    fulls = (full0, full1, full2, full3)
    spots = (gg_hbm, gu_hbm, gd_hbm, go_hbm)
    band_blocks = N_CTX
    copies = []
    edges = [0]
    for at, rows, columns in FF_PARTS:
        edges.append((at + (columns + 127) // 128 * rows) // BAND_ROWS)
    edges[-1] = 3 * band_blocks
    for part in range(4):
        mine = []
        lo = edges[part]
        while lo < edges[part + 1]:
            band = lo // band_blocks
            hi = min(edges[part + 1], (band + 1) * band_blocks)
            mine.append(
                pltpu.make_async_copy(
                    sums[band].at[pl.ds(lo - band * band_blocks, hi - lo), pl.ds(0, BAND_ROWS)],
                    held.at[pl.ds(lo, hi - lo)],
                    sem_in.at[part, len(mine)],
                )
            )
            mine[-1].start()
            lo = hi
        copies.append(mine)
    small = [
        pltpu.make_async_copy(
            sums[band].at[:, pl.ds(BAND_ROWS, BAND_ROWS_ONE)], held_one.at[band], sem_one.at[band]
        )
        for band in range(3)
    ]
    for copy in small:
        copy.start()
    outs = []

    def leave(src, dst):
        outs.append(pltpu.make_async_copy(src, dst, sem_out.at[len(outs)]))
        outs[-1].start()

    xt_ref[...] = gx_ref[...].T
    leave(xt_ref, xt_hbm)
    for part, (at, rows, columns) in enumerate(FF_PARTS):
        for copy in copies[part]:
            copy.wait()
        for tile in range((columns + 127) // 128):
            width = min(128, columns - 128 * tile)
            for row in range(0, rows, BAND_ROWS):
                piece = held[(at + tile * rows + row) // BAND_ROWS].astype(f32)
                fulls[part][row : row + BAND_ROWS, 128 * tile : 128 * tile + width] = piece[:, 0:width]
        leave(fulls[part], spots[part])
    for copy in small:
        copy.wait()

    def fetch_one(at):
        band, block = divmod(at // BAND_ROWS_ONE, N_CTX)
        return held_one[band, block].astype(f32)

    for tile in range(5):
        width = min(128, D - 128 * tile)
        lanes = slice(128 * tile, 128 * tile + width)
        for row in range(0, D, 16):
            gq_ref[row : row + 16, lanes] = fetch_one(Q_AT + tile * D + row)[:, 0:width]
        for row in range(0, 192, 16):
            gk_ref[row : row + 16, lanes] = fetch_one(KV_AT + tile * 384 + row)[:, 0:width]
            gv_ref[row : row + 16, lanes] = fetch_one(KV_AT + tile * 384 + 192 + row)[:, 0:width]
        ga_ref[lanes] = fetch_one(GAIN_ONE_AT)[tile, 0:width]
        gm_ref[lanes] = held[GAIN_AT // BAND_ROWS].astype(f32)[tile, 0:width]
    leave(gq_ref, gq_hbm)
    leave(gk_ref, gk_hbm)
    leave(gv_ref, gv_hbm)
    for copy in outs:
        copy.wait()


def unpack(sums, grad_x):
    vmem = pl.BlockSpec(memory_space=pltpu.VMEM)
    anywhere = pl.BlockSpec(memory_space=pl.ANY)
    shapes = ((D,), (D,), (D, ROWS), (D, D), (192, D), (192, D), (D, FF), (D, FF), (D, FF), (D, D))
    return pl.pallas_call(
        unpack_kernel,
        out_shape=tuple(jax.ShapeDtypeStruct(s, f32) for s in shapes),
        in_specs=[anywhere] * 3 + [vmem],
        out_specs=(vmem,) * 2 + (anywhere,) * 8,
        scratch_shapes=[
            pltpu.VMEM((3 * N_CTX, BAND_ROWS, 128), bf16),
            pltpu.VMEM((3, N_CTX, BAND_ROWS_ONE, 128), bf16),
            pltpu.VMEM((D, FF), f32),
            pltpu.VMEM((D, FF), f32),
            pltpu.VMEM((D, FF), f32),
            pltpu.VMEM((D, D), f32),
            pltpu.VMEM((D, ROWS), f32),
            pltpu.VMEM((D, D), f32),
            pltpu.VMEM((192, D), f32),
            pltpu.VMEM((192, D), f32),
            pltpu.SemaphoreType.DMA((4, 2)),
            pltpu.SemaphoreType.DMA((3,)),
            pltpu.SemaphoreType.DMA((8,)),
        ],
        compiler_params=pltpu.CompilerParams(vmem_limit_bytes=VMEM_LIMIT),
        name="unpack",
    )(
        *[s.reshape(N_CTX, FINAL_ROWS, 128) for s in sums],
        grad_x,
    )


def on_device(
    layer_input,
    attn_gain,
    w_query,
    w_key,
    w_value,
    w_out,
    mlp_gain,
    w_gate,
    w_up,
    w_down,
    cotangent,
    segment_ids,
    pair_table,
):
    own_pair = pair_table[0]
    within = jnp.arange(ROWS, dtype=jnp.int32)
    blocks = jnp.where(within < HALF, own_pair, 2 * N_CTX - 1 - own_pair)
    places = blocks * HALF + within % HALF
    lanes = jnp.arange(128, dtype=jnp.int32)
    frequency = ROPE_THETA ** (-2.0 * (lanes % (HEAD_DIM // 2)).astype(f32) / HEAD_DIM)
    turned = places.astype(f32)[:, None] * frequency[None, :]
    cos_wide = jnp.cos(turned)
    sin_wide = jnp.sin(turned) * jnp.where(lanes % HEAD_DIM < HEAD_DIM // 2, -1.0, 1.0)[None, :]

    segments = segment_ids[None, :]
    x_turned = layer_input.T
    wk_turned, wv_turned = w_key.T, w_value.T
    q_rot, normed, table, *kvs = project_and_gather(
        pair_table, x_turned, attn_gain, w_query, wk_turned, wv_turned, cos_wide, sin_wide, segments
    )
    result, grad_hidden, dq, *rest = layer(
        pair_table,
        table,
        [kv.reshape(N_CTX, ROWS, 128) for kv in kvs],
        [w_out, w_gate, w_up, w_down.T],
        q_rot,
        x_turned,
        cotangent.T,
        mlp_gain,
    )
    lead = (SIDE, SIDE, SIDE, 2)
    grad_x, *sums = reduce_all(
        [d.reshape(lead + (ROWS, 128)) for d in rest[0:3]],
        [d.reshape(lead + (BAND_ROWS, 128)) for d in rest[3:6]],
        dq,
        normed,
        x_turned,
        grad_hidden,
        cos_wide,
        sin_wide,
        attn_gain,
        w_query,
        wk_turned,
        wv_turned,
    )
    ga, gm, gx, gq, gk, gv, gg, gu, gd, go = unpack(sums, grad_x)
    return (result.T, gx.T, ga, gq, gk.T, gv.T, go, gm, gg, gu, gd.T)


def solution(mesh):
    return jax.shard_map(
        on_device,
        mesh=mesh,
        in_specs=(
            P("ctx", None),
            P(),
            P(),
            P(),
            P(),
            P(),
            P(),
            P(),
            P(),
            P(),
            P("ctx", None),
            P("ctx"),
            P("ctx"),
        ),
        out_specs=(P("ctx", None), P("ctx", None), P(), P(), P(), P(), P(), P(), P(), P(), P()),
        check_vma=False,
    )
```

```python
import functools
import jax
import jax.numpy as jnp
from jax import lax
from jax.experimental import pallas as pl
from jax.experimental.pallas import tpu as pltpu
from jax.sharding import PartitionSpec as P

f32 = jnp.float32
bf16 = jnp.bfloat16
D = 576
HEADS = 9
KV_HEADS = 3
HEAD_DIM = 64
PER_GROUP = HEADS // KV_HEADS
FF = 1536
NORM_EPS = 1e-05
ROPE_THETA = 100000.0
ROWS = 128
HALF = 64
N_CTX = 128
TOKENS = ROWS * N_CTX
DOCS = 18
META = 16
CHUNK = 512
PIECES = CHUNK // HALF
CHUNKS = TOKENS // CHUNK
BLANK = 4096
COLS = HEADS * HALF
NEG = -1e30
SCALE = HEAD_DIM ** (-0.5)
VMEM_LIMIT = 56 * 1024 * 1024

K_AT = (0, 64, 128)
V_AT = (128, 192, 64)

GATE_AT = 0
UP_AT = GATE_AT + 12 * D
DOWN_AT = UP_AT + 12 * D
OUT_AT = DOWN_AT + 12 * D
GAIN_AT = OUT_AT + 5 * D
BAND_ROWS = 64
FF_ROWS = 3 * N_CTX * BAND_ROWS
Q_AT = 0
KV_AT = Q_AT + 5 * D
GAIN_ONE_AT = KV_AT + 5 * 384
BAND_ROWS_ONE = 16
FINAL_ROWS = BAND_ROWS + BAND_ROWS_ONE
ATT_ROWS = 3 * N_CTX * BAND_ROWS_ONE

MESH = pl.DeviceIdType.MESH
SIDE = 4
ORDERS = ((2, 1, 0), (1, 0, 2), (0, 2, 1))
STRIDES = (32, 8, 2)


def whereabouts():
    me = lax.axis_index("ctx")
    coords = (me // 32, lax.rem(me // 8, SIDE), lax.rem(me // 2, SIDE))
    return me, coords, lax.rem(me, 2)


def wrap(coord, step):
    return lax.rem(coord + (step + SIDE), SIDE)


def neighbour(me, coords, axis, step):
    return me + (wrap(coords[axis], step) - coords[axis]) * STRIDES[axis]


PARTNERS = 10


def greet(me, coords, core):
    others = [me + 1 - 2 * core]
    for axis in range(3):
        others += [neighbour(me, coords, axis, step) for step in (1, -1, 2)]
    for other in others:
        pl.semaphore_signal(
            pltpu.get_barrier_semaphore(), inc=1, device_id=(other,), device_id_type=MESH
        )


def meet():
    pl.semaphore_wait(pltpu.get_barrier_semaphore(), PARTNERS)


def half_rows(rows):
    return rows // 32 * 16


class Pool:
    def __init__(self, sems):
        self.sems = sems
        self.used = 0

    def new(self):
        self.used += 1
        return self.sems.at[self.used - 1]


def send(src, dst, device, send_sem, recv_sem):
    pltpu.make_async_remote_copy(
        src_ref=src,
        dst_ref=dst,
        send_sem=send_sem,
        recv_sem=recv_sem,
        device_id=(device,),
        device_id_type=MESH,
    ).start()


def wait_for(ref, sem):
    pltpu.make_async_copy(ref, ref, sem).wait()


def at_axes(order, values):
    index = [None] * 3
    for axis, value in zip(order, values):
        index[axis] = value
    return tuple(index)


WHOLE = pl.ds(0, SIDE)


def gather_steps(own, out, pool):
    me, coords, core = whereabouts()
    sibling = me + 1 - 2 * core
    bands = range(len(own))
    orders = [ORDERS[band % 3] for band in bands]
    lines = (0, 1, -1, 2)
    steps = (1, -1, 2)

    def place(band, *values):
        return out[band].at[at_axes(orders[band], values) + (core,)]

    def mine(band, phase, step=0):
        return wrap(coords[orders[band][phase]], step)

    def device(band, phase, step):
        return neighbour(me, coords, orders[band][phase], step)

    def blocks(*shape):
        return out[0].at[tuple(pl.ds(0, size) for size in shape)]

    home, came, gone = pool.new(), [pool.new() for phase in range(3)], [pool.new(), pool.new()]
    ringed = [pool.new() for band in bands]
    across = [(pool.new(), pool.new()) for band in bands]
    ends = {line: (pool.new(), pool.new(), pool.new()) for line in lines}
    for step in steps:
        for phase in (1, 0):
            for band in bands:
                part = place(band, *(mine(band, p) for p in range(3)))
                send(own[band], part, device(band, phase, step), gone[0], came[phase])
    for band in bands:
        part = place(band, *(mine(band, p) for p in range(3)))
        pltpu.make_async_copy(own[band], part, home).start()

    def send_line(band, line):
        part = place(band, mine(band, 0, line), WHOLE, mine(band, 2))
        send(part, part, device(band, 2, 1), ringed[band], ends[line][0])
        send(part, part, device(band, 2, -1), ringed[band], ends[line][1])

    yield
    wait_for(blocks(1, 1, 3, 1), home)
    wait_for(blocks(1, 3, 3, 1), came[1])
    for band in bands:
        send_line(band, 0)
    wait_for(blocks(1, 3, 3, 1), came[0])
    for band in bands:
        for line in lines[1:]:
            part = place(band, mine(band, 0, line), mine(band, 1), mine(band, 2))
            for step in steps:
                send(part, part, device(band, 1, step), gone[1], came[2])
    yield
    wait_for(blocks(3, 3, 3, 1), came[2])
    for line in lines[1:]:
        for band in bands:
            send_line(band, line)
    for band in bands:
        part = place(band, WHOLE, WHOLE, mine(band, 2))
        send(part, part, sibling, *across[band])
    for line in lines:
        yield
        for side, step in ((0, -1), (1, 1)):
            wait_for(blocks(1, 3, 4, 1), ends[line][side])
            for band in bands:
                rows = own[band].shape[0]
                cut = half_rows(rows)
                part = place(band, mine(band, 0, line), WHOLE, mine(band, 2, step))
                half = part.at[:, pl.ds(0, cut) if side == 0 else pl.ds(cut, rows - cut)]
                send(half, half, device(band, 2, -step), ringed[band], ends[line][2])
                send(part, part, sibling, *across[band])
    for line in lines:
        yield
        wait_for(blocks(1, 3, 4, 1), ends[line][2])
        for band in bands:
            part = place(band, mine(band, 0, line), WHOLE, mine(band, 2, 2))
            send(part, part, sibling, *across[band])
    yield
    for band in bands:
        wait_for(out[band].at[:, :, :, 0], across[band][1])
        wait_for(out[band].at[:, :, :, 0], across[band][0])
        wait_for(out[band].at[0:3, :, :, 0], ringed[band])
    wait_for(blocks(3, 3, 1, 2), gone[0])
    wait_for(blocks(3, 3, 3, 1), gone[1])


GATHER_SEMS = 1 + 3 + 2 + 3 + 6 + 12


def gather_small_steps(own, out, pool):
    me, coords, core = whereabouts()
    sibling = me + 1 - 2 * core
    bands = range(len(own))
    homes = [pool.new() for band in bands]
    for band in bands:
        pltpu.make_async_copy(own[band], out[band].at[coords + (core,)], homes[band]).start()
    sent = []
    for phase in range(3):
        came = [pool.new() for band in bands]
        gone = [pool.new() for band in bands]
        for band in bands:
            order = ORDERS[band % 3]
            mine = [coords[axis] for axis in order]
            part = out[band].at[at_axes(order, [WHOLE] * phase + mine[phase:]) + (core,)]
            for step in (1, -1, 2):
                send(
                    own[band] if phase == 0 else part,
                    part,
                    neighbour(me, coords, order[phase], step),
                    gone[band],
                    came[band],
                )
        yield
        for band in bands:
            if phase == 0:
                wait_for(own[band], homes[band])
            three = (0, 0, pl.ds(0, 3), 0), (0, pl.ds(0, 3), WHOLE, 0), (pl.ds(0, 3), WHOLE, WHOLE, 0)
            wait_for(out[band].at[three[phase]], came[band])
            sent.append((out[band].at[three[phase]], gone[band]))
    across = [(pool.new(), pool.new()) for band in bands]
    for band in bands:
        part = out[band].at[:, :, :, core]
        send(part, part, sibling, *across[band])
    yield
    for band in bands:
        wait_for(out[band].at[:, :, :, 0], across[band][1])
        wait_for(out[band].at[:, :, :, 0], across[band][0])
    for ref, sem in sent:
        wait_for(ref, sem)


GATHER_SMALL_SEMS = 1 + 3 * 2 + 2


def run(steps):
    for _ in steps:
        pass


def scatter_scratch(rows, ring):
    shapes = [pltpu.VMEM((SIDE, SIDE, SIDE, rows, 128), bf16)] * 6
    for _ in range(3):
        shapes += [
            pltpu.VMEM((3, SIDE, SIDE, rows, 128), bf16),
            pltpu.VMEM((3, SIDE, rows, 128), bf16),
            pltpu.VMEM((3, rows, 128), bf16),
        ]
    return shapes + [pltpu.SemaphoreType.DMA((6 + 2 + 4 + 16 + 8 + 2 if ring else 6 + 2 + 6 + 3 + 2,))]


SCATTER_REFS = 16


def scatter_steps(parts, done, scratch, ring):
    acc, sib = scratch[0:3], scratch[3:6]
    landing = [scratch[6 + 3 * b : 9 + 3 * b] for b in range(3)]
    pool = Pool(scratch[15])
    me, coords, core = whereabouts()
    sibling = me + 1 - 2 * core
    bands = range(3)
    steps = (2, 1, -1, 0)
    rows = acc[0].shape[3]
    cut = half_rows(rows)
    def blocks(*shape):
        return acc[0].at[tuple(pl.ds(0, size) for size in shape)]

    sent = [[pool.new(), None, None, pool.new()] for band in bands]
    for phase in (1, 2):
        shared = pool.new()
        for band in bands:
            sent[band][phase] = shared
    homes, swaps = {}, {}

    def line_at(band, step, sub):
        order = ORDERS[band]
        return at_axes(order, (wrap(coords[order[0]], step), wrap(coords[order[1]], steps[sub]), WHOLE))

    if ring:
        for step in steps:
            for band in bands:
                order = ORDERS[band]
                plane = at_axes(order, (wrap(coords[order[0]], step), WHOLE, WHOLE))
                if band == 0:
                    homes[step] = pool.new()
                top = 0
                for part in parts[band]:
                    size = part.shape[4]
                    pltpu.make_async_copy(
                        part.at[plane + (core,)],
                        acc[band].at[plane + (pl.ds(top, size),)],
                        homes[step],
                    ).start()
                    top += size
        yield
        for step in steps:
            for sub in range(SIDE):
                for band in bands:
                    line = line_at(band, step, sub)
                    if band == 0:
                        swaps[step, sub] = pool.new()
                    top = 0
                    for part in parts[band]:
                        size = part.shape[4]
                        send(
                            part.at[line + (1 - core,)],
                            sib[band].at[line + (pl.ds(top, size),)],
                            sibling,
                            sent[band][3],
                            swaps[step, sub],
                        )
                        top += size
    else:
        for band in bands:
            homes[band], swaps[band] = pool.new(), pool.new()
            (part,) = parts[band]
            pltpu.make_async_copy(part.at[:, :, :, core], acc[band], homes[band]).start()
        yield
        for band in bands:
            (part,) = parts[band]
            send(part.at[:, :, :, 1 - core], sib[band], sibling, sent[band][3], swaps[band])

    def add_swap(band, step, sub):
        if band == 0:
            if sub == 0:
                wait_for(blocks(3, 4, 4), homes[step])
            wait_for(blocks(1, 3, 4), swaps[step, sub])

        line = line_at(band, step, sub)
        acc[band][line] = acc[band][line] + sib[band][line]

    def sum_up(band, region, landed):
        total = acc[band][region].astype(f32)
        for ref in landed:
            total = total + ref[...].astype(f32)
        acc[band][region] = total.astype(bf16)

    second = pool.new()

    def send_second(band, sub):
        if steps[sub]:
            send(
                acc[band].at[line_at(band, 0, sub)],
                landing[band][1].at[sub],
                neighbour(me, coords, ORDERS[band][1], steps[sub]),
                sent[band][1],
                second,
            )

    if ring:
        passing, ending = {}, {}
        for sub in range(SIDE):
            yield
            passing[sub], ending[sub] = pool.new(), pool.new()
            for band in bands:
                axis = ORDERS[band][0]
                add_swap(band, 2, sub)
                far = acc[band].at[line_at(band, 2, sub)]
                for lo, size, step in ((0, cut, 1), (cut, rows - cut, -1)):
                    send(
                        far.at[:, pl.ds(lo, size)],
                        landing[band][0].at[0, sub, :, pl.ds(lo, size)],
                        neighbour(me, coords, axis, step),
                        sent[band][0],
                        passing[sub],
                    )
        for sub in range(SIDE):
            yield
            for step in (1, -1):
                for band in bands:
                    add_swap(band, step, sub)
            wait_for(blocks(1, 3, 4), passing[sub])
            for band in bands:
                order = ORDERS[band]
                for slot, lo, size, step in ((1, 0, cut, 1), (2, cut, rows - cut, -1)):
                    half = line_at(band, step, sub) + (pl.ds(lo, size),)
                    acc[band][half] = acc[band][half] + landing[band][0][0, sub, :, lo : lo + size]
                    send(
                        acc[band].at[line_at(band, step, sub)],
                        landing[band][0].at[slot, sub],
                        neighbour(me, coords, order[0], step),
                        sent[band][0],
                        ending[sub],
                    )
        for sub in range(SIDE):
            yield
            for band in bands:
                add_swap(band, 0, sub)
            wait_for(blocks(2, 3, 4), ending[sub])
            for band in bands:
                order = ORDERS[band]
                sum_up(
                    band, line_at(band, 0, sub), [landing[band][0].at[slot, sub] for slot in (1, 2)]
                )
                send_second(band, sub)
    else:
        came = [pool.new() for band in bands]
        yield
        for band in bands:
            axis = ORDERS[band][0]
            wait_for(acc[band], homes[band])
            wait_for(sib[band], swaps[band])
            acc[band][...] = acc[band][...] + sib[band][...]
            for slot, step in enumerate((2, 1, -1)):
                plane = at_axes(ORDERS[band], (wrap(coords[axis], step), WHOLE, WHOLE))
                send(
                    acc[band].at[plane],
                    landing[band][0].at[slot],
                    neighbour(me, coords, axis, step),
                    sent[band][0],
                    came[band],
                )
        yield
        for band in bands:
            plane = at_axes(ORDERS[band], (coords[ORDERS[band][0]], WHOLE, WHOLE))
            wait_for(landing[band][0], came[band])
            total = acc[band][plane].astype(f32)
            for slot in range(3):
                total = total + landing[band][0][slot].astype(f32)
            acc[band][plane] = total.astype(bf16)
    if not ring:
        for sub in range(SIDE):
            for band in bands:
                send_second(band, sub)
    yield
    ends = pool.new()
    wait_for(blocks(3, 3, 4), second)
    for band in bands:
        order = ORDERS[band]
        line = at_axes(order, (coords[order[0]], coords[order[1]], WHOLE))
        sum_up(band, line, [landing[band][1].at[slot] for slot in range(3)])
        for slot, step in enumerate((2, 1, -1)):
            at = at_axes(order, (coords[order[0]], coords[order[1]], wrap(coords[order[2]], step)))
            send(
                acc[band].at[at],
                landing[band][2].at[slot],
                neighbour(me, coords, order[2], step),
                sent[band][2],
                ends,
            )
    yield
    wait_for(blocks(1, 3, 3), ends)
    for band in bands:
        total = acc[band][coords].astype(f32)
        for slot in range(3):
            total = total + landing[band][2][slot].astype(f32)
        done[band][...] = total
    for band in bands:
        wait_for(acc[band].at[0:3], sent[band][0])
        wait_for(acc[band], sent[band][3])
    wait_for(blocks(3, 3, 4), sent[0][1])
    wait_for(blocks(1, 3, 3), sent[0][2])


def rms_parts(features):
    return lax.rsqrt(jnp.mean(features * features, axis=-1, keepdims=True) + NORM_EPS)


def rms_back(features, gain, grad):
    inverse = rms_parts(features)
    scaled = grad * gain
    inner = jnp.mean(scaled * features, axis=-1, keepdims=True)
    by_features = inverse * scaled - features * (inverse * inverse * inverse * inner)
    by_gain = jnp.sum(grad * features * inverse, axis=0, keepdims=True)
    return by_features, by_gain


def nt_dot(left, right):
    return lax.dot_general(left, right, (((1,), (1,)), ((), ())), preferred_element_type=f32)


def tn_dot(left, right):
    return lax.dot_general(left, right, (((0,), (0,)), ((), ())), preferred_element_type=f32)


def nn_dot(left, right):
    return jnp.dot(left, right, preferred_element_type=f32)


def turn(tile, cos_wide, sin_wide):
    lanes = lax.broadcasted_iota(jnp.int32, tile.shape, 1)
    swapped = jnp.where(
        lax.rem(lanes, HEAD_DIM) < HEAD_DIM // 2, pltpu.roll(tile, 96, 1), pltpu.roll(tile, 32, 1)
    )
    return tile * cos_wide + swapped * sin_wide


def project_kernel(
    pair_ref, x_ref, gain_ref, wq_ref, wk_ref, wv_ref, cos_ref, sin_ref, seg_ref,
    q_ref, n_ref, table_ref, out0, out1, out2,
    own0, own1, own2, own_meta, metas, sems, meta_sems,
):
    me, coords, core = whereabouts()
    greet(me, coords, core)
    segments = jnp.broadcast_to(seg_ref[...].astype(f32), (ROWS, ROWS)).T
    lanes = lax.broadcasted_iota(jnp.int32, (ROWS, ROWS), 1)
    earlier = jnp.sum(jnp.where(segments < (lanes - 1).astype(f32), 1.0, 0.0), axis=0, keepdims=True)
    meta = jnp.where(lanes[0:1] == 0, pair_ref[0].astype(f32), earlier)
    own_meta[...] = jnp.broadcast_to(meta, (META, 128)).astype(bf16)
    features = x_ref[...].astype(f32).T
    normed = (features * rms_parts(features) * gain_ref[...].reshape(1, D)).astype(bf16)
    n_ref[...] = normed
    cos_wide, sin_wide = cos_ref[...], sin_ref[...]
    keys = nt_dot(normed, wk_ref[...])
    values = nt_dot(normed, wv_ref[...]).astype(bf16)
    queries = nn_dot(normed, wq_ref[...])
    own0[...] = turn(keys[:, 0:128], cos_wide, sin_wide).astype(bf16)
    mixed = turn(jnp.concatenate([keys[:, 128:192], queries[:, 512:576]], 1), cos_wide, sin_wide)
    own1[...] = jnp.concatenate([mixed[:, 0:64].astype(bf16), values[:, 128:192]], 1)
    own2[...] = values[:, 0:128]
    meet()
    steps = gather_steps((own0, own1, own2), (out0, out1, out2), Pool(sems))
    small = gather_small_steps((own_meta,), (metas,), Pool(meta_sems))
    next(small)
    next(steps)
    next(small)
    for tile in range(4):
        at = slice(128 * tile, 128 * tile + 128)
        q_ref[:, at] = (turn(queries[:, at], cos_wide, sin_wide).astype(bf16).astype(f32) * SCALE).astype(bf16)
    q_ref[:, 512:576] = (mixed[:, 64:128].astype(bf16).astype(f32) * SCALE).astype(bf16)
    next(steps)
    next(small)
    for _ in range(3):
        next(steps)
    next(small)
    for _ in range(3):
        next(steps)
    run(small)
    columns = metas[:, :, :, :, 0, :].astype(f32).reshape(N_CTX, 128)
    starts = jnp.sum(columns, axis=0, keepdims=True)
    numbers = lax.broadcasted_iota(jnp.int32, (N_CTX, N_CTX), 0).astype(f32)
    holders = jnp.sum(
        jnp.where(columns[:, 0:1] == lanes.astype(f32), numbers, 0.0), axis=0, keepdims=True
    )
    segment_row = seg_ref[...].astype(f32)
    row_starts = jnp.zeros((1, ROWS), f32)
    for document in range(DOCS):
        row_starts = jnp.where(
            segment_row == float(document), starts[:, document + 1 : document + 2], row_starts
        )
    table_ref[...] = jnp.concatenate(
        [holders, row_starts, jnp.zeros((6, 128), f32)], 0
    ).astype(jnp.int32)
    run(steps)


def project_and_gather(pair, x, gain, wq, wk, wv, cos_wide, sin_wide, segments):
    vmem = pl.BlockSpec(memory_space=pltpu.VMEM)
    anywhere = pl.BlockSpec(memory_space=pl.ANY)
    return pl.pallas_call(
        project_kernel,
        out_shape=(
            jax.ShapeDtypeStruct((ROWS, D), bf16),
            jax.ShapeDtypeStruct((ROWS, D), bf16),
            jax.ShapeDtypeStruct((8, 128), jnp.int32),
        )
        + (jax.ShapeDtypeStruct((SIDE, SIDE, SIDE, 2, ROWS, 128), bf16),) * 3,
        in_specs=[pl.BlockSpec(memory_space=pltpu.SMEM)] + [vmem] * 8,
        out_specs=(vmem, vmem, vmem, anywhere, anywhere, anywhere),
        scratch_shapes=[pltpu.VMEM((ROWS, 128), bf16)] * 3
        + [
            pltpu.VMEM((META, 128), bf16),
            pltpu.VMEM((SIDE, SIDE, SIDE, 2, META, 128), bf16),
            pltpu.SemaphoreType.DMA((GATHER_SEMS,)),
            pltpu.SemaphoreType.DMA((GATHER_SMALL_SEMS,)),
        ],
        compiler_params=pltpu.CompilerParams(
            collective_id=1, has_side_effects=True, vmem_limit_bytes=VMEM_LIMIT
        ),
        name="project_and_gather",
    )(pair, x, gain, wq, wk, wv, cos_wide, sin_wide, segments)


def needed(chunk, a_hi, b_lo, b_hi):
    return (chunk <= a_hi) | ((chunk >= b_lo) & (chunk <= b_hi))


def chunk_rows(chunk, count=1):
    return pl.ds(pl.multiple_of(chunk * CHUNK, CHUNK), count * CHUNK)


def wait_chunk(chunk, held, sem):
    window = held.at[chunk_rows(chunk)]
    pltpu.make_async_copy(window, window, sem.at[chunk]).wait()


def chunk_mask(chunk, count, place_row, start_row):
    keys = chunk * CHUNK + lax.broadcasted_iota(jnp.int32, (count * CHUNK, COLS), 0)
    return (keys <= place_row) & (keys >= start_row)


def layer_kernel(
    pair_ref, table,
    kv0, kv1, kv2, wo_hbm, wg_hbm, wu_hbm, wd_hbm,
    q_ref, starts_ref, x_ref, c_ref, gain_ref,
    result_ref, gh_ref, dq_ref, dkv0, dkv1, dkv2, dw0, dw1, dw2,
    held, sem, wo_ref, wg_ref, wu_ref, wd_ref, w_sem, q_spread, g_spread, mixed, top, total, att_ref,
    delta_ref, dw, dw_sem, staged, blank, out_sem, blank_sem, gain_rows,
    rows_ref,
):
    kvs, dkvs, dws = (kv0, kv1, kv2), (dkv0, dkv1, dkv2), (dw0, dw1, dw2)
    weights = [
        pltpu.make_async_copy(src, dst, w_sem.at[i])
        for i, (src, dst) in enumerate(
            ((wo_hbm, wo_ref), (wg_hbm, wg_ref), (wu_hbm, wu_ref), (wd_hbm, wd_ref))
        )
    ]
    pair = pair_ref[0]
    row_starts = starts_ref[1:2, :]
    for block in range(2):
        first = pair if block == 0 else 2 * N_CTX - 1 - pair
        places = first * HALF + lax.rem(lax.broadcasted_iota(jnp.int32, (1, COLS), 1), HALF)
        rows_ref[2 * block : 2 * block + 1, :] = places
        mine = row_starts[:, block * HALF : (block + 1) * HALF]
        rows_ref[2 * block + 1 : 2 * block + 2, :] = jnp.concatenate([mine] * HEADS, 1)
    a_hi, b_lo, b_hi = pair // PIECES, table[1, HALF] // CHUNK, (2 * N_CTX - 1 - pair) // PIECES

    def slot_of(block_number):
        low = table[0, jnp.minimum(block_number, 2 * N_CTX - 1 - block_number)]
        return low * ROWS + jnp.where(block_number < N_CTX, 0, HALF)


    def issue(chunk, carry):
        @pl.when(needed(chunk, a_hi, b_lo, b_hi))
        def _():
            for piece in range(PIECES):
                slot = slot_of(chunk * PIECES + piece)
                rows = pl.ds(pl.multiple_of(chunk * CHUNK + piece * HALF, HALF), HALF)
                device, top = slot // ROWS, pl.multiple_of(lax.rem(slot, ROWS), HALF)
                for band in range(3):
                    pltpu.make_async_copy(
                        kvs[band].at[device, pl.ds(top, HALF)],
                        held.at[rows, 128 * band : 128 * band + 128],
                        sem.at[chunk],
                    ).start()

        return carry

    lax.fori_loop(0, CHUNKS, issue, 0)
    for copy in weights:
        copy.start()

    def spread(rows, place, windows):
        for block in range(2):
            for head in range(HEADS):
                tile = rows[block * HALF : (block + 1) * HALF, head * HEAD_DIM : (head + 1) * HEAD_DIM]
                at = windows[head // PER_GROUP]
                place[block, head * HALF : (head + 1) * HALF, at : at + HEAD_DIM] = tile

    def unspread(columns, place, block, windows):
        for head in range(HEADS):
            at = windows[head // PER_GROUP]
            tile = columns[at : at + HEAD_DIM, head * HALF : (head + 1) * HALF]
            place[block * HALF : (block + 1) * HALF, head * HEAD_DIM : (head + 1) * HEAD_DIM] = tile.T

    blank[...] = jnp.zeros_like(blank)

    clears = [
        pltpu.make_async_copy(blank, dkvs[band].at[pl.ds(row, BLANK)], blank_sem.at[band, row // BLANK])
        for band in range(3)
        for row in range(0, TOKENS, BLANK)
    ]
    q_spread[...] = jnp.zeros_like(q_spread)
    g_spread[...] = jnp.zeros_like(g_spread)
    spread(q_ref[...], q_spread, K_AT)
    mixed[...] = jnp.zeros_like(mixed)
    top[...] = jnp.full_like(top, NEG)
    total[...] = jnp.zeros_like(total)

    def mask_of(block, chunk, count):
        return chunk_mask(
            chunk, count, rows_ref[2 * block : 2 * block + 1, :], rows_ref[2 * block + 1 : 2 * block + 2, :]
        )

    def forward(block, chunk, masked, count=1):
        window = chunk_rows(chunk, count)
        scores = nt_dot(held[window, 0:256], q_spread[block])
        if masked:
            scores = jnp.where(mask_of(block, chunk, count), scores, NEG)
        old = top[block : block + 1, :]
        new = jnp.maximum(old, jnp.max(scores, axis=0, keepdims=True))
        probs = jnp.exp(scores - new)
        shrink = jnp.exp(old - new)
        top[block : block + 1, :] = new
        total[block : block + 1, :] = total[block : block + 1, :] * shrink + jnp.sum(
            probs, axis=0, keepdims=True
        )
        values = held[window, 128:384].T[64:256]
        mixed[block, 64:256] = mixed[block, 64:256] * shrink + nn_dot(values, probs.astype(bf16))

    def forward_step(chunk, carry):
        in_b = (chunk >= b_lo) & (chunk <= b_hi)

        @pl.when(needed(chunk, a_hi, b_lo, b_hi))
        def _():
            wait_chunk(chunk, held, sem)

        @pl.when(chunk <= a_hi)
        def _():
            forward(0, chunk, True)

        @pl.when(in_b)
        def _():
            forward(1, chunk, True)

        return carry

    def forward_pair(pair_of, carry):
        wait_chunk(2 * pair_of, held, sem)
        wait_chunk(2 * pair_of + 1, held, sem)
        forward(0, 2 * pair_of, False, 2)
        return carry

    plain = jnp.minimum(a_hi, b_lo) // 2
    tail = 2 * plain
    paired = (a_hi == tail + 1) & (b_lo > a_hi)
    ahead = jnp.where(paired, tail + 2, tail)
    lax.fori_loop(0, plain, forward_pair, 0)

    @pl.when(paired)
    def _():
        wait_chunk(tail, held, sem)
        wait_chunk(tail + 1, held, sem)
        forward(0, tail, True, 2)

    lax.fori_loop(ahead, b_hi + 1, forward_step, 0)
    for block in range(2):
        sums = total[block : block + 1, :]
        top[block : block + 1, :] = top[block : block + 1, :] + jnp.log(sums)
        mixed[block] = mixed[block] / sums
        unspread(mixed.at[block], att_ref, block, V_AT)

    for copy in clears:
        copy.start()

    attended = att_ref[...].astype(bf16)
    cotangent = c_ref[...].astype(f32).T.astype(bf16)
    gain = gain_ref[...].reshape(1, D)
    for copy in weights:
        copy.wait()
    hidden = x_ref[...].astype(f32).T + nn_dot(attended, wo_ref[...])
    normed = (hidden * rms_parts(hidden) * gain).astype(bf16)
    gate = nn_dot(normed, wg_ref[...])
    upward = nn_dot(normed, wu_ref[...])
    open_gate = jax.nn.sigmoid(gate)
    silu = gate * open_gate
    active = (silu * upward).astype(bf16)
    result_ref[...] = (hidden + nt_dot(active, wd_ref[...])).T.astype(bf16)
    grad_active = nn_dot(cotangent, wd_ref[...])
    grad_gate = (grad_active * upward * open_gate * (1.0 + gate * (1.0 - open_gate))).astype(bf16)
    grad_up = (grad_active * silu).astype(bf16)
    grad_normed = nt_dot(grad_gate, wg_ref[...]) + nt_dot(grad_up, wu_ref[...])
    by_hidden, by_gain = rms_back(hidden, gain, grad_normed)
    grad_hidden = cotangent.astype(f32) + by_hidden
    gh_ref[...] = grad_hidden
    grad_out = grad_hidden.astype(bf16)
    spread(nt_dot(grad_out, wo_ref[...]).astype(bf16), g_spread, V_AT)
    for block in range(2):
        turned = g_spread[block].astype(f32).T
        delta_ref[block : block + 1, :] = jnp.sum(turned * mixed[block], axis=0, keepdims=True)

    def pack(at, grads):
        rows = grads.shape[0]
        for tile in range(grads.shape[1] // 128):
            dw[at + tile * rows : at + (tile + 1) * rows, :] = grads[:, 128 * tile : 128 * tile + 128].astype(bf16)
        if grads.shape[1] % 128:
            tile = grads.shape[1] // 128
            dw[at + tile * rows : at + (tile + 1) * rows, 0:64] = grads[:, 128 * tile : 128 * tile + 64].astype(bf16)
            dw[at + tile * rows : at + (tile + 1) * rows, 64:128] = jnp.zeros((rows, 64), bf16)

    pack(GATE_AT, tn_dot(normed, grad_gate))
    pack(UP_AT, tn_dot(normed, grad_up))
    pack(DOWN_AT, tn_dot(cotangent, active))
    pack(OUT_AT, tn_dot(attended, grad_out))
    gain_rows[...] = jnp.zeros_like(gain_rows)
    for tile in range(4):
        gain_rows[tile : tile + 1, :] = by_gain[:, 128 * tile : 128 * tile + 128]
    gain_rows[4:5, 0:64] = by_gain[:, 512:576]
    dw[GAIN_AT : GAIN_AT + 16, :] = gain_rows[...].astype(bf16)
    dw[GAIN_AT + 16 : FF_ROWS, :] = jnp.zeros((FF_ROWS - GAIN_AT - 16, 128), bf16)
    band_rows = FF_ROWS // 3
    dw_copies = [
        pltpu.make_async_copy(dw.at[pl.ds(band * band_rows, band_rows)], dws[band], dw_sem.at[band])
        for band in range(3)
    ]
    for copy in dw_copies:
        copy.start()

    for copy in clears:
        copy.wait()
    mixed[...] = jnp.zeros_like(mixed)

    def backward(block, chunk, masked, mode, count=1):
        window = chunk_rows(chunk, count)
        keys = held[window, 0:256]
        values = held[window, 128:384]
        scores = nt_dot(keys, q_spread[block])
        probs = jnp.exp(scores - top[block : block + 1, :])
        if masked:
            probs = jnp.where(mask_of(block, chunk, count), probs, 0.0)
        grad_probs = nt_dot(values, g_spread[block])
        grad_scores = (probs * (grad_probs - delta_ref[block : block + 1, :])).astype(bf16)
        mixed[block, 0:192] += nn_dot(keys.T[0:192], grad_scores)
        dk = nn_dot(grad_scores, q_spread[block])
        dv = nn_dot(probs.astype(bf16), g_spread[block])
        parts = (dk[:, 0:128], dk[:, 128:256] + dv[:, 0:128], dv[:, 128:256])
        for band in range(3):
            at = slice(128 * band, 128 * band + 128)
            if mode == "first":
                staged[:, at] = parts[band]
            elif mode == "second":
                held[window, at] = (staged[:, at] + parts[band]).astype(bf16)
            else:
                held[window, at] = parts[band].astype(bf16)

    def put_back(chunk):
        for piece in range(PIECES):
            row = pl.multiple_of(slot_of(chunk * PIECES + piece), HALF)
            rows = pl.ds(pl.multiple_of(chunk * CHUNK + piece * HALF, HALF), HALF)
            for band in range(3):
                pltpu.make_async_copy(
                    held.at[rows, 128 * band : 128 * band + 128],
                    dkvs[band].at[pl.ds(row, HALF)],
                    out_sem.at[chunk],
                ).start()

    def backward_step(chunk, carry):
        in_a = chunk <= a_hi
        in_b = (chunk >= b_lo) & (chunk <= b_hi)

        @pl.when(in_a & jnp.logical_not(in_b))
        def _():
            backward(0, chunk, True, "only")

        @pl.when(in_b & jnp.logical_not(in_a))
        def _():
            backward(1, chunk, True, "only")

        @pl.when(in_a & in_b)
        def _():
            backward(0, chunk, True, "first")
            backward(1, chunk, True, "second")

        @pl.when(in_a | in_b)
        def _():
            put_back(chunk)

        return carry

    def backward_pair(pair_of, carry):
        backward(0, 2 * pair_of, False, "only", 2)
        put_back(2 * pair_of)
        put_back(2 * pair_of + 1)
        return carry

    lax.fori_loop(0, plain, backward_pair, 0)

    @pl.when(paired)
    def _():
        backward(0, tail, True, "only", 2)
        put_back(tail)
        put_back(tail + 1)

    lax.fori_loop(ahead, b_hi + 1, backward_step, 0)
    for block in range(2):
        unspread(mixed.at[block], dq_ref, block, K_AT)

    def drain(chunk, carry):
        use = needed(chunk, a_hi, b_lo, b_hi)

        @pl.when(use)
        def _():
            wait_chunk(chunk, held, out_sem)

        return carry

    lax.fori_loop(0, CHUNKS, drain, 0)
    for copy in dw_copies:
        copy.wait()


def layer(pair, table, kvs, weights, q, x, cotangent, gain):
    vmem = pl.BlockSpec(memory_space=pltpu.VMEM)
    anywhere = pl.BlockSpec(memory_space=pl.ANY)
    return pl.pallas_call(
        layer_kernel,
        out_shape=(
            jax.ShapeDtypeStruct((D, ROWS), bf16),
            jax.ShapeDtypeStruct((ROWS, D), f32),
            jax.ShapeDtypeStruct((ROWS, D), f32),
        )
        + (jax.ShapeDtypeStruct((TOKENS, 128), bf16),) * 3
        + (jax.ShapeDtypeStruct((FF_ROWS // 3, 128), bf16),) * 3,
        grid_spec=pltpu.PrefetchScalarGridSpec(
            num_scalar_prefetch=2,
            in_specs=[anywhere] * 7 + [vmem] * 5,
            out_specs=(vmem,) * 3 + (anywhere,) * 6,
            scratch_shapes=[
                pltpu.VMEM((TOKENS, 384), bf16),
                pltpu.SemaphoreType.DMA((CHUNKS,)),
                pltpu.VMEM((D, D), bf16),
                pltpu.VMEM((D, FF), bf16),
                pltpu.VMEM((D, FF), bf16),
                pltpu.VMEM((D, FF), bf16),
                pltpu.SemaphoreType.DMA((4,)),
                pltpu.VMEM((2, COLS, 256), bf16),
                pltpu.VMEM((2, COLS, 256), bf16),
                pltpu.VMEM((2, 256, COLS), f32),
                pltpu.VMEM((2, COLS), f32),
                pltpu.VMEM((2, COLS), f32),
                pltpu.VMEM((ROWS, D), f32),
                pltpu.VMEM((2, COLS), f32),
                pltpu.VMEM((FF_ROWS, 128), bf16),
                pltpu.SemaphoreType.DMA((3,)),
                pltpu.VMEM((CHUNK, 384), f32),
                pltpu.VMEM((BLANK, 128), bf16),
                pltpu.SemaphoreType.DMA((CHUNKS,)),
                pltpu.SemaphoreType.DMA((3, TOKENS // BLANK)),
                pltpu.VMEM((16, 128), f32),
                pltpu.VMEM((4, COLS), jnp.int32),
            ],
        ),
        compiler_params=pltpu.CompilerParams(vmem_limit_bytes=VMEM_LIMIT),
        name="layer",
    )(pair, table, *kvs, *weights, q, table, x, cotangent, gain)


def reduce_kernel(*refs):
    dkv, dws = refs[0:3], refs[3:6]
    dq_ref, n_ref, x_ref, gh_ref, cos_ref, sin_ref, gain_ref, wq_ref, wk_ref, wv_ref = refs[6:16]
    gx_ref, outs = refs[16], refs[17:20]
    rest = refs[20:]
    done, done_ff, done_one, rest = rest[0:3], rest[3:6], rest[6:9], rest[9:]
    first, rest = rest[:SCATTER_REFS], rest[SCATTER_REFS:]
    second, rest = rest[:SCATTER_REFS], rest[SCATTER_REFS:]
    third, rest = rest[:SCATTER_REFS], rest[SCATTER_REFS:]
    parts, own, rest = rest[0:3], rest[3:6], rest[6:]
    gain_rows, sems = rest
    me, coords, core = whereabouts()
    greet(me, coords, core)

    def advance(steps, count):
        for _ in range(count):
            next(steps)

    scatter = scatter_steps([(d,) for d in dkv], done, first, True)
    other = scatter_steps([(dw,) for dw in dws], done_ff, second, True)
    advance(scatter, 1)
    advance(other, 1)
    meet()
    advance(scatter, 1)
    advance(other, 1)
    advance(scatter, 12)

    cos_wide, sin_wide = cos_ref[...], -sin_ref[...]
    normed = n_ref[...]
    features = x_ref[...].astype(f32).T
    tiles = [turn(dq_ref[:, 128 * t : 128 * t + 128] * SCALE, cos_wide, sin_wide).astype(bf16) for t in range(4)]
    last = turn(
        jnp.concatenate([dq_ref[:, 512:576], jnp.zeros((ROWS, 64), f32)], 1) * SCALE, cos_wide, sin_wide
    ).astype(bf16)
    grad_q = jnp.concatenate(tiles + [last[:, 0:64]], 1)
    grad_normed = nt_dot(grad_q, wq_ref[...])

    def put(at, rows16):
        block = at // 16
        band, device = divmod(block, N_CTX)
        index = (device // 32, device // 8 % 4, device // 2 % 4, device % 2)
        parts[band][index] = rows16

    def pack(at, grads):
        height, width = grads.shape
        grads = jnp.concatenate([grads, jnp.zeros((height, 128 - width % 128), f32)], 1).astype(bf16)
        for tile in range(grads.shape[1] // 128):
            for row in range(0, height, 16):
                put(at + tile * height + row, grads[row : row + 16, 128 * tile : 128 * tile + 128])

    pack(Q_AT, tn_dot(normed, grad_q))
    for at in range(GAIN_ONE_AT + 16, ATT_ROWS, 16):
        put(at, jnp.zeros((16, 128), bf16))
    gain_rows[...] = jnp.zeros_like(gain_rows)
    advance(other, SIDE)
    advance(scatter, 1)
    advance(other, SIDE)
    run(scatter)

    last = turn(
        jnp.concatenate([done[1][:, 0:64], jnp.zeros((ROWS, 64), f32)], 1), cos_wide, sin_wide
    ).astype(bf16)
    grad_k = jnp.concatenate([turn(done[0][...], cos_wide, sin_wide).astype(bf16), last[:, 0:64]], 1)
    grad_v = jnp.concatenate([done[2][...], done[1][:, 64:128]], 1).astype(bf16)
    pack(KV_AT, tn_dot(jnp.concatenate([grad_k, grad_v], 1), normed))
    grad_normed = grad_normed + nn_dot(grad_k, wk_ref[...]) + nn_dot(grad_v, wv_ref[...])
    by_x, by_gain = rms_back(features, gain_ref[...].reshape(1, D), grad_normed)
    for tile in range(4):
        gain_rows[tile : tile + 1, :] = by_gain[:, 128 * tile : 128 * tile + 128]
    gain_rows[4:5, 0:64] = by_gain[:, 512:576]
    put(GAIN_ONE_AT, gain_rows[...].astype(bf16))

    small = scatter_steps([(part,) for part in parts], done_one, third, False)
    advance(small, 2)
    gx_ref[...] = gh_ref[...] + by_x
    turns = [(other, 2), (small, 1)]
    while turns:
        for steps, count in list(turns):
            try:
                advance(steps, count)
            except StopIteration:
                turns.remove((steps, count))
    for band in range(3):
        own[band][0:BAND_ROWS, :] = done_ff[band][...].astype(bf16)
        own[band][BAND_ROWS:FINAL_ROWS, :] = done_one[band][...].astype(bf16)
    run(gather_steps(own, outs, Pool(sems)))


def reduce_all(dkvs, dws, dq, normed, x, grad_hidden, cos_wide, sin_wide, gain, wq, wk, wv):
    vmem = pl.BlockSpec(memory_space=pltpu.VMEM)
    anywhere = pl.BlockSpec(memory_space=pl.ANY)
    one = BAND_ROWS_ONE
    return pl.pallas_call(
        reduce_kernel,
        out_shape=(jax.ShapeDtypeStruct((ROWS, D), f32),)
        + (jax.ShapeDtypeStruct((SIDE, SIDE, SIDE, 2, FINAL_ROWS, 128), bf16),) * 3,
        in_specs=[anywhere] * 6 + [vmem] * 10,
        out_specs=(vmem,) + (anywhere,) * 3,
        scratch_shapes=[pltpu.VMEM((ROWS, 128), f32)] * 3
        + [pltpu.VMEM((BAND_ROWS, 128), f32)] * 3
        + [pltpu.VMEM((one, 128), f32)] * 3
        + scatter_scratch(ROWS, True)
        + scatter_scratch(BAND_ROWS, True)
        + scatter_scratch(one, False)
        + [pltpu.VMEM((SIDE, SIDE, SIDE, 2, one, 128), bf16)] * 3
        + [pltpu.VMEM((FINAL_ROWS, 128), bf16)] * 3
        + [pltpu.VMEM((16, 128), f32), pltpu.SemaphoreType.DMA((GATHER_SEMS,))],
        compiler_params=pltpu.CompilerParams(
            collective_id=2, has_side_effects=True, vmem_limit_bytes=VMEM_LIMIT
        ),
        name="reduce_all",
    )(*dkvs, *dws, dq, normed, x, grad_hidden, cos_wide, sin_wide, gain, wq, wk, wv)


FF_PARTS = ((GATE_AT, D, FF), (UP_AT, D, FF), (DOWN_AT, D, FF), (OUT_AT, D, D))


def unpack_kernel(
    sums0, sums1, sums2, gx_ref,
    ga_ref, gm_ref, xt_hbm, gq_hbm, gk_hbm, gv_hbm, gg_hbm, gu_hbm, gd_hbm, go_hbm,
    held, held_one, full0, full1, full2, full3, xt_ref, gq_ref, gk_ref, gv_ref, sem_in, sem_one, sem_out,
):
    sums = (sums0, sums1, sums2)
    fulls = (full0, full1, full2, full3)
    spots = (gg_hbm, gu_hbm, gd_hbm, go_hbm)
    band_blocks = N_CTX
    copies = []
    edges = [0]
    for at, rows, columns in FF_PARTS:
        edges.append((at + (columns + 127) // 128 * rows) // BAND_ROWS)
    edges[-1] = 3 * band_blocks
    for part in range(4):
        mine = []
        lo = edges[part]
        while lo < edges[part + 1]:
            band = lo // band_blocks
            hi = min(edges[part + 1], (band + 1) * band_blocks)
            mine.append(
                pltpu.make_async_copy(
                    sums[band].at[pl.ds(lo - band * band_blocks, hi - lo), pl.ds(0, BAND_ROWS)],
                    held.at[pl.ds(lo, hi - lo)],
                    sem_in.at[part, len(mine)],
                )
            )
            mine[-1].start()
            lo = hi
        copies.append(mine)
    small = [
        pltpu.make_async_copy(
            sums[band].at[:, pl.ds(BAND_ROWS, BAND_ROWS_ONE)], held_one.at[band], sem_one.at[band]
        )
        for band in range(3)
    ]
    for copy in small:
        copy.start()
    outs = []

    def leave(src, dst):
        outs.append(pltpu.make_async_copy(src, dst, sem_out.at[len(outs)]))
        outs[-1].start()

    xt_ref[...] = gx_ref[...].T
    leave(xt_ref, xt_hbm)
    for part, (at, rows, columns) in enumerate(FF_PARTS):
        for copy in copies[part]:
            copy.wait()
        for tile in range((columns + 127) // 128):
            width = min(128, columns - 128 * tile)
            for row in range(0, rows, BAND_ROWS):
                piece = held[(at + tile * rows + row) // BAND_ROWS].astype(f32)
                fulls[part][row : row + BAND_ROWS, 128 * tile : 128 * tile + width] = piece[:, 0:width]
        leave(fulls[part], spots[part])
    for copy in small:
        copy.wait()

    def fetch_one(at):
        band, block = divmod(at // BAND_ROWS_ONE, N_CTX)
        return held_one[band, block].astype(f32)

    for tile in range(5):
        width = min(128, D - 128 * tile)
        lanes = slice(128 * tile, 128 * tile + width)
        for row in range(0, D, 16):
            gq_ref[row : row + 16, lanes] = fetch_one(Q_AT + tile * D + row)[:, 0:width]
        for row in range(0, 192, 16):
            gk_ref[row : row + 16, lanes] = fetch_one(KV_AT + tile * 384 + row)[:, 0:width]
            gv_ref[row : row + 16, lanes] = fetch_one(KV_AT + tile * 384 + 192 + row)[:, 0:width]
        ga_ref[lanes] = fetch_one(GAIN_ONE_AT)[tile, 0:width]
        gm_ref[lanes] = held[GAIN_AT // BAND_ROWS].astype(f32)[tile, 0:width]
    leave(gq_ref, gq_hbm)
    leave(gk_ref, gk_hbm)
    leave(gv_ref, gv_hbm)
    for copy in outs:
        copy.wait()


def unpack(sums, grad_x):
    vmem = pl.BlockSpec(memory_space=pltpu.VMEM)
    anywhere = pl.BlockSpec(memory_space=pl.ANY)
    shapes = ((D,), (D,), (D, ROWS), (D, D), (192, D), (192, D), (D, FF), (D, FF), (D, FF), (D, D))
    return pl.pallas_call(
        unpack_kernel,
        out_shape=tuple(jax.ShapeDtypeStruct(s, f32) for s in shapes),
        in_specs=[anywhere] * 3 + [vmem],
        out_specs=(vmem,) * 2 + (anywhere,) * 8,
        scratch_shapes=[
            pltpu.VMEM((3 * N_CTX, BAND_ROWS, 128), bf16),
            pltpu.VMEM((3, N_CTX, BAND_ROWS_ONE, 128), bf16),
            pltpu.VMEM((D, FF), f32),
            pltpu.VMEM((D, FF), f32),
            pltpu.VMEM((D, FF), f32),
            pltpu.VMEM((D, D), f32),
            pltpu.VMEM((D, ROWS), f32),
            pltpu.VMEM((D, D), f32),
            pltpu.VMEM((192, D), f32),
            pltpu.VMEM((192, D), f32),
            pltpu.SemaphoreType.DMA((4, 2)),
            pltpu.SemaphoreType.DMA((3,)),
            pltpu.SemaphoreType.DMA((8,)),
        ],
        compiler_params=pltpu.CompilerParams(vmem_limit_bytes=VMEM_LIMIT),
        name="unpack",
    )(
        *[s.reshape(N_CTX, FINAL_ROWS, 128) for s in sums],
        grad_x,
    )


def on_device(
    layer_input,
    attn_gain,
    w_query,
    w_key,
    w_value,
    w_out,
    mlp_gain,
    w_gate,
    w_up,
    w_down,
    cotangent,
    segment_ids,
    pair_table,
):
    own_pair = pair_table[0]
    within = jnp.arange(ROWS, dtype=jnp.int32)
    blocks = jnp.where(within < HALF, own_pair, 2 * N_CTX - 1 - own_pair)
    places = blocks * HALF + within % HALF
    lanes = jnp.arange(128, dtype=jnp.int32)
    frequency = ROPE_THETA ** (-2.0 * (lanes % (HEAD_DIM // 2)).astype(f32) / HEAD_DIM)
    turned = places.astype(f32)[:, None] * frequency[None, :]
    cos_wide = jnp.cos(turned)
    sin_wide = jnp.sin(turned) * jnp.where(lanes % HEAD_DIM < HEAD_DIM // 2, -1.0, 1.0)[None, :]

    segments = segment_ids[None, :]
    x_turned = layer_input.T
    wk_turned, wv_turned = w_key.T, w_value.T
    q_rot, normed, table, *kvs = project_and_gather(
        pair_table, x_turned, attn_gain, w_query, wk_turned, wv_turned, cos_wide, sin_wide, segments
    )
    result, grad_hidden, dq, *rest = layer(
        pair_table,
        table,
        [kv.reshape(N_CTX, ROWS, 128) for kv in kvs],
        [w_out, w_gate, w_up, w_down.T],
        q_rot,
        x_turned,
        cotangent.T,
        mlp_gain,
    )
    lead = (SIDE, SIDE, SIDE, 2)
    grad_x, *sums = reduce_all(
        [d.reshape(lead + (ROWS, 128)) for d in rest[0:3]],
        [d.reshape(lead + (BAND_ROWS, 128)) for d in rest[3:6]],
        dq,
        normed,
        x_turned,
        grad_hidden,
        cos_wide,
        sin_wide,
        attn_gain,
        w_query,
        wk_turned,
        wv_turned,
    )
    ga, gm, gx, gq, gk, gv, gg, gu, gd, go = unpack(sums, grad_x)
    return (result.T, gx.T, ga, gq, gk.T, gv.T, go, gm, gg, gu, gd.T)


def solution(mesh):
    return jax.shard_map(
        on_device,
        mesh=mesh,
        in_specs=(
            P("ctx", None),
            P(),
            P(),
            P(),
            P(),
            P(),
            P(),
            P(),
            P(),
            P(),
            P("ctx", None),
            P("ctx"),
            P("ctx"),
        ),
        out_specs=(P("ctx", None), P("ctx", None), P(), P(), P(), P(), P(), P(), P(), P(), P()),
        check_vma=False,
    )
```
